32 devices in a mesh: dp: 8 (over y, x, core), ctx: 4 (over z).
Axes of the slice: x: 2, y: 2, z: 4, core: 2. Of those that a mesh axis runs over, the one named last changes fastest.
Arguments:
- tokens: bfloat16 [16, 1024, 2048], P('dp', 'ctx'), may hold values from -6 to 6
- cotangent: bfloat16 [16, 1024, 2048], P('dp', 'ctx'), may hold values from -6 to 6
- positions: int32 [16, 1024], P('dp', 'ctx'), may hold values from 0 to 1023, as said below
- wqkv_master: float32 [2048, 6144], P(('dp', 'ctx')), may hold values from -0.125 to 0.125
- fc1_master: float32 [2048, 8192], P(('dp', 'ctx')), may hold values from -0.125 to 0.125
- out_master: float32 [2048, 2048], P(('dp', 'ctx')), may hold values from -1.5 to 1.5
- fc2_master: float32 [2048, 8192], P(('dp', 'ctx')), may hold values from -0.0625 to 0.0625
- small_master: float32 [2048, 11], P(('dp', 'ctx')), may hold values from -0.6 to 1.3, as said below
- wqkv_first: float32 [2048, 6144], P(('dp', 'ctx')), may hold values from -128 to 128
- wqkv_second: float32 [2048, 6144], P(('dp', 'ctx')), may hold values from 1949.696 to 7815.168
- fc1_first: float32 [2048, 8192], P(('dp', 'ctx')), may hold values from -24 to 24
- fc1_second: float32 [2048, 8192], P(('dp', 'ctx')), may hold values from 78.6432 to 311.296
- out_first: float32 [2048, 2048], P(('dp', 'ctx')), may hold values from -12 to 12
- out_second: float32 [2048, 2048], P(('dp', 'ctx')), may hold values from 19.6608 to 78.6432
- fc2_first: float32 [2048, 8192], P(('dp', 'ctx')), may hold values from -56 to 56
- fc2_second: float32 [2048, 8192], P(('dp', 'ctx')), may hold values from 367.0016 to 1474.56
- small_first: float32 [2048, 11], P(('dp', 'ctx')), may hold values from -105.6 to 105.6
- small_second: float32 [2048, 11], P(('dp', 'ctx')), may hold values from 78.15168 to 21708.8
Outputs:
- mixed: bfloat16 [16, 1024, 2048], P('dp', 'ctx')
- input_grad: float32 [16, 1024, 2048], P('dp', 'ctx')
- wqkv_first_new: float32 [2048, 6144], P(('dp', 'ctx'))
- wqkv_second_new: float32 [2048, 6144], P(('dp', 'ctx'))
- wqkv_new: float32 [2048, 6144], P(('dp', 'ctx'))
- fc1_first_new: float32 [2048, 8192], P(('dp', 'ctx'))
- fc1_second_new: float32 [2048, 8192], P(('dp', 'ctx'))
- fc1_new: float32 [2048, 8192], P(('dp', 'ctx'))
- out_first_new: float32 [2048, 2048], P(('dp', 'ctx'))
- out_second_new: float32 [2048, 2048], P(('dp', 'ctx'))
- out_new: float32 [2048, 2048], P(('dp', 'ctx'))
- fc2_first_new: float32 [2048, 8192], P(('dp', 'ctx'))
- fc2_second_new: float32 [2048, 8192], P(('dp', 'ctx'))
- fc2_new: float32 [2048, 8192], P(('dp', 'ctx'))
- small_first_new: float32 [2048, 11], P(('dp', 'ctx'))
- small_second_new: float32 [2048, 11], P(('dp', 'ctx'))
- small_new: float32 [2048, 11], P(('dp', 'ctx'))
The draws below stay inside these ranges and needn't reach their ends.
Inputs may be any that keep to these rules, and one draw needn't show every extreme that they name: In each sequence the positions rise by one from token to token, except at one token at most, where they restart at 0. `small_master`: column 0 holds gains, the others biases.
All inputs are finite; a program needn't handle non-finite values.
Results may differ from the reference program's by a relative error of at most 0.012.
The reference program's roundings to bfloat16 on the way count: a program that leaves them out, or rounds other values in their place, can miss the bound.
Values may be sent and summed in bfloat16 or wider, within the bound.
A program may use at most 640 MiB of HBM per device.

```python
import math
import jax
import jax.numpy as jnp
from jax import lax

D = 2048
H = 32
HD = 64
ROT = 32
FF = 8192
LEN = 1024
STEP = 10
SEQS = 16


def column_scales():
    return jnp.array([2.5, 2.5, 1.5, 1.5, 1.5, 1.0, 0.3, 0.3, 0.3, 0.3, 1.0], jnp.float32)


def draw_positions(key, part):
    key = jax.random.fold_in(key, 3)
    shifts = jax.random.randint(key, (SEQS, 1), 0, LEN, dtype=jnp.int32)
    return ((jnp.arange(LEN, dtype=jnp.int32)[None, :] + shifts) % LEN).astype(jnp.int32)


def draw_small_master(key, part):
    key = jax.random.fold_in(key, 5)
    normal_draw = jnp.clip(jax.random.normal(key, (D, 11), jnp.float32), -3.0, 3.0)
    column = jnp.arange(11)[None, :]
    return jnp.where(column == 0, 1.0 + 0.1 * normal_draw, 0.2 * normal_draw).astype(jnp.float32)


def draw_small_first(key, part):
    key = jax.random.fold_in(key, 7)
    normal_draw = jnp.clip(jax.random.normal(key, (D, 11), jnp.float32), -3.0, 3.0)
    return (normal_draw * (0.11 * (SEQS * LEN) ** 0.5) * column_scales()[None, :]).astype(jnp.float32)


def draw_small_second(key, part):
    key = jax.random.fold_in(key, 9)
    spread = jax.random.uniform(key, (D, 11), jnp.float32)
    scales = column_scales()
    return (0.053 * SEQS * LEN * (scales * scales)[None, :] * jnp.power(4.0, spread)).astype(jnp.float32)


def strengthened(values, rng, source, target, shards_of, factor):
    owner, partner = [(jnp.arange(values.shape[axis_at]) // (values.shape[axis_at] // shards_of)).reshape([-1 if axis == axis_at else 1 for axis in range(values.ndim)]) for axis_at in (source, target)]
    chosen = jax.random.permutation(rng, shards_of)[partner]
    strong = (owner == chosen) | (owner == (partner + shards_of // 2) % shards_of)
    return jnp.where(strong, factor * values, values)


def level_of(key, shape, split, least, top_value):
    def one(dim, blocks):
        steps = jax.random.uniform(jax.random.fold_in(jax.random.fold_in(key, 6), dim), (blocks,), jnp.float32, least / len(split), top_value / len(split))
        return jnp.repeat(jnp.exp(steps), shape[dim] // blocks).reshape((-1,) + (1,) * (len(shape) - dim - 1))

    gain = one(*split[0])
    for cut in split[1:]:
        gain = gain * one(*cut)
    return gain


def scatter_about(stream_key, dims, scale, limit, pieces=(), kind=jnp.bfloat16):
    gain = level_of(stream_key, dims, pieces, -0.22, 0.18) if pieces else 1.0
    result = jax.random.normal(stream_key, dims, jnp.float32) * scale * gain
    return jnp.minimum(jnp.maximum(result, -limit), limit).astype(kind)


def gaussian_with(key, extent, deviation, limit, shards, heavy, kind=jnp.bfloat16):
    values = deviation * jax.random.normal(key, extent, jnp.float32)
    if shards:
        values = values * level_of(key, extent, shards, -0.22, 0.18)
    return jnp.clip(strengthened(values, jax.random.fold_in(key, 3), *heavy), -limit, limit).astype(kind)


def setup_inputs(seed: int = 0) -> dict:
    splits = jax.random.split(jax.random.key(seed), 19)
    tokens = scatter_about(splits[0], (SEQS, LEN, D), 1.0, 6.0, ((0, 8), (1, 4)))
    cotangent = gaussian_with(splits[1], (SEQS, LEN, D), 1.0, 6.0, ((0, 8), (1, 4)), (0, 2, 8, 2.0))
    positions = draw_positions(jax.random.fold_in(splits[18], 71), 0)
    wqkv_master = scatter_about(splits[3], (D, 3 * D), D ** -0.5, 0.125, ((0, 32),), jnp.float32)
    fc1_master = scatter_about(splits[4], (D, FF), D ** -0.5, 0.125, ((0, 32),), jnp.float32)
    out_master = scatter_about(splits[5], (D, D), (max(D // 128, 2)) ** -0.5, 1.5, ((0, 32),), jnp.float32)
    fc2_master = scatter_about(splits[6], (D, FF), FF ** -0.5, 0.0625, ((0, 32),), jnp.float32)
    small_master = draw_small_master(jax.random.fold_in(splits[18], 71), 0)
    wqkv_first = scatter_about(splits[8], (D, 3 * D), (0.165 * (SEQS * LEN) ** 0.5), 128.0, ((0, 32),), jnp.float32)
    wqkv_second = jnp.clip(jnp.exp(math.log(7815.168) - 1.38839297 * jax.random.uniform(splits[9], (D, 3 * D), jnp.float32) ** level_of(splits[9], (D, 3 * D), ((0, 32),), -0.2, 0.2)), 1949.696, 7815.168)
    fc1_first = scatter_about(splits[10], (D, FF), (0.033 * (SEQS * LEN) ** 0.5), 24.0, ((0, 32),), jnp.float32)
    fc1_second = jnp.clip(jnp.exp(math.log(311.296) - 1.375823 * jax.random.uniform(splits[11], (D, FF), jnp.float32) ** level_of(splits[11], (D, FF), ((0, 32),), -0.2, 0.2)), 78.6432, 311.296)
    out_first = scatter_about(splits[12], (D, D), (0.0165 * (SEQS * LEN) ** 0.5), 12.0, ((0, 32),), jnp.float32)
    out_second = jnp.clip(jnp.exp(math.log(78.6432) - 1.3862944 * jax.random.uniform(splits[13], (D, D), jnp.float32) ** level_of(splits[13], (D, D), ((0, 32),), -0.2, 0.2)), 19.6608, 78.6432)
    fc2_first = scatter_about(splits[14], (D, FF), (0.072 * (SEQS * LEN) ** 0.5), 56.0, ((0, 32),), jnp.float32)
    fc2_second = jnp.clip(jnp.exp(math.log(1474.56) - 1.39074879 * jax.random.uniform(splits[15], (D, FF), jnp.float32) ** level_of(splits[15], (D, FF), ((0, 32),), -0.2, 0.2)), 367.0016, 1474.56)
    small_first = draw_small_first(jax.random.fold_in(splits[18], 71), 0)
    small_second = draw_small_second(jax.random.fold_in(splits[18], 71), 0)
    return {"tokens": tokens, "cotangent": cotangent, "positions": positions, "wqkv_master": wqkv_master, "fc1_master": fc1_master, "out_master": out_master, "fc2_master": fc2_master, "small_master": small_master, "wqkv_first": wqkv_first, "wqkv_second": wqkv_second, "fc1_first": fc1_first, "fc1_second": fc1_second, "out_first": out_first, "out_second": out_second, "fc2_first": fc2_first, "fc2_second": fc2_second, "small_first": small_first, "small_second": small_second}


@jax.custom_vjp
def low(v):
    return lax.optimization_barrier(v.astype(jnp.bfloat16)).astype(jnp.float32)

@jax.custom_vjp
def low_back(v):
    return v

def low_keep(v):
    return (low(v), None)

def low_pass(kept, grad):
    return (grad,)

def back_keep(v):
    return (v, None)

def back_low(kept, grad):
    return (low(grad),)
low.defvjp(low_keep, low_pass)
low_back.defvjp(back_keep, back_low)
beta_one = 0.9
beta_two = 0.95
epsilon = 1e-08
highest = lax.Precision.HIGHEST

def adamw(weight, first_old, second_old, gradient, step_rate, decay):
    first_new = beta_one * first_old + (1.0 - beta_one) * gradient
    second_new = beta_two * second_old + (1.0 - beta_two) * gradient * gradient
    first_hat = first_new / (1.0 - beta_one ** STEP)
    second_hat = second_new / (1.0 - beta_two ** STEP)
    weight_new = weight - step_rate * (first_hat / (jnp.sqrt(second_hat) + epsilon) + decay * weight)
    return (first_new, second_new, weight_new)

def rotation_tables(positions):
    half_rot = ROT // 2
    exponent = jnp.arange(half_rot, dtype=jnp.float32) * (-2.0 / ROT)
    frequency = jnp.power(jnp.float32(10000.0), exponent)
    angles = positions.astype(jnp.float32)[..., None] * frequency
    return (jnp.cos(angles)[..., None, :], jnp.sin(angles)[..., None, :])

def rotate(head_vals, cos_table, sin_table):
    half_rot = ROT // 2
    first_half = head_vals[..., :half_rot]
    second = head_vals[..., half_rot:ROT]
    return jnp.concatenate([first_half * cos_table - second * sin_table, second * cos_table + first_half * sin_table, head_vals[..., ROT:]], axis=-1)

def block_attend(query_part, begin_at, keys_low, values):
    scores = low_back(jnp.einsum('gqhd,gkhd->ghqk', query_part, keys_low, precision=highest) * HD ** (-0.5))
    query_pos = begin_at + jnp.arange(query_part.shape[1], dtype=jnp.int32)
    key_pos = jnp.arange(keys_low.shape[1], dtype=jnp.int32)
    allowed = key_pos[None, :] <= query_pos[:, None]
    masked = jnp.where(allowed, scores, -1e+30)
    log_total = jax.nn.logsumexp(masked, axis=-1, keepdims=True)
    prob_low = low(jnp.exp(masked - log_total))
    return jnp.einsum('ghqk,gkhd->gqhd', prob_low, values, precision=highest)

def attention(queries, keys_low, values):
    groups, length = (queries.shape[0], queries.shape[1])
    block_rows = min(512, length)
    block_count = length // block_rows
    query_parts = queries.reshape(groups, block_count, block_rows, H, HD).transpose(1, 0, 2, 3, 4)
    starts = jnp.arange(block_count, dtype=jnp.int32) * block_rows
    checked = jax.checkpoint(block_attend)
    outputs = lax.map(lambda block_item: checked(block_item[0], block_item[1], keys_low, values), (query_parts, starts))
    return outputs.transpose(1, 0, 2, 3, 4).reshape(groups, length, H, HD)

def layer(inputs, w_qkv, w_fc1, w_out, w_fc2, params, cos_table, sin_table):
    groups = inputs.shape[0]
    row_mean = lax.optimization_barrier(jnp.mean(inputs, axis=-1, keepdims=True))
    centred = inputs - row_mean
    variance = lax.optimization_barrier(jnp.mean(centred * centred, axis=-1, keepdims=True))
    normed = centred * lax.rsqrt(variance + 1e-05)
    normal_low = low(normed * params[:, 0] + params[:, 1])
    bias_qkv = params[:, 2:5].T.reshape(3 * D)
    bias_fc1 = params[:, 6:10].T.reshape(FF)
    mixed_qkv = low_back(jnp.einsum('gtd,de->gte', normal_low, w_qkv, precision=highest) + bias_qkv)
    split_heads = mixed_qkv.reshape(groups, LEN, 3, H, HD)
    queries = low(rotate(split_heads[:, :, 0], cos_table, sin_table))
    keys_low = low(rotate(split_heads[:, :, 1], cos_table, sin_table))
    values = low(split_heads[:, :, 2])
    attended = low(low_back(attention(queries, keys_low, values))).reshape(groups, LEN, D)
    pre_act = low_back(jnp.einsum('gtd,df->gtf', normal_low, w_fc1, precision=highest) + bias_fc1)
    hidden = low(jax.nn.gelu(pre_act, approximate=True))
    attn_branch = jnp.einsum('gti,oi->gto', attended, w_out, precision=highest) + params[:, 5]
    mlp_branch = jnp.einsum('gtf,of->gto', hidden, w_fc2, precision=highest) + params[:, 10]
    return inputs + attn_branch + mlp_branch

def reference(tokens, cotangent, positions, wqkv_master, fc1_master, out_master, fc2_master, small_master, wqkv_first, wqkv_second, fc1_first, fc1_second, out_first, out_second, fc2_first, fc2_second, small_first, small_second):
    masters = (wqkv_master, fc1_master, out_master, fc2_master, small_master)
    lowered = tuple((weight.astype(jnp.bfloat16).astype(jnp.float32) for weight in masters))
    cos_table, sin_table = rotation_tables(positions)
    group_size = math.gcd(SEQS, 4)
    group_count = SEQS // group_size
    inputs = tokens.astype(jnp.float32).reshape(group_count, group_size, LEN, D)
    back_in = cotangent.astype(jnp.float32).reshape(group_count, group_size, LEN, D)
    cos_groups = cos_table.reshape(group_count, group_size, LEN, 1, ROT // 2)
    sin_groups = sin_table.reshape(group_count, group_size, LEN, 1, ROT // 2)

    def one_group(totals, block_item):
        block_in, block_back, block_cos, block_sin = block_item

        def forward(values_in, w_qkv, w_fc1, w_out, w_fc2, params):
            return layer(values_in, w_qkv, w_fc1, w_out, w_fc2, params, block_cos, block_sin)
        output, pullback = jax.vjp(forward, block_in, *lowered)
        gradients = pullback(block_back)
        totals = tuple((held + added for held, added in zip(totals, gradients[1:])))
        return (totals, (output, gradients[0]))
    zero_sums = tuple((jnp.zeros_like(weight) for weight in lowered))
    totals, (outputs, input_grads) = lax.scan(one_group, zero_sums, (inputs, back_in, cos_groups, sin_groups))
    mixed = outputs.reshape(SEQS, LEN, D).astype(jnp.bfloat16)
    input_grad = input_grads.reshape(SEQS, LEN, D)
    qkv_a, qkv_b, qkv_c = adamw(wqkv_master, wqkv_first, wqkv_second, totals[0], 0.04, 0.1)
    fc1_a, fc1_b, fc1_c = adamw(fc1_master, fc1_first, fc1_second, totals[1], 0.04, 0.1)
    out_a, out_b, out_c = adamw(out_master, out_first, out_second, totals[2], 0.4, 0.1)
    fc2_a, fc2_b, fc2_c = adamw(fc2_master, fc2_first, fc2_second, totals[3], 0.02, 0.1)
    small_a, small_b, small_c = adamw(small_master, small_first, small_second, totals[4], 0.3, 0.0)
    return (mixed, input_grad, qkv_a, qkv_b, qkv_c, fc1_a, fc1_b, fc1_c, out_a, out_b, out_c, fc2_a, fc2_b, fc2_c, small_a, small_b, small_c)
```

```python
import functools

import jax
import jax.numpy as jnp
from jax import lax
from jax.experimental import pallas as pl
from jax.experimental.pallas import tpu as pltpu
from jax.sharding import PartitionSpec as P

D = 2048
H = 32
HD = 64
ROT = 32
FF = 8192
STEP = 10
LANES = 128
BLOCK = 256

beta_one = 0.9
beta_two = 0.95
epsilon = 1e-08

f32 = jnp.float32
bf16 = jnp.bfloat16
EVERY = ("dp", "ctx")
GRANT = 56 * 1024 * 1024


def adamw(weight, first_old, second_old, gradient, step_rate, decay):
    first_new = beta_one * first_old + (1.0 - beta_one) * gradient
    second_new = beta_two * second_old + (1.0 - beta_two) * gradient * gradient
    first_hat = first_new / (1.0 - beta_one**STEP)
    second_hat = second_new / (1.0 - beta_two**STEP)
    weight_new = weight - step_rate * (
        first_hat / (jnp.sqrt(second_hat) + epsilon) + decay * weight
    )
    return (first_new, second_new, weight_new)


def mm(left, right, dims):
    return lax.dot_general(left, right, ((dims[:1], dims[1:]), ((), ())), preferred_element_type=f32)


def rotated(vals, cos_t, lead, trail):
    return (
        vals * cos_t + pltpu.roll(vals, LANES - 16, 1) * lead + pltpu.roll(vals, 16, 1) * trail
    )


def unrotated(vals, cos_t, lead, trail):
    return (
        vals * cos_t - pltpu.roll(vals, LANES - 16, 1) * lead - pltpu.roll(vals, 16, 1) * trail
    )


def attend_kernel(
    q_in, k_in, v_in, bias, cos_ref, lead_ref, trail_ref, q_out, k_out, v_out, o_out, log_out
):
    rows = q_in.shape[0]
    cos_t, lead, trail = cos_ref[...], lead_ref[...], trail_ref[...]
    scale = HD ** (-0.5)
    query = rotated(q_in[...] + bias[0:1, :], cos_t, lead, trail).astype(bf16)
    key = rotated(k_in[...] + bias[1:2, :], cos_t, lead, trail).astype(bf16)
    value = (v_in[...] + bias[2:3, :]).astype(bf16)
    query = query * jnp.asarray(scale, bf16)
    q_out[...] = query
    k_out[...] = key
    v_out[...] = value
    lane = lax.broadcasted_iota(jnp.int32, (BLOCK, LANES), 1)
    on_diagonal = lax.broadcasted_iota(jnp.int32, (BLOCK, BLOCK), 1) <= lax.broadcasted_iota(
        jnp.int32, (BLOCK, BLOCK), 0
    )
    for step in range(rows // BLOCK):
        start = step * BLOCK
        stop = start + BLOCK
        out = None
        for head in range(2):
            mine = (lane < HD) if head == 0 else (lane >= HD)
            q_head = jnp.where(mine, query[start:stop], jnp.zeros((), bf16))
            last = jnp.where(on_diagonal, mm(q_head, key[start:stop], (1, 1)), -1e30)
            parts = [last]
            if start:
                parts = [mm(q_head, key[:start], (1, 1)), last]
            best = functools.reduce(
                jnp.maximum, [jnp.max(part, axis=1, keepdims=True) for part in parts]
            )
            parts = [jnp.exp(part - best) for part in parts]
            total = sum(jnp.sum(part, axis=1, keepdims=True) for part in parts)
            log_out[0, head, start:stop] = (best + jnp.log(total))[:, 0]
            mixed = mm(parts[-1].astype(bf16), value[start:stop], (1, 0))
            if start:
                mixed = mixed + mm(parts[0].astype(bf16), value[:start], (1, 0))
            mixed = mixed / total
            out = mixed if head == 0 else jnp.where(mine, mixed, out)
        o_out[start:stop, :] = out.astype(bf16)


def attend_back_kernel(
    q_in, k_in, v_in, g_in, log_in, cos_ref, lead_ref, trail_ref, dq_out, dk_out, dv_out,
    dq_sum, dk_sum, dv_sum,
):
    rows = q_in.shape[0]
    scale = HD ** (-0.5)
    lane = lax.broadcasted_iota(jnp.int32, (BLOCK, LANES), 1)
    on_diagonal = lax.broadcasted_iota(jnp.int32, (BLOCK, BLOCK), 0) <= lax.broadcasted_iota(
        jnp.int32, (BLOCK, BLOCK), 1
    )
    dk_sum[...] = jnp.zeros_like(dk_sum)
    dv_sum[...] = jnp.zeros_like(dv_sum)
    key_all = k_in[...]
    value_all = v_in[...]
    zero = jnp.zeros((), bf16)
    for step in range(rows // BLOCK):
        start = step * BLOCK
        stop = start + BLOCK
        d_query = None
        for head in range(2):
            mine = (lane < HD) if head == 0 else (lane >= HD)
            q_head = jnp.where(mine, q_in[start:stop], zero)
            g_head = jnp.where(mine, g_in[start:stop], zero)
            log_row = log_in[0, head : head + 1, start:stop]
            last = jnp.where(
                on_diagonal, jnp.exp(mm(key_all[start:stop], q_head, (1, 1)) - log_row), 0.0
            )
            probs = [(start, stop, last)]
            if start:
                probs.append((0, start, jnp.exp(mm(key_all[:start], q_head, (1, 1)) - log_row)))
            grads = [mm(value_all[lo:hi], g_head, (1, 1)) for lo, hi, _ in probs]
            delta = sum(
                jnp.sum(prob * grad, axis=0, keepdims=True)
                for (_, _, prob), grad in zip(probs, grads)
            )
            part = None
            for (lo, hi, prob), grad in zip(probs, grads):
                d_score = (prob * (grad - delta)).astype(bf16)
                dv_sum[lo:hi, :] += mm(prob.astype(bf16), g_head, (1, 0))
                dk_sum[lo:hi, :] += mm(d_score, q_head, (1, 0))
                added = mm(d_score, key_all[lo:hi], (0, 0))
                part = added if part is None else part + added
            d_query = part if head == 0 else jnp.where(mine, part, d_query)
        dq_sum[start:stop, :] = d_query * scale
    cos_t, lead, trail = cos_ref[...], lead_ref[...], trail_ref[...]
    dq_out[...] = unrotated(dq_sum[...], cos_t, lead, trail).astype(bf16)
    dk_out[...] = unrotated(dk_sum[...], cos_t, lead, trail).astype(bf16)
    dv_out[...] = dv_sum[...].astype(bf16)


def attend(mixed_qkv, bias, tables, seqs):
    rows, width = mixed_qkv.shape[0] // seqs, mixed_qkv.shape[1] // 3
    pairs = width // LANES

    def part(which):
        return pl.BlockSpec((rows, LANES), lambda s, p: (s, which * pairs + p))

    block = pl.BlockSpec((rows, LANES), lambda s, p: (s, p))
    table = pl.BlockSpec((rows, LANES), lambda s, p: (s, 0))
    low = jax.ShapeDtypeStruct((seqs * rows, width), bf16)
    return pl.pallas_call(
        attend_kernel,
        grid=(seqs, pairs),
        in_specs=[part(0), part(1), part(2), pl.BlockSpec((3, LANES), lambda s, p: (0, p))]
        + [table] * 3,
        out_specs=[block] * 4 + [pl.BlockSpec((1, 2, rows), lambda s, p: (s * pairs + p, 0, 0))],
        out_shape=[low] * 4 + [jax.ShapeDtypeStruct((seqs * pairs, 2, rows), f32)],
        compiler_params=pltpu.CompilerParams(vmem_limit_bytes=GRANT),
        name="attend",
    )(mixed_qkv, mixed_qkv, mixed_qkv, bias, *tables)


def attend_back(query, key, value, back, log_total, tables, seqs):
    rows, width = query.shape[0] // seqs, query.shape[1]
    pairs = width // LANES
    block = pl.BlockSpec((rows, LANES), lambda s, p: (s, p))
    table = pl.BlockSpec((rows, LANES), lambda s, p: (s, 0))
    low = jax.ShapeDtypeStruct((seqs * rows, width), bf16)
    return pl.pallas_call(
        attend_back_kernel,
        grid=(seqs, pairs),
        in_specs=[block] * 4
        + [pl.BlockSpec((1, 2, rows), lambda s, p: (s * pairs + p, 0, 0))]
        + [table] * 3,
        out_specs=[block] * 3,
        out_shape=[low] * 3,
        scratch_shapes=[pltpu.VMEM((rows, LANES), f32)] * 3,
        compiler_params=pltpu.CompilerParams(vmem_limit_bytes=GRANT),
        name="attend_back",
    )(query, key, value, back, log_total, *tables)


def normalised(rows_in):
    row_mean = jnp.mean(rows_in, axis=-1, keepdims=True)
    centred = rows_in - row_mean
    variance = jnp.mean(centred * centred, axis=-1, keepdims=True)
    inv_std = lax.rsqrt(variance + 1e-05)
    return centred * inv_std, inv_std


def gelu_both(pre):
    return jax.vjp(lambda vals: jax.nn.gelu(vals, approximate=True), pre)


def per_device(
    tokens,
    cotangent,
    positions,
    wqkv_master,
    fc1_master,
    out_master,
    fc2_master,
    small_master,
    wqkv_first,
    wqkv_second,
    fc1_first,
    fc1_second,
    out_first,
    out_second,
    fc2_first,
    fc2_second,
    small_first,
    small_second,
):
    seqs, span = tokens.shape[0], tokens.shape[1]
    ctx, dp = lax.axis_size("ctx"), lax.axis_size("dp")
    ctx_index = lax.axis_index("ctx")
    length = span * ctx
    total_rows = seqs * length
    own_rows = wqkv_master.shape[0]
    head_cols, ff_cols = D // ctx, FF // ctx

    small_low = jnp.pad(small_master.astype(bf16), ((0, 0), (0, 5)))
    small_sent = jnp.broadcast_to(small_low.reshape(1, 1, own_rows * 16), (ctx * dp, 1, own_rows * 16))
    small_all = lax.all_to_all(small_sent, EVERY, 0, 0, tiled=True)
    params = small_all.reshape(D, 16).astype(f32)
    place = lax.all_gather(positions, "ctx", axis=1, tiled=True).reshape(total_rows)

    qkv_cut = wqkv_master.astype(bf16).reshape(own_rows, 3, ctx, head_cols)
    qkv_cut = jnp.transpose(qkv_cut, (2, 0, 1, 3)).reshape(ctx, own_rows, 3 * head_cols)

    def cut(master, cols):
        return jnp.transpose(master.astype(bf16).reshape(own_rows, ctx, cols), (1, 0, 2))

    cuts = jnp.concatenate(
        [qkv_cut, cut(fc1_master, ff_cols), cut(out_master, head_cols), cut(fc2_master, ff_cols)],
        axis=2,
    )
    mine = lax.all_to_all(cuts, "ctx", 0, 0, tiled=True).reshape(ctx * own_rows, -1)
    edges = [0, 3 * head_cols, 3 * head_cols + ff_cols, 4 * head_cols + ff_cols, 4 * head_cols + 2 * ff_cols]
    qkv_w = lax.all_gather(mine[:, edges[0] : edges[1]], "dp", axis=0, tiled=True)
    fc1_w = lax.all_gather(mine[:, edges[1] : edges[2]], "dp", axis=0, tiled=True)
    of_w = lax.all_gather(mine[:, edges[2] : edges[4]], "dp", axis=0, tiled=True)

    tok_all = lax.all_gather(tokens, "ctx", axis=1, tiled=True).reshape(total_rows, D)
    cot_all = lax.all_gather(cotangent, "ctx", axis=1, tiled=True).reshape(total_rows, D)

    half_rot = ROT // 2
    exponent = jnp.arange(half_rot, dtype=f32) * (-2.0 / ROT)
    frequency = jnp.power(f32(10000.0), exponent)
    angles = place.astype(f32)[:, None] * frequency
    cos_s, sin_s = jnp.cos(angles), jnp.sin(angles)
    none = jnp.zeros_like(cos_s)
    rest = jnp.zeros((total_rows, HD - ROT), f32)
    tables = [
        jnp.concatenate([cos_s, cos_s, rest + 1.0] * 2, axis=1),
        jnp.concatenate([-sin_s, none, rest] * 2, axis=1),
        jnp.concatenate([none, sin_s, rest] * 2, axis=1),
    ]

    def my_part(values, cols):
        return lax.dynamic_slice_in_dim(values, ctx_index * cols, cols, values.ndim - 1)

    qkv_bias = my_part(params[:, 2:5].T, head_cols)
    fc1_bias = my_part(params[:, 6:10].T.reshape(FF), ff_cols)
    gain, shift = params[:, 0], params[:, 1]

    normal_all = normalised(tok_all.astype(f32))[0]
    normal_low = (normal_all * gain + shift).astype(bf16)
    mixed_qkv = mm(normal_low, qkv_w, (1, 0))
    query, key, value, attended, log_total = attend(mixed_qkv, qkv_bias, tables, seqs)
    pre_act = mm(normal_low, fc1_w, (1, 0)) + fc1_bias
    hidden_full, gelu_pull = gelu_both(pre_act)
    hidden_low = hidden_full.astype(bf16)
    branch_in = jnp.concatenate([attended, hidden_low], axis=1)
    branch = mm(branch_in, of_w, (1, 1)).astype(bf16).reshape(seqs, length, D)
    branch = lax.psum_scatter(branch, "ctx", scatter_dimension=1, tiled=True)
    inputs = tokens.astype(f32)
    mixed = (inputs + branch.astype(f32) + params[:, 5] + params[:, 10]).astype(bf16)

    back = mm(cot_all, of_w[:, :head_cols], (1, 0)).astype(bf16)
    grad_hidden = mm(cot_all, of_w[:, head_cols:], (1, 0))
    d_pre = gelu_pull(grad_hidden)[0].astype(bf16)
    d_query, d_key, d_value = attend_back(query, key, value, back, log_total, tables, seqs)
    d_qkv = jnp.concatenate([d_query, d_key, d_value], axis=1)
    d_normal = (mm(d_qkv, qkv_w, (1, 1)) + mm(d_pre, fc1_w, (1, 1))).astype(bf16)
    d_normal = lax.psum_scatter(
        d_normal.reshape(seqs, length, D), "ctx", scatter_dimension=1, tiled=True
    ).astype(f32)

    of_grad = mm(cot_all, branch_in, (0, 0)).astype(bf16)
    of_grad = lax.psum_scatter(of_grad, "dp", scatter_dimension=0, tiled=True)
    fc1_grad = mm(normal_low, d_pre, (0, 0)).astype(bf16)
    fc1_grad = lax.psum_scatter(fc1_grad, "dp", scatter_dimension=0, tiled=True)
    qkv_grad = mm(normal_low, d_qkv, (0, 0)).astype(bf16)
    qkv_grad = lax.psum_scatter(qkv_grad, "dp", scatter_dimension=0, tiled=True)

    normed, inv_std = normalised(inputs)
    d_scaled = d_normal * gain
    grad_out = cotangent.astype(f32)
    input_grad = grad_out + inv_std * (
        d_scaled
        - jnp.mean(d_scaled, axis=-1, keepdims=True)
        - normed * jnp.mean(d_scaled * normed, axis=-1, keepdims=True)
    )

    def spread(sums, count, cols):
        whole = jnp.zeros((count, ctx * cols), f32)
        return lax.dynamic_update_slice_in_dim(whole, sums.reshape(count, cols), ctx_index * cols, 1)

    sum_qkv = spread(jnp.sum(d_qkv, axis=0, dtype=f32), 3, head_cols)
    sum_pre = spread(jnp.sum(d_pre, axis=0, dtype=f32), 1, ff_cols).reshape(4, D)
    sum_out = jnp.sum(grad_out, axis=(0, 1))[None]
    gain_terms = jnp.sum(d_normal * normed, axis=(0, 1))[None]
    shift_terms = jnp.sum(d_normal, axis=(0, 1))[None]
    small_terms = jnp.concatenate(
        [gain_terms, shift_terms, sum_qkv, sum_out, sum_pre, sum_out], axis=0
    )
    small_sent = jnp.transpose(small_terms.reshape(11, ctx * dp, own_rows), (1, 0, 2))
    small_got = lax.all_to_all(small_sent.reshape(ctx * dp, 1, 11 * own_rows), EVERY, 0, 0, tiled=True)
    small_grad = jnp.sum(small_got, axis=(0, 1)).reshape(11, own_rows).T

    grads = jnp.concatenate([qkv_grad, fc1_grad, of_grad], axis=1).reshape(ctx, own_rows, -1)
    grads = lax.all_to_all(grads, "ctx", 0, 0, tiled=True).astype(f32)

    def joined(lo, hi, count):
        piece = grads[:, :, lo:hi].reshape(ctx, own_rows, count, (hi - lo) // count)
        return jnp.transpose(piece, (1, 2, 0, 3)).reshape(own_rows, ctx * (hi - lo))

    qkv_new = adamw(wqkv_master, wqkv_first, wqkv_second, joined(edges[0], edges[1], 3), 0.04, 0.1)
    fc1_new = adamw(fc1_master, fc1_first, fc1_second, joined(edges[1], edges[2], 1), 0.04, 0.1)
    out_new = adamw(out_master, out_first, out_second, joined(edges[2], edges[3], 1), 0.4, 0.1)
    fc2_new = adamw(fc2_master, fc2_first, fc2_second, joined(edges[3], edges[4], 1), 0.02, 0.1)
    small_new = adamw(small_master, small_first, small_second, small_grad, 0.3, 0.0)
    return (mixed, input_grad, *qkv_new, *fc1_new, *out_new, *fc2_new, *small_new)


def solution(mesh):
    split = P("dp", "ctx", None)
    rows = P(("dp", "ctx"), None)
    return jax.shard_map(
        per_device,
        mesh=mesh,
        in_specs=(split, split, P("dp", "ctx")) + (rows,) * 15,
        out_specs=(split, split) + (rows,) * 15,
        check_vma=False,
    )
```

```python
import functools

import jax
import jax.numpy as jnp
from jax import lax
from jax.experimental import pallas as pl
from jax.experimental.pallas import tpu as pltpu
from jax.sharding import PartitionSpec as P

D = 2048
H = 32
HD = 64
ROT = 32
FF = 8192
STEP = 10
LANES = 128
BLOCK = 256

beta_one = 0.9
beta_two = 0.95
epsilon = 1e-08

f32 = jnp.float32
bf16 = jnp.bfloat16
EVERY = ("dp", "ctx")
GRANT = 58 * 1024 * 1024


def adamw(weight, first_old, second_old, gradient, step_rate, decay):
    first_new = beta_one * first_old + (1.0 - beta_one) * gradient
    second_new = beta_two * second_old + (1.0 - beta_two) * gradient * gradient
    first_hat = first_new / (1.0 - beta_one**STEP)
    second_hat = second_new / (1.0 - beta_two**STEP)
    weight_new = weight - step_rate * (
        first_hat / (jnp.sqrt(second_hat) + epsilon) + decay * weight
    )
    return (first_new, second_new, weight_new)


def mm(left, right, dims):
    return lax.dot_general(left, right, ((dims[:1], dims[1:]), ((), ())), preferred_element_type=f32)


def rotated(vals, cos_t, lead, trail):
    return (
        vals * cos_t + pltpu.roll(vals, LANES - 16, 1) * lead + pltpu.roll(vals, 16, 1) * trail
    )


def unrotated(vals, cos_t, lead, trail):
    return (
        vals * cos_t - pltpu.roll(vals, LANES - 16, 1) * lead - pltpu.roll(vals, 16, 1) * trail
    )


def attend_kernel(
    q_in, k_in, v_in, bias, cos_ref, lead_ref, trail_ref, q_out, k_out, v_out, o_out, log_out
):
    rows = q_in.shape[0]
    cos_t, lead, trail = cos_ref[...], lead_ref[...], trail_ref[...]
    scale = HD ** (-0.5)
    query = rotated(q_in[...] + bias[0:1, :], cos_t, lead, trail).astype(bf16)
    key = rotated(k_in[...] + bias[1:2, :], cos_t, lead, trail).astype(bf16)
    value = (v_in[...] + bias[2:3, :]).astype(bf16)
    query = query * jnp.asarray(scale, bf16)
    q_out[...] = query
    k_out[...] = key
    v_out[...] = value
    lane = lax.broadcasted_iota(jnp.int32, (BLOCK, LANES), 1)
    on_diagonal = lax.broadcasted_iota(jnp.int32, (BLOCK, BLOCK), 1) <= lax.broadcasted_iota(
        jnp.int32, (BLOCK, BLOCK), 0
    )
    for step in range(rows // BLOCK):
        start = step * BLOCK
        stop = start + BLOCK
        out = None
        for head in range(2):
            mine = (lane < HD) if head == 0 else (lane >= HD)
            q_head = jnp.where(mine, query[start:stop], jnp.zeros((), bf16))
            last = jnp.where(on_diagonal, mm(q_head, key[start:stop], (1, 1)), -1e30)
            parts = [last]
            if start:
                parts = [mm(q_head, key[:start], (1, 1)), last]
            best = functools.reduce(
                jnp.maximum, [jnp.max(part, axis=1, keepdims=True) for part in parts]
            )
            parts = [jnp.exp(part - best) for part in parts]
            total = sum(jnp.sum(part, axis=1, keepdims=True) for part in parts)
            log_out[0, head, start:stop] = (best + jnp.log(total))[:, 0]
            mixed = mm(parts[-1].astype(bf16), value[start:stop], (1, 0))
            if start:
                mixed = mixed + mm(parts[0].astype(bf16), value[:start], (1, 0))
            mixed = mixed / total
            out = mixed if head == 0 else jnp.where(mine, mixed, out)
        o_out[start:stop, :] = out.astype(bf16)


def attend_back_kernel(
    q_in, k_in, v_in, g_in, log_in, cos_ref, lead_ref, trail_ref, dq_out, dk_out, dv_out,
    dq_sum, dk_sum, dv_sum,
):
    rows = q_in.shape[0]
    scale = HD ** (-0.5)
    lane = lax.broadcasted_iota(jnp.int32, (BLOCK, LANES), 1)
    on_diagonal = lax.broadcasted_iota(jnp.int32, (BLOCK, BLOCK), 0) <= lax.broadcasted_iota(
        jnp.int32, (BLOCK, BLOCK), 1
    )
    dk_sum[...] = jnp.zeros_like(dk_sum)
    dv_sum[...] = jnp.zeros_like(dv_sum)
    key_all = k_in[...]
    value_all = v_in[...]
    zero = jnp.zeros((), bf16)
    for step in range(rows // BLOCK):
        start = step * BLOCK
        stop = start + BLOCK
        d_query = None
        for head in range(2):
            mine = (lane < HD) if head == 0 else (lane >= HD)
            q_head = jnp.where(mine, q_in[start:stop], zero)
            g_head = jnp.where(mine, g_in[start:stop], zero)
            log_row = log_in[0, head : head + 1, start:stop]
            last = jnp.where(
                on_diagonal, jnp.exp(mm(key_all[start:stop], q_head, (1, 1)) - log_row), 0.0
            )
            probs = [(start, stop, last)]
            if start:
                probs.append((0, start, jnp.exp(mm(key_all[:start], q_head, (1, 1)) - log_row)))
            grads = [mm(value_all[lo:hi], g_head, (1, 1)) for lo, hi, _ in probs]
            delta = sum(
                jnp.sum(prob * grad, axis=0, keepdims=True)
                for (_, _, prob), grad in zip(probs, grads)
            )
            part = None
            for (lo, hi, prob), grad in zip(probs, grads):
                d_score = (prob * (grad - delta)).astype(bf16)
                dv_sum[lo:hi, :] += mm(prob.astype(bf16), g_head, (1, 0))
                dk_sum[lo:hi, :] += mm(d_score, q_head, (1, 0))
                added = mm(d_score, key_all[lo:hi], (0, 0))
                part = added if part is None else part + added
            d_query = part if head == 0 else jnp.where(mine, part, d_query)
        dq_sum[start:stop, :] = d_query * scale
    cos_t, lead, trail = cos_ref[...], lead_ref[...], trail_ref[...]
    dq_out[...] = unrotated(dq_sum[...], cos_t, lead, trail).astype(bf16)
    dk_out[...] = unrotated(dk_sum[...], cos_t, lead, trail).astype(bf16)
    dv_out[...] = dv_sum[...].astype(bf16)


def attend(mixed_qkv, bias, tables, seqs):
    rows, width = mixed_qkv.shape[0] // seqs, mixed_qkv.shape[1] // 3
    pairs = width // LANES

    def part(which):
        return pl.BlockSpec((rows, LANES), lambda s, p: (s, which * pairs + p))

    block = pl.BlockSpec((rows, LANES), lambda s, p: (s, p))
    table = pl.BlockSpec((rows, LANES), lambda s, p: (s, 0))
    low = jax.ShapeDtypeStruct((seqs * rows, width), bf16)
    return pl.pallas_call(
        attend_kernel,
        grid=(seqs, pairs),
        in_specs=[part(0), part(1), part(2), pl.BlockSpec((3, LANES), lambda s, p: (0, p))]
        + [table] * 3,
        out_specs=[block] * 4 + [pl.BlockSpec((1, 2, rows), lambda s, p: (s * pairs + p, 0, 0))],
        out_shape=[low] * 4 + [jax.ShapeDtypeStruct((seqs * pairs, 2, rows), f32)],
        compiler_params=pltpu.CompilerParams(vmem_limit_bytes=GRANT),
        name="attend",
    )(mixed_qkv, mixed_qkv, mixed_qkv, bias, *tables)


def attend_back(query, key, value, back, log_total, tables, seqs):
    rows, width = query.shape[0] // seqs, query.shape[1]
    pairs = width // LANES
    block = pl.BlockSpec((rows, LANES), lambda s, p: (s, p))
    table = pl.BlockSpec((rows, LANES), lambda s, p: (s, 0))
    low = jax.ShapeDtypeStruct((seqs * rows, width), bf16)
    return pl.pallas_call(
        attend_back_kernel,
        grid=(seqs, pairs),
        in_specs=[block] * 4
        + [pl.BlockSpec((1, 2, rows), lambda s, p: (s * pairs + p, 0, 0))]
        + [table] * 3,
        out_specs=[block] * 3,
        out_shape=[low] * 3,
        scratch_shapes=[pltpu.VMEM((rows, LANES), f32)] * 3,
        compiler_params=pltpu.CompilerParams(vmem_limit_bytes=GRANT),
        name="attend_back",
    )(query, key, value, back, log_total, *tables)


def bits_of(count):
    bits = []
    bit = 1
    while bit < count:
        bits.append(bit)
        bit *= 2
    return bits


def flipped(index, bit):
    return index + bit * (1 - 2 * ((index // bit) % 2))


def run_chains(chains):
    chains = [chain for chain in chains]
    for chain in chains:
        next(chain)
    while chains:
        left = []
        for chain in chains:
            try:
                next(chain)
                left.append(chain)
            except StopIteration:
                pass
        chains = left


class Sems:
    def __init__(self, send, recv):
        self.send, self.recv, self.used = send, recv, 0

    def take(self):
        self.used += 1
        return self.send.at[self.used - 1], self.recv.at[self.used - 1]


def remote(src, dst, sems, target):
    return pltpu.make_async_remote_copy(
        src_ref=src,
        dst_ref=dst,
        send_sem=sems[0],
        recv_sem=sems[1],
        device_id=target,
        device_id_type=pl.DeviceIdType.MESH,
    )


def greet(ctx, dp):
    here, mine = lax.axis_index("ctx"), lax.axis_index("dp")
    barrier = pltpu.get_barrier_semaphore()
    targets = [{"ctx": lax.rem(here + by, ctx)} for by in range(1, ctx)]
    targets += [{"dp": flipped(mine, bit)} for bit in bits_of(dp)]
    for target in targets:
        pl.semaphore_signal(barrier, inc=1, device_id=target, device_id_type=pl.DeviceIdType.MESH)
    pl.semaphore_wait(barrier, len(targets))


def line_chain(src, out, sems, ctx):
    here = lax.axis_index("ctx")
    ups = [sems.take() for _ in range(1, ctx)]
    downs = [sems.take() for _ in range(1, ctx)]

    def hop(block, slot, step, going):
        by = 1 if going is ups else -1
        return remote(block, out.at[slot], going[step], {"ctx": here + by})

    @pl.when(here < ctx - 1)
    def _():
        hop(src, here, 0, ups).start()

    @pl.when(here > 0)
    def _():
        hop(src, here, 0, downs).start()

    yield
    for step in range(1, ctx):
        for going, sign in ((ups, -1), (downs, 1)):
            slot = here + sign * step
            inside = (slot >= 0) if sign < 0 else (slot < ctx)
            more = (here < ctx - 1) if sign < 0 else (here > 0)
            if step < ctx - 1:

                @pl.when(jnp.logical_and(inside, more))
                def _():
                    hop(out.at[slot], slot, step - 1, going).wait_recv()
                    hop(out.at[slot], slot, step, going).start()

                @pl.when(jnp.logical_and(inside, jnp.logical_not(more)))
                def _():
                    hop(out.at[slot], slot, step - 1, going).wait_recv()

            else:

                @pl.when(inside)
                def _():
                    hop(out.at[slot], slot, step - 1, going).wait_recv()

        yield

    for step in range(ctx - 1):
        for going, sign in ((ups, -1), (downs, 1)):
            slot = here + sign * step
            inside = (slot >= 0) if sign < 0 else (slot < ctx)
            more = (here < ctx - 1) if sign < 0 else (here > 0)

            @pl.when(jnp.logical_and(inside, more))
            def _():
                hop(out.at[slot], slot, step, going).wait_send()


def weight_chain(cut, out, sems, own_sem, ctx, dp):
    here, mine = lax.axis_index("ctx"), lax.axis_index("dp")
    rows = cut.shape[1]
    slab = rows * ctx
    half = slab // 2

    def piece(owner):
        return out.at[pl.ds(pl.multiple_of((mine * ctx + owner) * rows, rows), rows)]

    def part(owner, which):
        return out.at[pl.ds(pl.multiple_of(owner * slab + which * half, half), half)]

    trades = []
    for by in range(1, ctx):
        peer = lax.rem(here + by, ctx)
        sem = sems.take()
        copy = remote(cut.at[peer], piece(here), sem, {"ctx": peer})
        copy.start()
        trades.append((copy, remote(cut.at[peer], piece(lax.rem(here + ctx - by, ctx)), sem, {"ctx": peer})))
    own = pltpu.make_async_copy(cut.at[here], piece(here), own_sem)
    own.start()
    yield
    for _, arrival in trades:
        arrival.wait_recv()
    own.wait()
    far = bits_of(dp)[1:]
    orders = [far + [1], far[::-1] + [1]]
    held = [[mine], [mine]]
    sent = []
    for stage in range(len(far) + 1):
        arrivals = []
        for which in range(2):
            bit = orders[which][stage]
            for owner in list(held[which]):
                sem = sems.take()
                copy = remote(part(owner, which), part(owner, which), sem, {"dp": flipped(mine, bit)})
                copy.start()
                sent.append(copy)
                coming = flipped(owner, bit)
                arrivals.append(remote(part(coming, which), part(coming, which), sem, {"dp": flipped(mine, bit)}))
                held[which].append(coming)
        yield
        for arrival in arrivals:
            arrival.wait_recv()
    for copy, _ in trades:
        copy.wait_send()
    for copy in sent:
        copy.wait_send()


def gather_kernel(ctx, dp, seqs, groups, *refs):
    tokens, places, cuts = refs[0], refs[1], refs[2 : 2 + groups]
    tok_out, place_out, outs = refs[2 + groups], refs[3 + groups], refs[4 + groups : 4 + 2 * groups]
    send, recv, own_sems, tok_sems = refs[4 + 2 * groups :]
    here = lax.axis_index("ctx")
    sems = Sems(send, recv)
    greet(ctx, dp)
    chains = [line_chain(places, place_out, sems, ctx)]
    for group in range(groups):
        chains.append(weight_chain(cuts[group], outs[group], sems, own_sems.at[group], ctx, dp))
        if group < seqs:
            chains.append(line_chain(tokens.at[group], tok_out.at[group], sems, ctx))
    for seq in range(groups, seqs):
        chains.append(line_chain(tokens.at[seq], tok_out.at[seq], sems, ctx))
    locals_ = [
        pltpu.make_async_copy(tokens.at[seq], tok_out.at[seq, here], tok_sems.at[seq])
        for seq in range(seqs)
    ]
    locals_.append(pltpu.make_async_copy(places, place_out.at[here], tok_sems.at[seqs]))
    for copy in locals_:
        copy.start()
    run_chains(chains)
    for copy in locals_:
        copy.wait()


def gather_all(tokens, places, cuts, ctx, dp):
    seqs, span = tokens.shape[0], tokens.shape[1]
    groups = len(cuts)
    copies = (seqs + 1) * 2 * (ctx - 1) + groups * (ctx - 1 + 2 * (dp - 1))
    hbm = pl.BlockSpec(memory_space=pl.ANY)
    outs = pl.pallas_call(
        functools.partial(gather_kernel, ctx, dp, seqs, groups),
        in_specs=[hbm] * (2 + groups),
        out_specs=[hbm] * (2 + groups),
        out_shape=[
            jax.ShapeDtypeStruct((seqs, ctx, span, D), bf16),
            jax.ShapeDtypeStruct((ctx,) + places.shape, f32),
        ]
        + [jax.ShapeDtypeStruct((dp * ctx * cut.shape[1], cut.shape[2]), bf16) for cut in cuts],
        scratch_shapes=[
            pltpu.SemaphoreType.DMA((copies,)),
            pltpu.SemaphoreType.DMA((copies,)),
            pltpu.SemaphoreType.DMA((groups,)),
            pltpu.SemaphoreType.DMA((seqs + 1,)),
        ],
        compiler_params=pltpu.CompilerParams(collective_id=1, has_side_effects=True),
        name="gather_all",
    )(tokens, places, *cuts)
    return outs[0], outs[1], outs[2:]


def add_into(target, other, rows):
    step = 32

    @pl.loop(0, rows // step)
    def _(index):
        here = pl.ds(pl.multiple_of(index * step, step), step)
        target[here, :] = target[here, :] + other[here, :]


def without(pattern, bit):
    return tuple(item for item in pattern if item != bit)


def patterns_of(bits):
    found = [()]
    for bit in bits:
        found += [pattern + (bit,) for pattern in found]
    return found


def owner_of(mine, pattern):
    for bit in pattern:
        mine = flipped(mine, bit)
    return mine


def pooled_chain(grad, out, own, land_core, lands, sems, own_sems, ctx, dp):
    here, mine = lax.axis_index("ctx"), lax.axis_index("dp")
    slab = grad.shape[0] // dp
    rows, half = slab // ctx, slab // 2
    far = bits_of(dp)[1:]
    patterns = sorted(patterns_of(far), key=len, reverse=True)
    partner = flipped(mine, 1)

    def slab_at(owner):
        return grad.at[pl.ds(pl.multiple_of(owner * slab, slab), slab)]

    sent, arrivals, loads = [], [], []
    for index, pattern in enumerate(patterns):
        copy = remote(
            slab_at(owner_of(partner, pattern)), land_core.at[index], sems.take(), {"dp": partner}
        )
        copy.start()
        sent.append(copy)
        load = pltpu.make_async_copy(
            slab_at(owner_of(mine, pattern)), own.at[index], own_sems.at[index]
        )
        load.start()
        loads.append(load)
    yield
    held = [{}, {}]
    for index, pattern in enumerate(patterns):
        loads[index].wait()
        sent[index].wait_recv()
        add_into(land_core.at[index], own.at[index], slab)
        for which in range(2):
            held[which][pattern] = land_core.at[index, pl.ds(which * half, half)]
        if index == len(patterns) // 2 - 1:
            yield
    orders = [far, far[::-1]]
    used = 0
    for stage in range(len(far)):
        arrivals = []
        for which in range(2):
            bit = orders[which][stage]
            kept = {}
            for pattern, block in held[which].items():
                if bit in pattern:
                    landing = lands.at[used]
                    used += 1
                    copy = remote(block, landing, sems.take(), {"dp": flipped(mine, bit)})
                    copy.start()
                    sent.append(copy)
                    rest = without(pattern, bit)
                    arrivals.append((copy, landing, held[which][rest]))
                    kept[rest] = landing
            held[which] = kept
        yield
        for copy, landing, block in arrivals:
            copy.wait_recv()
            add_into(landing, block, half)
    final = [held[0][()], held[1][()]]
    trades = []
    for by in range(1, ctx):
        peer = lax.rem(here + by, ctx)
        source = lax.rem(here + ctx - by, ctx)
        sem = sems.take()

        def piece(which, peer=peer):
            first = pl.multiple_of(peer * rows - which * half, rows)
            return final[which].at[pl.ds(first, rows)]

        for which in range(2):

            @pl.when(peer // (ctx // 2) == which)
            def _():
                remote(piece(which), out.at[here], sem, {"ctx": peer}).start()

        trades.append((sem, peer, source))
    own_piece = []
    for which in range(2):

        @pl.when(here // (ctx // 2) == which)
        def _():
            first = pl.multiple_of(here * rows - which * half, rows)
            copy = pltpu.make_async_copy(
                final[which].at[pl.ds(first, rows)], out.at[here], own_sems.at[0]
            )
            copy.start()
            copy.wait()

    yield
    some = final[0].at[pl.ds(0, rows)]
    for sem, peer, source in trades:
        remote(some, out.at[source], sem, {"ctx": peer}).wait_recv()
    for sem, peer, source in trades:
        remote(some, out.at[source], sem, {"ctx": peer}).wait_send()
    for copy in sent:
        copy.wait_send()


def sum_chain(partial, out, held, downs_land, ups_land, sems, load_sem, ctx):
    here = lax.axis_index("ctx")
    rows = held.shape[0] // ctx
    load = pltpu.make_async_copy(partial, held, load_sem)
    load.start()
    down_sems = [sems.take() for _ in range(1, ctx)]
    up_sems = [sems.take() for _ in range(1, ctx)]

    def chunk(index):
        return held.at[pl.ds(pl.multiple_of(index * rows, rows), rows)]

    def hop(block, step, down):
        lands, going = (downs_land, down_sems) if down else (ups_land, up_sems)
        by = -1 if down else 1
        return remote(block, lands.at[step - 1], going[step - 1], {"ctx": here + by})

    load.wait()

    @pl.when(here == ctx - 1)
    def _():
        for step in range(1, ctx):
            hop(chunk(step - 1), step, True).start()

    @pl.when(here == 0)
    def _():
        for step in range(1, ctx):
            hop(chunk(ctx - step), step, False).start()

    yield
    for step in range(2, ctx):

        @pl.when(jnp.logical_and(here < ctx - 1, here + step - ctx >= 0))
        def _():
            block = downs_land.at[step - 2]
            hop(block, step - 1, True).wait_recv()
            add_into(block, chunk(here + step - ctx), rows)
            hop(block, step, True).start()

        @pl.when(jnp.logical_and(here > 0, here + ctx - step <= ctx - 1))
        def _():
            block = ups_land.at[step - 2]
            hop(block, step - 1, False).wait_recv()
            add_into(block, chunk(here + ctx - step), rows)
            hop(block, step, False).start()

        yield

    @pl.when(here < ctx - 1)
    def _():
        hop(downs_land.at[ctx - 2], ctx - 1, True).wait_recv()

    @pl.when(here > 0)
    def _():
        hop(ups_land.at[ctx - 2], ctx - 1, False).wait_recv()

    step = 32

    @pl.loop(0, rows // step)
    def _(index):
        at = pl.ds(pl.multiple_of(index * step, step), step)
        mine = held[pl.ds(pl.multiple_of(here * rows + index * step, step), step), :].astype(f32)
        down = downs_land[ctx - 2, at, :].astype(f32)
        up = ups_land[ctx - 2, at, :].astype(f32)
        out[at, :] = (
            mine + jnp.where(here < ctx - 1, down, 0.0) + jnp.where(here > 0, up, 0.0)
        )

    for step in range(1, ctx):

        @pl.when(here + step - ctx >= 0)
        def _():
            hop(chunk(0), step, True).wait_send()

        @pl.when(here + ctx - step <= ctx - 1)
        def _():
            hop(chunk(0), step, False).wait_send()


def reduce_kernel(ctx, dp, groups, *refs):
    partial, grads = refs[0], refs[1 : 1 + groups]
    sum_out, outs = refs[1 + groups], refs[2 + groups : 2 + 2 * groups]
    held, downs_land, ups_land = refs[2 + 2 * groups : 5 + 2 * groups]
    own, land_core, lands = (
        refs[5 + 2 * groups + part * groups : 5 + 2 * groups + (part + 1) * groups]
        for part in range(3)
    )
    send, recv, load_sem, own_sems = refs[5 + 5 * groups :]
    sems = Sems(send, recv)
    greet(ctx, dp)
    chains = [sum_chain(partial, sum_out, held, downs_land, ups_land, sems, load_sem, ctx)]
    for group in range(groups):
        chains.append(
            pooled_chain(
                grads[group], outs[group], own[group], land_core[group], lands[group],
                sems, own_sems.at[group], ctx, dp,
            )
        )
    run_chains(chains)


def reduce_all(partial, grads, ctx, dp):
    groups = len(grads)
    rows = partial.shape[0] // ctx
    slab = grads[0].shape[0] // dp
    copies = 2 * (ctx - 1) + groups * (dp // 2 + dp - 2 + ctx - 1)
    hbm = pl.BlockSpec(memory_space=pl.ANY)
    vmem = pl.BlockSpec(memory_space=pltpu.VMEM)
    cols = [grad.shape[1] for grad in grads]
    outs = pl.pallas_call(
        functools.partial(reduce_kernel, ctx, dp, groups),
        in_specs=[hbm] * (1 + groups),
        out_specs=[vmem] + [hbm] * groups,
        out_shape=[jax.ShapeDtypeStruct((rows, partial.shape[1]), f32)]
        + [jax.ShapeDtypeStruct((ctx, slab // ctx, width), bf16) for width in cols],
        scratch_shapes=[pltpu.VMEM(partial.shape, bf16)]
        + [pltpu.VMEM((ctx - 1, rows, partial.shape[1]), bf16)] * 2
        + [pltpu.VMEM((dp // 2, slab, width), bf16) for width in cols] * 2
        + [pltpu.VMEM((dp - 2, slab // 2, width), bf16) for width in cols]
        + [
            pltpu.SemaphoreType.DMA((copies,)),
            pltpu.SemaphoreType.DMA((copies,)),
            pltpu.SemaphoreType.DMA,
            pltpu.SemaphoreType.DMA((groups, dp // 2)),
        ],
        compiler_params=pltpu.CompilerParams(
            collective_id=2, has_side_effects=True, vmem_limit_bytes=GRANT
        ),
        name="reduce_all",
    )(partial, *grads)
    return outs[0], outs[1:]


def normalised(rows_in):
    row_mean = jnp.mean(rows_in, axis=-1, keepdims=True)
    centred = rows_in - row_mean
    variance = jnp.mean(centred * centred, axis=-1, keepdims=True)
    inv_std = lax.rsqrt(variance + 1e-05)
    return centred * inv_std, inv_std


def gelu_both(pre):
    return jax.vjp(lambda vals: jax.nn.gelu(vals, approximate=True), pre)


def per_device(
    tokens,
    cotangent,
    positions,
    wqkv_master,
    fc1_master,
    out_master,
    fc2_master,
    small_master,
    wqkv_first,
    wqkv_second,
    fc1_first,
    fc1_second,
    out_first,
    out_second,
    fc2_first,
    fc2_second,
    small_first,
    small_second,
):
    seqs, span = tokens.shape[0], tokens.shape[1]
    ctx, dp = lax.axis_size("ctx"), lax.axis_size("dp")
    ctx_index = lax.axis_index("ctx")
    length = span * ctx
    total_rows = seqs * length
    own_rows = wqkv_master.shape[0]
    head_cols, ff_cols = D // ctx, FF // ctx

    def cut(master, count, cols):
        pieces = master.astype(bf16).reshape(own_rows, count, ctx, cols)
        return jnp.transpose(pieces, (2, 0, 1, 3)).reshape(ctx, own_rows, count * cols)

    gate = lax.optimization_barrier
    small_cut = jnp.pad(small_master.astype(bf16), ((0, 0), (0, LANES - small_master.shape[1])))
    cuts = [
        jnp.concatenate([cut(wqkv_master, 3, head_cols), cut(fc1_master, 1, ff_cols)], axis=2),
        jnp.concatenate([cut(out_master, 1, head_cols), cut(fc2_master, 1, ff_cols)], axis=2),
        jnp.broadcast_to(small_cut[None], (ctx,) + small_cut.shape),
    ]
    places = jnp.pad(positions.astype(f32).reshape(-1, LANES), ((0, 8 - seqs * span // LANES), (0, 0)))
    tok_all, place, (in_w, of_w, small_all) = gather_all(tokens, places, cuts, ctx, dp)
    qkv_w, fc1_w = in_w[:, : 3 * head_cols], in_w[:, 3 * head_cols :]
    params = small_all[:, :16].astype(f32)
    place = place[:, : seqs * span // LANES].reshape(ctx, seqs, span)
    place = jnp.transpose(place, (1, 0, 2)).reshape(total_rows)
    half_rot = ROT // 2
    exponent = jnp.arange(half_rot, dtype=f32) * (-2.0 / ROT)
    frequency = jnp.power(f32(10000.0), exponent)
    angles = place[:, None] * frequency
    cos_s, sin_s = jnp.cos(angles), jnp.sin(angles)
    none = jnp.zeros_like(cos_s)
    rest = jnp.zeros((total_rows, HD - ROT), f32)
    tables = [
        jnp.concatenate([cos_s, cos_s, rest + 1.0] * 2, axis=1),
        jnp.concatenate([-sin_s, none, rest] * 2, axis=1),
        jnp.concatenate([none, sin_s, rest] * 2, axis=1),
    ]

    def my_part(values, cols):
        return lax.dynamic_slice_in_dim(values, ctx_index * cols, cols, values.ndim - 1)

    qkv_bias = my_part(params[:, 2:5].T, head_cols)
    fc1_bias = my_part(params[:, 6:10].T.reshape(FF), ff_cols)
    gain, shift = params[:, 0], params[:, 1]
    seq_tables = [
        [table[seq * length : (seq + 1) * length] for table in tables] for seq in range(seqs)
    ]

    def norm_of(seq):
        return (normalised(tok_all[seq].reshape(length, D).astype(f32))[0] * gain + shift).astype(bf16)

    def attend_of(seq):
        projected = mm(normal_low[seq], qkv_w, (1, 0))
        return attend(projected, qkv_bias, seq_tables[seq], 1)

    def hidden_of(seq):
        return mm(normal_low[seq], fc1_w, (1, 0)) + fc1_bias

    def branch_of(seq):
        joined_in = jnp.concatenate([attn[seq][3], gelu_both(pre[seq])[0].astype(bf16)], axis=1)
        return joined_in, mm(joined_in, of_w, (1, 1)).astype(bf16)

    def back_of(seq):
        grad_hidden = mm(cot_all[seq], of_w[:, head_cols:], (1, 0))
        return (
            mm(cot_all[seq], of_w[:, :head_cols], (1, 0)).astype(bf16),
            gelu_both(pre[seq])[1](grad_hidden)[0].astype(bf16),
        )

    def attend_back_of(seq):
        query, key, value, _, log_total = attn[seq]
        parts = attend_back(query, key, value, back[seq], log_total, seq_tables[seq], 1)
        return jnp.concatenate(parts, axis=1)

    def normal_back_of(seq):
        part = mm(d_qkv[seq], qkv_w, (1, 1)) + mm(d_pre[seq], fc1_w, (1, 1))
        return part.astype(bf16)

    def summed(lefts, rights):
        left, right = jnp.concatenate(lefts, axis=0), jnp.concatenate(rights, axis=0)
        return mm(left, right, (0, 0)).astype(bf16)

    def gathered(block):
        return lax.all_gather(block, "ctx", axis=0, tiled=True)

    def scattered(partial):
        return lax.psum_scatter(partial, "ctx", scatter_dimension=0, tiled=True).astype(f32)

    two = [None] * seqs
    normal_low, attn, pre, branch_in, mix, back, d_pre, d_qkv, d_sum, cot_all = (
        list(two) for _ in range(10)
    )
    d_sum = list(two)
    cot, tok_all = gate(([cotangent[seq] for seq in range(seqs)], tok_all))
    cot_all[0] = gathered(cot[0])
    normal_low[0] = norm_of(0)
    attn[0] = attend_of(0)
    cot[1], normal_low[0], attn[0], tok_all = gate((cot[1], normal_low[0], attn[0], tok_all))
    cot_all[1] = gathered(cot[1])
    normal_low[1] = norm_of(1)
    attn[1] = attend_of(1)
    normal_low, attn = gate((normal_low, attn))
    pre = [hidden_of(0), hidden_of(1)]
    normal_low, pre, attn = gate((normal_low, pre, attn))
    for seq in range(seqs):
        branch_in[seq], part = branch_of(seq)
        mix[seq] = scattered(part)
    pre, attn, branch_in = gate((pre, attn, branch_in))
    for seq in range(seqs):
        back[seq], d_pre[seq] = back_of(seq)
        d_qkv[seq] = attend_back_of(seq)
        d_sum[seq] = normal_back_of(seq)
        if seq == 0:
            pre, attn, d_qkv[0], d_pre[0], part = gate(
                (pre, attn, d_qkv[0], d_pre[0], d_sum[0])
            )
            d_sum[0] = scattered(part)
    last, grads = reduce_all(
        d_sum[1],
        [summed(normal_low, d_qkv), summed(normal_low, d_pre), summed(cot_all, branch_in)],
        ctx,
        dp,
    )
    qkv_grad, fc1_grad, of_grad = (grad.astype(f32) for grad in grads)
    d_normal = [d_sum[0], last]
    mixed = [
        (tokens[seq].astype(f32) + mix[seq] + params[:, 5] + params[:, 10]).astype(bf16)
        for seq in range(seqs)
    ]
    d_normal = jnp.stack(d_normal)
    normed, inv_std = normalised(tokens.astype(f32))
    d_scaled = d_normal * gain
    grad_out = cotangent.astype(f32)
    input_grad = grad_out + inv_std * (
        d_scaled
        - jnp.mean(d_scaled, axis=-1, keepdims=True)
        - normed * jnp.mean(d_scaled * normed, axis=-1, keepdims=True)
    )

    def spread(parts, count, cols):
        sums = sum(jnp.sum(part, axis=0, dtype=f32) for part in parts).reshape(count, cols)
        whole = jnp.zeros((count, ctx * cols), f32)
        return lax.dynamic_update_slice_in_dim(whole, sums, ctx_index * cols, 1)

    sum_qkv = spread(d_qkv, 3, head_cols)
    sum_pre = spread(d_pre, 1, ff_cols).reshape(4, D)
    sum_out = jnp.sum(grad_out, axis=(0, 1))[None]
    gain_terms = jnp.sum(d_normal * normed, axis=(0, 1))[None]
    shift_terms = jnp.sum(d_normal, axis=(0, 1))[None]
    small_terms = jnp.concatenate(
        [gain_terms, shift_terms, sum_qkv, sum_out, sum_pre, sum_out], axis=0
    )
    small_sent = jnp.transpose(small_terms.reshape(11, ctx * dp, own_rows), (1, 0, 2))
    small_got = lax.all_to_all(small_sent.reshape(ctx * dp, 1, 11 * own_rows), EVERY, 0, 0, tiled=True)
    small_grad = jnp.sum(small_got, axis=(0, 1)).reshape(11, own_rows).T

    def joined(piece, count):
        piece = piece.reshape(ctx, own_rows, count, -1)
        return jnp.transpose(piece, (1, 2, 0, 3)).reshape(own_rows, -1)

    qkv_new = adamw(wqkv_master, wqkv_first, wqkv_second, joined(qkv_grad, 3), 0.04, 0.1)
    fc1_new = adamw(fc1_master, fc1_first, fc1_second, joined(fc1_grad, 1), 0.04, 0.1)
    out_new = adamw(out_master, out_first, out_second, joined(of_grad[:, :, :head_cols], 1), 0.4, 0.1)
    fc2_new = adamw(fc2_master, fc2_first, fc2_second, joined(of_grad[:, :, head_cols:], 1), 0.02, 0.1)
    small_new = adamw(small_master, small_first, small_second, small_grad, 0.3, 0.0)
    return (jnp.stack(mixed), input_grad, *qkv_new, *fc1_new, *out_new, *fc2_new, *small_new)


def solution(mesh):
    split = P("dp", "ctx", None)
    rows = P(("dp", "ctx"), None)
    return jax.shard_map(
        per_device,
        mesh=mesh,
        in_specs=(split, split, P("dp", "ctx")) + (rows,) * 15,
        out_specs=(split, split) + (rows,) * 15,
        check_vma=False,
    )
```

```python
import functools

import jax
import jax.numpy as jnp
from jax import lax
from jax.experimental import pallas as pl
from jax.experimental.pallas import tpu as pltpu
from jax.sharding import PartitionSpec as P

D = 2048
H = 32
HD = 64
ROT = 32
FF = 8192
STEP = 10
LANES = 128
BLOCK = 256

beta_one = 0.9
beta_two = 0.95
epsilon = 1e-08

f32 = jnp.float32
bf16 = jnp.bfloat16
EVERY = ("dp", "ctx")
GRANT = 58 * 1024 * 1024


def adamw(weight, first_old, second_old, gradient, step_rate, decay):
    first_new = beta_one * first_old + (1.0 - beta_one) * gradient
    second_new = beta_two * second_old + (1.0 - beta_two) * gradient * gradient
    first_hat = first_new / (1.0 - beta_one**STEP)
    second_hat = second_new / (1.0 - beta_two**STEP)
    weight_new = weight - step_rate * (
        first_hat / (jnp.sqrt(second_hat) + epsilon) + decay * weight
    )
    return (first_new, second_new, weight_new)


def mm(left, right, dims):
    return lax.dot_general(left, right, ((dims[:1], dims[1:]), ((), ())), preferred_element_type=f32)


def rotated(vals, cos_t, lead, trail):
    return (
        vals * cos_t + pltpu.roll(vals, LANES - 16, 1) * lead + pltpu.roll(vals, 16, 1) * trail
    )


def unrotated(vals, cos_t, lead, trail):
    return (
        vals * cos_t - pltpu.roll(vals, LANES - 16, 1) * lead - pltpu.roll(vals, 16, 1) * trail
    )


def attend_kernel(
    q_in, k_in, v_in, bias, cos_ref, lead_ref, trail_ref, q_out, k_out, v_out, o_out, log_out
):
    rows = q_in.shape[0]
    cos_t, lead, trail = cos_ref[...].T, lead_ref[...].T, trail_ref[...].T
    scale = HD ** (-0.5)
    query = rotated(q_in[...] + bias[0:1, :], cos_t, lead, trail).astype(bf16)
    key = rotated(k_in[...] + bias[1:2, :], cos_t, lead, trail).astype(bf16)
    value = (v_in[...] + bias[2:3, :]).astype(bf16)
    query = query * jnp.asarray(scale, bf16)
    q_out[...] = query
    k_out[...] = key
    v_out[...] = value
    lane = lax.broadcasted_iota(jnp.int32, (BLOCK, LANES), 1)
    on_diagonal = lax.broadcasted_iota(jnp.int32, (BLOCK, BLOCK), 1) <= lax.broadcasted_iota(
        jnp.int32, (BLOCK, BLOCK), 0
    )
    for step in range(rows // BLOCK):
        start = step * BLOCK
        stop = start + BLOCK
        out = None
        for head in range(2):
            mine = (lane < HD) if head == 0 else (lane >= HD)
            q_head = jnp.where(mine, query[start:stop], jnp.zeros((), bf16))
            last = jnp.where(on_diagonal, mm(q_head, key[start:stop], (1, 1)), -1e30)
            parts = [last]
            if start:
                parts = [mm(q_head, key[:start], (1, 1)), last]
            best = functools.reduce(
                jnp.maximum, [jnp.max(part, axis=1, keepdims=True) for part in parts]
            )
            parts = [jnp.exp(part - best) for part in parts]
            total = sum(jnp.sum(part, axis=1, keepdims=True) for part in parts)
            log_out[0, head, start:stop] = (best + jnp.log(total))[:, 0]
            mixed = mm(parts[-1].astype(bf16), value[start:stop], (1, 0))
            if start:
                mixed = mixed + mm(parts[0].astype(bf16), value[:start], (1, 0))
            mixed = mixed / total
            out = mixed if head == 0 else jnp.where(mine, mixed, out)
        o_out[start:stop, :] = out.astype(bf16)


def attend_back_kernel(
    q_in, k_in, v_in, g_in, log_in, cos_ref, lead_ref, trail_ref, d_out, dq_sum, dk_sum, dv_sum
):
    rows = q_in.shape[0]
    scale = HD ** (-0.5)
    lane = lax.broadcasted_iota(jnp.int32, (BLOCK, LANES), 1)
    on_diagonal = lax.broadcasted_iota(jnp.int32, (BLOCK, BLOCK), 0) <= lax.broadcasted_iota(
        jnp.int32, (BLOCK, BLOCK), 1
    )
    dk_sum[...] = jnp.zeros_like(dk_sum)
    dv_sum[...] = jnp.zeros_like(dv_sum)
    key_all = k_in[...]
    value_all = v_in[...]
    zero = jnp.zeros((), bf16)
    for step in range(rows // BLOCK):
        start = step * BLOCK
        stop = start + BLOCK
        d_query = None
        for head in range(2):
            mine = (lane < HD) if head == 0 else (lane >= HD)
            q_head = jnp.where(mine, q_in[start:stop], zero)
            g_head = jnp.where(mine, g_in[start:stop], zero)
            log_row = log_in[0, head : head + 1, start:stop]
            last = jnp.where(
                on_diagonal, jnp.exp(mm(key_all[start:stop], q_head, (1, 1)) - log_row), 0.0
            )
            probs = [(start, stop, last)]
            if start:
                probs.append((0, start, jnp.exp(mm(key_all[:start], q_head, (1, 1)) - log_row)))
            grads = [mm(value_all[lo:hi], g_head, (1, 1)) for lo, hi, _ in probs]
            delta = sum(
                jnp.sum(prob * grad, axis=0, keepdims=True)
                for (_, _, prob), grad in zip(probs, grads)
            )
            part = None
            for (lo, hi, prob), grad in zip(probs, grads):
                d_score = (prob * (grad - delta)).astype(bf16)
                dv_sum[lo:hi, :] += mm(prob.astype(bf16), g_head, (1, 0))
                dk_sum[lo:hi, :] += mm(d_score, q_head, (1, 0))
                added = mm(d_score, key_all[lo:hi], (0, 0))
                part = added if part is None else part + added
            d_query = part if head == 0 else jnp.where(mine, part, d_query)
        dq_sum[start:stop, :] = d_query * scale
    cos_t, lead, trail = cos_ref[...].T, lead_ref[...].T, trail_ref[...].T
    width = d_out.shape[1] // 3

    def put(which, vals):
        first = pl.multiple_of(which * width + pl.program_id(1) * LANES, LANES)
        d_out[:, pl.ds(first, LANES)] = vals.astype(bf16)

    put(0, unrotated(dq_sum[...], cos_t, lead, trail))
    put(1, unrotated(dk_sum[...], cos_t, lead, trail))
    put(2, dv_sum[...])


def attend(mixed_qkv, bias, tables, seqs):
    rows, width = mixed_qkv.shape[0] // seqs, mixed_qkv.shape[1] // 3
    pairs = width // LANES

    def part(which):
        return pl.BlockSpec((rows, LANES), lambda s, p: (s, which * pairs + p))

    block = pl.BlockSpec((rows, LANES), lambda s, p: (s, p))
    table = pl.BlockSpec((LANES, rows), lambda s, p: (0, s))
    low = jax.ShapeDtypeStruct((seqs * rows, width), bf16)
    return pl.pallas_call(
        attend_kernel,
        grid=(seqs, pairs),
        in_specs=[part(0), part(1), part(2), pl.BlockSpec((3, LANES), lambda s, p: (0, p))]
        + [table] * 3,
        out_specs=[block] * 4 + [pl.BlockSpec((1, 2, rows), lambda s, p: (s * pairs + p, 0, 0))],
        out_shape=[low] * 4 + [jax.ShapeDtypeStruct((seqs * pairs, 2, rows), f32)],
        compiler_params=pltpu.CompilerParams(vmem_limit_bytes=GRANT),
        name="attend",
    )(mixed_qkv, mixed_qkv, mixed_qkv, bias, *tables)


def attend_back(query, key, value, back, log_total, tables, seqs):
    rows, width = query.shape[0] // seqs, query.shape[1]
    pairs = width // LANES
    block = pl.BlockSpec((rows, LANES), lambda s, p: (s, p))
    table = pl.BlockSpec((LANES, rows), lambda s, p: (0, s))
    return pl.pallas_call(
        attend_back_kernel,
        grid=(seqs, pairs),
        in_specs=[block] * 4
        + [pl.BlockSpec((1, 2, rows), lambda s, p: (s * pairs + p, 0, 0))]
        + [table] * 3,
        out_specs=pl.BlockSpec((rows, 3 * width), lambda s, p: (s, 0)),
        out_shape=jax.ShapeDtypeStruct((seqs * rows, 3 * width), bf16),
        scratch_shapes=[pltpu.VMEM((rows, LANES), f32)] * 3,
        compiler_params=pltpu.CompilerParams(vmem_limit_bytes=GRANT),
        name="attend_back",
    )(query, key, value, back, log_total, *tables)


def bits_of(count):
    bits = []
    bit = 1
    while bit < count:
        bits.append(bit)
        bit *= 2
    return bits


def flipped(index, bit):
    return index + bit * (1 - 2 * ((index // bit) % 2))


def run_chains(chains):
    chains = [chain for chain in chains]
    for chain in chains:
        next(chain)
    while chains:
        left = []
        for chain in chains:
            try:
                next(chain)
                left.append(chain)
            except StopIteration:
                pass
        chains = left


class Sems:
    def __init__(self, send, recv):
        self.send, self.recv, self.used = send, recv, 0

    def take(self):
        self.used += 1
        return self.send.at[self.used - 1], self.recv.at[self.used - 1]


def remote(src, dst, sems, target):
    return pltpu.make_async_remote_copy(
        src_ref=src,
        dst_ref=dst,
        send_sem=sems[0],
        recv_sem=sems[1],
        device_id=target,
        device_id_type=pl.DeviceIdType.MESH,
    )


def greet(ctx, dp):
    here, mine = lax.axis_index("ctx"), lax.axis_index("dp")
    barrier = pltpu.get_barrier_semaphore()
    targets = [{"ctx": lax.rem(here + by, ctx)} for by in range(1, ctx)]
    targets += [{"dp": flipped(mine, bit)} for bit in bits_of(dp)]
    for target in targets:
        pl.semaphore_signal(barrier, inc=1, device_id=target, device_id_type=pl.DeviceIdType.MESH)
    pl.semaphore_wait(barrier, len(targets))


def line_chain(src, out, sems, ctx):
    here = lax.axis_index("ctx")
    ups = [sems.take() for _ in range(1, ctx)]
    downs = [sems.take() for _ in range(1, ctx)]

    def hop(block, slot, step, going):
        by = 1 if going is ups else -1
        return remote(block, out.at[slot], going[step], {"ctx": here + by})

    @pl.when(here < ctx - 1)
    def _():
        hop(src, here, 0, ups).start()

    @pl.when(here > 0)
    def _():
        hop(src, here, 0, downs).start()

    yield
    for step in range(1, ctx):
        for going, sign in ((ups, -1), (downs, 1)):
            slot = here + sign * step
            inside = (slot >= 0) if sign < 0 else (slot < ctx)
            more = (here < ctx - 1) if sign < 0 else (here > 0)
            if step < ctx - 1:

                @pl.when(jnp.logical_and(inside, more))
                def _():
                    hop(out.at[slot], slot, step - 1, going).wait_recv()
                    hop(out.at[slot], slot, step, going).start()

                @pl.when(jnp.logical_and(inside, jnp.logical_not(more)))
                def _():
                    hop(out.at[slot], slot, step - 1, going).wait_recv()

            else:

                @pl.when(inside)
                def _():
                    hop(out.at[slot], slot, step - 1, going).wait_recv()

        yield

    for step in range(ctx - 1):
        for going, sign in ((ups, -1), (downs, 1)):
            slot = here + sign * step
            inside = (slot >= 0) if sign < 0 else (slot < ctx)
            more = (here < ctx - 1) if sign < 0 else (here > 0)

            @pl.when(jnp.logical_and(inside, more))
            def _():
                hop(out.at[slot], slot, step, going).wait_send()


def weight_chain(cuts, out, sems, own_sem, ctx, dp):
    here, mine = lax.axis_index("ctx"), lax.axis_index("dp")
    rows = cuts[0][0].shape[0]
    slab = rows * ctx
    half = slab // 2

    def piece(owner, cut):
        at = pl.ds(pl.multiple_of((mine * ctx + owner) * rows, rows), rows)
        return out.at[at, pl.ds(cut[3], cut[1])]

    def taken(peer, cut):
        block, width, first, _ = cut
        if first is None:
            return block
        return block.at[:, pl.ds(pl.multiple_of(first + peer * width, LANES), width)]

    def part(owner, which):
        return out.at[pl.ds(pl.multiple_of(owner * slab + which * half, half), half)]

    trades, own = [], []
    for by in range(1, ctx):
        peer = lax.rem(here + by, ctx)
        source = lax.rem(here + ctx - by, ctx)
        for cut in cuts:
            sem = sems.take()
            copy = remote(taken(peer, cut), piece(here, cut), sem, {"ctx": peer})
            copy.start()
            trades.append((copy, remote(taken(peer, cut), piece(source, cut), sem, {"ctx": peer})))
    for index, cut in enumerate(cuts):
        copy = pltpu.make_async_copy(taken(here, cut), piece(here, cut), own_sem.at[index])
        copy.start()
        own.append(copy)
    yield
    for _, arrival in trades:
        arrival.wait_recv()
    for copy in own:
        copy.wait()
    far = bits_of(dp)[1:]
    orders = [far + [1], far[::-1] + [1]]
    held = [[mine], [mine]]
    sent = []
    for stage in range(len(far) + 1):
        arrivals = []
        for which in range(2):
            bit = orders[which][stage]
            for owner in list(held[which]):
                sem = sems.take()
                copy = remote(part(owner, which), part(owner, which), sem, {"dp": flipped(mine, bit)})
                copy.start()
                sent.append(copy)
                coming = flipped(owner, bit)
                arrivals.append(remote(part(coming, which), part(coming, which), sem, {"dp": flipped(mine, bit)}))
                held[which].append(coming)
        yield
        for arrival in arrivals:
            arrival.wait_recv()
    for copy, _ in trades:
        copy.wait_send()
    for copy in sent:
        copy.wait_send()


def cuts_of(blocks, ctx):
    qkv, fc1, out, fc2, small = blocks
    head_cols, ff_cols = D // ctx, FF // ctx
    first = [(qkv, head_cols, part * D, part * head_cols) for part in range(3)]
    first.append((fc1, ff_cols, 0, 3 * head_cols))
    return [first, [(out, head_cols, 0, 0), (fc2, ff_cols, 0, head_cols)], [(small, LANES, None, 0)]]


def gather_kernel(ctx, dp, seqs, *refs):
    tokens, places, blocks = refs[0], refs[1], refs[2:7]
    tok_out, place_out, outs = refs[7], refs[8], refs[9:12]
    send, recv, own_sems, tok_sems = refs[12:]
    here = lax.axis_index("ctx")
    sems = Sems(send, recv)
    greet(ctx, dp)
    chains = [line_chain(places, place_out, sems, ctx)]
    for group, cuts in enumerate(cuts_of(blocks, ctx)):
        chains.append(weight_chain(cuts, outs[group], sems, own_sems.at[group], ctx, dp))
        if group < seqs:
            chains.append(line_chain(tokens.at[group], tok_out.at[group], sems, ctx))
    local = [
        pltpu.make_async_copy(tokens.at[seq], tok_out.at[seq, here], tok_sems.at[seq])
        for seq in range(seqs)
    ]
    local.append(pltpu.make_async_copy(places, place_out.at[here], tok_sems.at[seqs]))
    for copy in local:
        copy.start()
    run_chains(chains)
    for copy in local:
        copy.wait()


def gather_all(tokens, places, blocks, ctx, dp):
    seqs, span = tokens.shape[0], tokens.shape[1]
    rows = blocks[0].shape[0] * ctx * dp
    head_cols, ff_cols = D // ctx, FF // ctx
    copies = (seqs + 1) * 2 * (ctx - 1) + 7 * (ctx - 1) + 3 * 2 * (dp - 1)
    hbm = pl.BlockSpec(memory_space=pl.ANY)
    outs = pl.pallas_call(
        functools.partial(gather_kernel, ctx, dp, seqs),
        in_specs=[hbm] * 7,
        out_specs=[hbm] * 5,
        out_shape=[
            jax.ShapeDtypeStruct((seqs, ctx, span, D), bf16),
            jax.ShapeDtypeStruct((ctx,) + places.shape, f32),
            jax.ShapeDtypeStruct((rows, 3 * head_cols + ff_cols), bf16),
            jax.ShapeDtypeStruct((rows, head_cols + ff_cols), bf16),
            jax.ShapeDtypeStruct((rows, LANES), bf16),
        ],
        scratch_shapes=[
            pltpu.SemaphoreType.DMA((copies,)),
            pltpu.SemaphoreType.DMA((copies,)),
            pltpu.SemaphoreType.DMA((3, 4)),
            pltpu.SemaphoreType.DMA((seqs + 1,)),
        ],
        compiler_params=pltpu.CompilerParams(collective_id=1, has_side_effects=True),
        name="gather_all",
    )(tokens, places, *blocks)
    return outs[0], outs[1], outs[2:]


def add_into(target, other, rows):
    step = 32

    @pl.loop(0, rows // step)
    def _(index):
        here = pl.ds(pl.multiple_of(index * step, step), step)
        target[here, :] = target[here, :] + other[here, :]


def without(pattern, bit):
    return tuple(item for item in pattern if item != bit)


def patterns_of(bits):
    found = [()]
    for bit in bits:
        found += [pattern + (bit,) for pattern in found]
    return found


def owner_of(mine, pattern):
    for bit in pattern:
        mine = flipped(mine, bit)
    return mine


def patterns_for(dp):
    return sorted(patterns_of(bits_of(dp)[1:]), key=len, reverse=True)


class Slabs:
    def __init__(self, plan, x_v, turned, x_sems):
        self.plan, self.x_v, self.turned, self.x_sems = plan, x_v, turned, x_sems
        self.next = 0
        self.start(0)

    def copies(self, index):
        arrays, owner = self.plan[index]
        slab = self.turned.shape[0]
        at = pl.ds(pl.multiple_of(owner * slab, LANES), slab)
        found = []
        for seq, array in enumerate(arrays):
            length = array.shape[0]
            found.append(
                pltpu.make_async_copy(
                    array.at[:, at],
                    self.x_v.at[index % 2, pl.ds(seq * length, length)],
                    self.x_sems.at[index % 2, seq],
                )
            )
        return found

    def start(self, index):
        for copy in self.copies(index):
            copy.start()

    def take(self):
        for copy in self.copies(self.next):
            copy.wait()
        if self.next + 1 < len(self.plan):
            self.start(self.next + 1)
        self.turned[...] = self.x_v[self.next % 2].T
        self.next += 1


def product_into(turned, y_v, cols, store):
    tile = 512 if cols % 512 == 0 else 256

    @pl.loop(0, cols // tile)
    def _(index):
        at = pl.ds(pl.multiple_of(index * tile, tile), tile)
        store(at, mm(turned[...], y_v[:, at], (1, 0)))


def pooled_chain(ys, parts, slabs, boxes, land_core, lands, sems, y_v, y_sems, own_sem, ctx, dp):
    here, mine = lax.axis_index("ctx"), lax.axis_index("dp")
    slab, cols = land_core.shape[1:]
    rows, half = slab // ctx, slab // 2
    far = bits_of(dp)[1:]
    patterns = patterns_for(dp)
    partner = flipped(mine, 1)
    loads = []
    for arrays, first in ys:
        for seq, array in enumerate(arrays):
            length, width = array.shape
            loads.append(
                pltpu.make_async_copy(
                    array,
                    y_v.at[pl.ds(seq * length, length), pl.ds(first, width)],
                    y_sems.at[len(loads)],
                )
            )
    for load in loads:
        load.start()
    for load in loads:
        load.wait()
    sent = []
    for index in range(len(patterns)):
        slabs.take()
        if boxes["sent"][index] is not None:
            boxes["sent"][index].wait_send()
        box = boxes["box"].at[index, :, pl.ds(0, cols)]

        def store(at, vals, index=index):
            boxes["box"][index, :, at] = vals.astype(bf16)

        product_into(slabs.turned, y_v, cols, store)
        copy = remote(box, land_core.at[index], sems.take(), {"dp": partner})
        copy.start()
        boxes["sent"][index] = copy
        sent.append(copy)
    yield
    held = [{}, {}]
    for index, pattern in enumerate(patterns):
        slabs.take()
        sent[index].wait_recv()

        def store(at, vals, index=index):
            land_core[index, :, at] = (vals + land_core[index, :, at].astype(f32)).astype(bf16)

        product_into(slabs.turned, y_v, cols, store)
        for which in range(2):
            held[which][pattern] = land_core.at[index, pl.ds(which * half, half)]
    sent = []
    orders = [far, far[::-1]]
    used = 0
    for stage in range(len(far)):
        arrivals = []
        for which in range(2):
            bit = orders[which][stage]
            kept = {}
            for pattern, block in held[which].items():
                if bit in pattern:
                    landing = lands.at[used]
                    used += 1
                    copy = remote(block, landing, sems.take(), {"dp": flipped(mine, bit)})
                    copy.start()
                    sent.append(copy)
                    rest = without(pattern, bit)
                    arrivals.append((copy, landing, held[which][rest]))
                    kept[rest] = landing
            held[which] = kept
        yield
        for copy, landing, block in arrivals:
            copy.wait_recv()
            add_into(landing, block, half)
    final = [held[0][()], held[1][()]]
    trades = []

    def piece(which, peer, part):
        first = pl.multiple_of(peer * rows - which * half, rows)
        return final[which].at[pl.ds(first, rows), pl.ds(part[1], part[2])]

    def target(source, part):
        first = pl.multiple_of(part[3] + source * part[2], LANES)
        return part[0].at[:, pl.ds(first, part[2])]

    for by in range(1, ctx):
        peer = lax.rem(here + by, ctx)
        source = lax.rem(here + ctx - by, ctx)
        for part in parts:
            sem = sems.take()
            for which in range(2):

                @pl.when(peer // (ctx // 2) == which)
                def _():
                    remote(piece(which, peer, part), target(here, part), sem, {"ctx": peer}).start()

            trades.append((sem, peer, source, part))
    for which in range(2):

        @pl.when(here // (ctx // 2) == which)
        def _():
            for part in parts:
                copy = pltpu.make_async_copy(piece(which, here, part), target(here, part), own_sem)
                copy.start()
                copy.wait()

    yield
    for sem, peer, source, part in trades:
        some = final[0].at[pl.ds(0, rows), pl.ds(part[1], part[2])]
        remote(some, target(source, part), sem, {"ctx": peer}).wait_recv()
    for sem, peer, source, part in trades:
        some = final[0].at[pl.ds(0, rows), pl.ds(part[1], part[2])]
        remote(some, target(source, part), sem, {"ctx": peer}).wait_send()
    for copy in sent:
        copy.wait_send()


def sum_chain(partial, out, held, downs_land, ups_land, sems, load_sem, ctx):
    here = lax.axis_index("ctx")
    rows = held.shape[0] // ctx
    load = pltpu.make_async_copy(partial, held, load_sem)
    load.start()
    down_sems = [sems.take() for _ in range(1, ctx)]
    up_sems = [sems.take() for _ in range(1, ctx)]

    def chunk(index):
        return held.at[pl.ds(pl.multiple_of(index * rows, rows), rows)]

    def hop(block, step, down):
        lands, going = (downs_land, down_sems) if down else (ups_land, up_sems)
        by = -1 if down else 1
        return remote(block, lands.at[step - 1], going[step - 1], {"ctx": here + by})

    load.wait()

    @pl.when(here == ctx - 1)
    def _():
        for step in range(1, ctx):
            hop(chunk(step - 1), step, True).start()

    @pl.when(here == 0)
    def _():
        for step in range(1, ctx):
            hop(chunk(ctx - step), step, False).start()

    yield
    for step in range(2, ctx):

        @pl.when(jnp.logical_and(here < ctx - 1, here + step - ctx >= 0))
        def _():
            block = downs_land.at[step - 2]
            hop(block, step - 1, True).wait_recv()
            add_into(block, chunk(here + step - ctx), rows)
            hop(block, step, True).start()

        @pl.when(jnp.logical_and(here > 0, here + ctx - step <= ctx - 1))
        def _():
            block = ups_land.at[step - 2]
            hop(block, step - 1, False).wait_recv()
            add_into(block, chunk(here + ctx - step), rows)
            hop(block, step, False).start()

        yield

    @pl.when(here < ctx - 1)
    def _():
        hop(downs_land.at[ctx - 2], ctx - 1, True).wait_recv()

    @pl.when(here > 0)
    def _():
        hop(ups_land.at[ctx - 2], ctx - 1, False).wait_recv()

    step = 32

    @pl.loop(0, rows // step)
    def _(index):
        at = pl.ds(pl.multiple_of(index * step, step), step)
        mine = held[pl.ds(pl.multiple_of(here * rows + index * step, step), step), :].astype(f32)
        down = downs_land[ctx - 2, at, :].astype(f32)
        up = ups_land[ctx - 2, at, :].astype(f32)
        out[at, :] = (
            mine + jnp.where(here < ctx - 1, down, 0.0) + jnp.where(here > 0, up, 0.0)
        )

    for step in range(1, ctx):

        @pl.when(here + step - ctx >= 0)
        def _():
            hop(chunk(0), step, True).wait_send()

        @pl.when(here + ctx - step <= ctx - 1)
        def _():
            hop(chunk(0), step, False).wait_send()


def reduce_kernel(ctx, dp, seqs, *refs):
    partial, refs = refs[0], refs[1:]
    normal, cot, d_qkv, d_pre, attended, hidden = (
        refs[part * seqs : (part + 1) * seqs] for part in range(6)
    )
    sum_out, qkv_out, fc1_out, out_out, fc2_out = refs[6 * seqs : 6 * seqs + 5]
    held, downs_land, ups_land, box, x_v, turned, y_v = refs[6 * seqs + 5 : 6 * seqs + 12]
    land_core, lands = refs[6 * seqs + 12 : 6 * seqs + 15], refs[6 * seqs + 15 : 6 * seqs + 18]
    send, recv, load_sem, x_sems, y_sems, own_sems = refs[6 * seqs + 18 :]
    head_cols, ff_cols = D // ctx, FF // ctx
    parts = [
        [(out_out, 0, head_cols, 0), (fc2_out, head_cols, ff_cols, 0)],
        [(fc1_out, 0, ff_cols, 0)],
        [(qkv_out, part * head_cols, head_cols, part * D) for part in range(3)],
    ]
    ys = [[(attended, 0), (hidden, head_cols)], [(d_pre, 0)], [(d_qkv, 0)]]
    mine = lax.axis_index("dp")
    plan = []
    for arrays in (cot, normal, normal):
        for first in (flipped(mine, 1), mine):
            plan += [(arrays, owner_of(first, pattern)) for pattern in patterns_for(dp)]
    sems = Sems(send, recv)
    greet(ctx, dp)
    slabs = Slabs(plan, x_v, turned, x_sems)
    boxes = {"box": box, "sent": [None] * (dp // 2)}
    line = sum_chain(partial, sum_out, held, downs_land, ups_land, sems, load_sem, ctx)
    groups = [
        pooled_chain(
            ys[group], parts[group], slabs, boxes, land_core[group], lands[group],
            sems, y_v, y_sems, own_sems.at[group], ctx, dp,
        )
        for group in range(3)
    ]
    order = [line, groups[0], groups[0], groups[1], groups[0], line, groups[1], groups[2]]
    order += [groups[1], groups[2], line, groups[2], line]
    run_in(order, [line] + groups)
    for copy in boxes["sent"]:
        copy.wait_send()


def run_in(order, chains):
    ended = set()
    turn = 0
    while len(ended) < len(chains):
        chain = order[turn] if turn < len(order) else chains[(turn - len(order)) % len(chains)]
        turn += 1
        if id(chain) in ended:
            continue
        try:
            next(chain)
        except StopIteration:
            ended.add(id(chain))


def reduce_all(partial, normal, cot, d_qkv, d_pre, attended, hidden, ctx, dp):
    seqs, length = len(normal), normal[0].shape[0]
    rows = partial.shape[0] // ctx
    slab = D // dp
    copies = 2 * (ctx - 1) + 3 * (dp // 2 + dp - 2) + 6 * (ctx - 1)
    hbm = pl.BlockSpec(memory_space=pl.ANY)
    vmem = pl.BlockSpec(memory_space=pltpu.VMEM)
    head_cols, ff_cols = D // ctx, FF // ctx
    cols = [head_cols + ff_cols, ff_cols, 3 * head_cols]
    outs = pl.pallas_call(
        functools.partial(reduce_kernel, ctx, dp, seqs),
        in_specs=[hbm] * (1 + 6 * seqs),
        out_specs=[vmem] + [hbm] * 4,
        out_shape=[jax.ShapeDtypeStruct((rows, partial.shape[1]), f32)]
        + [jax.ShapeDtypeStruct((slab // ctx, width), bf16) for width in (3 * D, FF, D, FF)],
        scratch_shapes=[pltpu.VMEM(partial.shape, bf16)]
        + [pltpu.VMEM((ctx - 1, rows, partial.shape[1]), bf16)] * 2
        + [
            pltpu.VMEM((dp // 2, slab, cols[0]), bf16),
            pltpu.VMEM((2, seqs * length, slab), bf16),
            pltpu.VMEM((slab, seqs * length), bf16),
            pltpu.VMEM((seqs * length, cols[0]), bf16),
        ]
        + [pltpu.VMEM((dp // 2, slab, width), bf16) for width in cols]
        + [pltpu.VMEM((dp - 2, slab // 2, width), bf16) for width in cols]
        + [
            pltpu.SemaphoreType.DMA((copies,)),
            pltpu.SemaphoreType.DMA((copies,)),
            pltpu.SemaphoreType.DMA,
            pltpu.SemaphoreType.DMA((2, seqs)),
            pltpu.SemaphoreType.DMA((2 * seqs,)),
            pltpu.SemaphoreType.DMA((3,)),
        ],
        compiler_params=pltpu.CompilerParams(
            collective_id=2, has_side_effects=True, vmem_limit_bytes=GRANT
        ),
        name="reduce_all",
    )(partial, *normal, *cot, *d_qkv, *d_pre, *attended, *hidden)
    return outs[0], outs[1:]


def normalised(rows_in):
    row_mean = jnp.mean(rows_in, axis=-1, keepdims=True)
    centred = rows_in - row_mean
    variance = jnp.mean(centred * centred, axis=-1, keepdims=True)
    inv_std = lax.rsqrt(variance + 1e-05)
    return centred * inv_std, inv_std


def gelu_both(pre):
    return jax.vjp(lambda vals: jax.nn.gelu(vals, approximate=True), pre)


def per_device(
    tokens,
    cotangent,
    positions,
    wqkv_master,
    fc1_master,
    out_master,
    fc2_master,
    small_master,
    wqkv_first,
    wqkv_second,
    fc1_first,
    fc1_second,
    out_first,
    out_second,
    fc2_first,
    fc2_second,
    small_first,
    small_second,
):
    seqs, span = tokens.shape[0], tokens.shape[1]
    ctx, dp = lax.axis_size("ctx"), lax.axis_size("dp")
    ctx_index = lax.axis_index("ctx")
    length = span * ctx
    total_rows = seqs * length
    own_rows = wqkv_master.shape[0]
    head_cols, ff_cols = D // ctx, FF // ctx

    gate = lax.optimization_barrier
    small_low = jnp.pad(small_master.astype(bf16), ((0, 0), (0, LANES - small_master.shape[1])))
    blocks = [wqkv_master, fc1_master, out_master, fc2_master]
    blocks = [block.astype(bf16) for block in blocks] + [small_low]
    places = jnp.pad(positions.astype(f32).reshape(-1, LANES), ((0, 8 - seqs * span // LANES), (0, 0)))
    tok_all, place, (in_w, of_w, small_all) = gather_all(tokens, places, blocks, ctx, dp)
    qkv_w, fc1_w = in_w[:, : 3 * head_cols], in_w[:, 3 * head_cols :]
    params = small_all[:, :16].astype(f32)
    place = place[:, : seqs * span // LANES].reshape(ctx, seqs, span)
    place = jnp.transpose(place, (1, 0, 2)).reshape(total_rows)
    half_rot = ROT // 2
    exponent = jnp.arange(half_rot, dtype=f32) * (-2.0 / ROT)
    frequency = jnp.power(f32(10000.0), exponent)
    angles = frequency[:, None] * place[None, :]
    cos_s, sin_s = jnp.cos(angles), jnp.sin(angles)
    none = jnp.zeros_like(cos_s)
    rest = jnp.zeros((HD - ROT, total_rows), f32)
    tables = [
        jnp.concatenate([cos_s, cos_s, rest + 1.0] * 2, axis=0),
        jnp.concatenate([-sin_s, none, rest] * 2, axis=0),
        jnp.concatenate([none, sin_s, rest] * 2, axis=0),
    ]

    def my_part(values, cols):
        return lax.dynamic_slice_in_dim(values, ctx_index * cols, cols, values.ndim - 1)

    qkv_bias = my_part(params[:, 2:5].T, head_cols)
    fc1_bias = my_part(params[:, 6:10].T.reshape(FF), ff_cols)
    gain, shift = params[:, 0], params[:, 1]
    seq_tables = [
        [table[:, seq * length : (seq + 1) * length] for table in tables] for seq in range(seqs)
    ]

    def norm_of(seq):
        return (normalised(tok_all[seq].reshape(length, D).astype(f32))[0] * gain + shift).astype(bf16)

    def attend_of(seq):
        projected = mm(normal_low[seq], qkv_w, (1, 0))
        return attend(projected, qkv_bias, seq_tables[seq], 1)

    def hidden_of(seq):
        return mm(normal_low[seq], fc1_w, (1, 0)) + fc1_bias

    def branch_of(seq):
        low = gelu_both(pre[seq])[0].astype(bf16)
        return low, mm(jnp.concatenate([attn[seq][3], low], axis=1), of_w, (1, 1)).astype(bf16)

    def back_of(seq):
        grad_hidden = mm(cot_all[seq], of_w[:, head_cols:], (1, 0))
        return (
            mm(cot_all[seq], of_w[:, :head_cols], (1, 0)).astype(bf16),
            gelu_both(pre[seq])[1](grad_hidden)[0].astype(bf16),
        )

    def attend_back_of(seq):
        query, key, value, _, log_total = attn[seq]
        return attend_back(query, key, value, back[seq], log_total, seq_tables[seq], 1)

    def normal_back_of(seq):
        return mm(jnp.concatenate([d_qkv[seq], d_pre[seq]], axis=1), in_w, (1, 1)).astype(bf16)

    def gathered(block):
        return lax.all_gather(block, "ctx", axis=0, tiled=True)

    def scattered(partial):
        return lax.psum_scatter(partial, "ctx", scatter_dimension=0, tiled=True).astype(f32)

    two = [None] * seqs
    normal_low, attn, pre, hidden, mix, back, d_pre, d_qkv, d_sum, cot_all = (
        list(two) for _ in range(10)
    )
    d_sum = list(two)
    cot, tok_all = gate(([cotangent[seq] for seq in range(seqs)], tok_all))
    cot_all[0] = gathered(cot[0])
    normal_low[0] = norm_of(0)
    attn[0] = attend_of(0)
    cot[1], normal_low[0], attn[0], tok_all = gate((cot[1], normal_low[0], attn[0], tok_all))
    cot_all[1] = gathered(cot[1])
    normal_low[1] = norm_of(1)
    attn[1] = attend_of(1)
    normal_low, attn = gate((normal_low, attn))
    pre = [hidden_of(0), hidden_of(1)]
    normal_low, pre, attn = gate((normal_low, pre, attn))
    for seq in range(seqs):
        hidden[seq], mix[seq] = branch_of(seq)
    pre, attn, hidden, mix = gate((pre, attn, hidden, mix))
    mix = [scattered(part) for part in mix]
    for seq in range(seqs):
        back[seq], d_pre[seq] = back_of(seq)
        d_qkv[seq] = attend_back_of(seq)
        d_sum[seq] = normal_back_of(seq)
        if seq == 0:
            pre, attn, d_qkv[0], d_pre[0], part = gate((pre, attn, d_qkv[0], d_pre[0], d_sum[0]))
            d_sum[0] = scattered(part)
    d_qkv, d_pre, d_sum = gate((d_qkv, d_pre, d_sum))
    sum_qkv = sum(jnp.sum(part, axis=0, dtype=f32) for part in d_qkv)
    sum_pre = sum(jnp.sum(part, axis=0, dtype=f32) for part in d_pre)
    sum_out = jnp.sum(cotangent.astype(f32), axis=(0, 1))[None]
    normed, inv_std = normalised(tokens.astype(f32))
    attended = [item[3] for item in attn]
    last, grads = reduce_all(
        d_sum[1], normal_low, cot_all, d_qkv, d_pre, attended, hidden, ctx, dp
    )
    qkv_grad, fc1_grad, out_grad, fc2_grad = (grad.astype(f32) for grad in grads)
    mixed = (tokens.astype(f32) + jnp.stack(mix) + params[:, 5] + params[:, 10]).astype(bf16)
    d_normal = jnp.stack([d_sum[0], last])
    d_scaled = d_normal * gain
    input_grad = cotangent.astype(f32) + inv_std * (
        d_scaled
        - jnp.mean(d_scaled, axis=-1, keepdims=True)
        - normed * jnp.mean(d_scaled * normed, axis=-1, keepdims=True)
    )

    def spread(sums, count, cols):
        whole = jnp.zeros((count, ctx * cols), f32)
        return lax.dynamic_update_slice_in_dim(whole, sums.reshape(count, cols), ctx_index * cols, 1)

    sum_qkv = spread(sum_qkv, 3, head_cols)
    sum_pre = spread(sum_pre, 1, ff_cols).reshape(4, D)
    gain_terms = jnp.sum(d_normal * normed, axis=(0, 1))[None]
    shift_terms = jnp.sum(d_normal, axis=(0, 1))[None]
    small_terms = jnp.concatenate(
        [gain_terms, shift_terms, sum_qkv, sum_out, sum_pre, sum_out], axis=0
    )
    small_sent = jnp.transpose(small_terms.reshape(11, ctx * dp, own_rows), (1, 0, 2))
    small_got = lax.all_to_all(small_sent.reshape(ctx * dp, 1, 11 * own_rows), EVERY, 0, 0, tiled=True)
    small_grad = jnp.sum(small_got, axis=(0, 1)).reshape(11, own_rows).T

    qkv_new = adamw(wqkv_master, wqkv_first, wqkv_second, qkv_grad, 0.04, 0.1)
    fc1_new = adamw(fc1_master, fc1_first, fc1_second, fc1_grad, 0.04, 0.1)
    out_new = adamw(out_master, out_first, out_second, out_grad, 0.4, 0.1)
    fc2_new = adamw(fc2_master, fc2_first, fc2_second, fc2_grad, 0.02, 0.1)
    small_new = adamw(small_master, small_first, small_second, small_grad, 0.3, 0.0)
    return (mixed, input_grad, *qkv_new, *fc1_new, *out_new, *fc2_new, *small_new)


def solution(mesh):
    split = P("dp", "ctx", None)
    rows = P(("dp", "ctx"), None)
    return jax.shard_map(
        per_device,
        mesh=mesh,
        in_specs=(split, split, P("dp", "ctx")) + (rows,) * 15,
        out_specs=(split, split) + (rows,) * 15,
        check_vma=False,
    )
```

```python
import functools

import jax
import jax.numpy as jnp
from jax import lax
from jax.experimental import pallas as pl
from jax.experimental.pallas import tpu as pltpu
from jax.sharding import PartitionSpec as P

D = 2048
H = 32
HD = 64
ROT = 32
FF = 8192
STEP = 10
LANES = 128
BLOCK = 256

beta_one = 0.9
beta_two = 0.95
epsilon = 1e-08

f32 = jnp.float32
bf16 = jnp.bfloat16
EVERY = ("dp", "ctx")
GRANT = 58 * 1024 * 1024


def adamw(weight, first_old, second_old, gradient, step_rate, decay):
    first_new = beta_one * first_old + (1.0 - beta_one) * gradient
    second_new = beta_two * second_old + (1.0 - beta_two) * gradient * gradient
    first_hat = first_new / (1.0 - beta_one**STEP)
    second_hat = second_new / (1.0 - beta_two**STEP)
    weight_new = weight - step_rate * (
        first_hat / (jnp.sqrt(second_hat) + epsilon) + decay * weight
    )
    return (first_new, second_new, weight_new)


def mm(left, right, dims):
    return lax.dot_general(left, right, ((dims[:1], dims[1:]), ((), ())), preferred_element_type=f32)


def rotated(vals, cos_t, lead, trail):
    return (
        vals * cos_t + pltpu.roll(vals, LANES - 16, 1) * lead + pltpu.roll(vals, 16, 1) * trail
    )


def unrotated(vals, cos_t, lead, trail):
    return (
        vals * cos_t - pltpu.roll(vals, LANES - 16, 1) * lead - pltpu.roll(vals, 16, 1) * trail
    )


def attend_kernel(
    q_in, k_in, v_in, bias, cos_ref, lead_ref, trail_ref, q_out, k_out, v_out, o_out, log_out
):
    rows = q_in.shape[0]
    cos_t, lead, trail = cos_ref[...].T, lead_ref[...].T, trail_ref[...].T
    scale = HD ** (-0.5)
    query = rotated(q_in[...] + bias[0:1, :], cos_t, lead, trail).astype(bf16)
    key = rotated(k_in[...] + bias[1:2, :], cos_t, lead, trail).astype(bf16)
    value = (v_in[...] + bias[2:3, :]).astype(bf16)
    query = query * jnp.asarray(scale, bf16)
    q_out[...] = query
    k_out[...] = key
    v_out[...] = value
    lane = lax.broadcasted_iota(jnp.int32, (BLOCK, LANES), 1)
    on_diagonal = lax.broadcasted_iota(jnp.int32, (BLOCK, BLOCK), 1) <= lax.broadcasted_iota(
        jnp.int32, (BLOCK, BLOCK), 0
    )
    for step in range(rows // BLOCK):
        start = step * BLOCK
        stop = start + BLOCK
        out = None
        for head in range(2):
            mine = (lane < HD) if head == 0 else (lane >= HD)
            q_head = jnp.where(mine, query[start:stop], jnp.zeros((), bf16))
            last = jnp.where(on_diagonal, mm(q_head, key[start:stop], (1, 1)), -1e30)
            parts = [last]
            if start:
                parts = [mm(q_head, key[:start], (1, 1)), last]
            best = functools.reduce(
                jnp.maximum, [jnp.max(part, axis=1, keepdims=True) for part in parts]
            )
            parts = [jnp.exp(part - best) for part in parts]
            total = sum(jnp.sum(part, axis=1, keepdims=True) for part in parts)
            log_out[0, head, start:stop] = (best + jnp.log(total))[:, 0]
            mixed = mm(parts[-1].astype(bf16), value[start:stop], (1, 0))
            if start:
                mixed = mixed + mm(parts[0].astype(bf16), value[:start], (1, 0))
            mixed = mixed / total
            out = mixed if head == 0 else jnp.where(mine, mixed, out)
        o_out[start:stop, :] = out.astype(bf16)


def attend_back_kernel(
    q_in, k_in, v_in, g_in, log_in, cos_ref, lead_ref, trail_ref, d_out, dq_sum, dk_sum, dv_sum
):
    rows = q_in.shape[0]
    scale = HD ** (-0.5)
    lane = lax.broadcasted_iota(jnp.int32, (BLOCK, LANES), 1)
    on_diagonal = lax.broadcasted_iota(jnp.int32, (BLOCK, BLOCK), 0) <= lax.broadcasted_iota(
        jnp.int32, (BLOCK, BLOCK), 1
    )
    dk_sum[...] = jnp.zeros_like(dk_sum)
    dv_sum[...] = jnp.zeros_like(dv_sum)
    key_all = k_in[...]
    value_all = v_in[...]
    zero = jnp.zeros((), bf16)
    for step in range(rows // BLOCK):
        start = step * BLOCK
        stop = start + BLOCK
        d_query = None
        for head in range(2):
            mine = (lane < HD) if head == 0 else (lane >= HD)
            q_head = jnp.where(mine, q_in[start:stop], zero)
            g_head = jnp.where(mine, g_in[start:stop], zero)
            log_row = log_in[0, head : head + 1, start:stop]
            last = jnp.where(
                on_diagonal, jnp.exp(mm(key_all[start:stop], q_head, (1, 1)) - log_row), 0.0
            )
            probs = [(start, stop, last)]
            if start:
                probs.append((0, start, jnp.exp(mm(key_all[:start], q_head, (1, 1)) - log_row)))
            grads = [mm(value_all[lo:hi], g_head, (1, 1)) for lo, hi, _ in probs]
            delta = sum(
                jnp.sum(prob * grad, axis=0, keepdims=True)
                for (_, _, prob), grad in zip(probs, grads)
            )
            part = None
            for (lo, hi, prob), grad in zip(probs, grads):
                d_score = (prob * (grad - delta)).astype(bf16)
                dv_sum[lo:hi, :] += mm(prob.astype(bf16), g_head, (1, 0))
                dk_sum[lo:hi, :] += mm(d_score, q_head, (1, 0))
                added = mm(d_score, key_all[lo:hi], (0, 0))
                part = added if part is None else part + added
            d_query = part if head == 0 else jnp.where(mine, part, d_query)
        dq_sum[start:stop, :] = d_query * scale
    cos_t, lead, trail = cos_ref[...].T, lead_ref[...].T, trail_ref[...].T
    width = d_out.shape[1] // 3

    def put(which, vals):
        first = pl.multiple_of(which * width + pl.program_id(1) * LANES, LANES)
        d_out[:, pl.ds(first, LANES)] = vals.astype(bf16)

    put(0, unrotated(dq_sum[...], cos_t, lead, trail))
    put(1, unrotated(dk_sum[...], cos_t, lead, trail))
    put(2, dv_sum[...])


def attend(mixed_qkv, bias, tables, seqs):
    rows, width = mixed_qkv.shape[0] // seqs, mixed_qkv.shape[1] // 3
    pairs = width // LANES

    def part(which):
        return pl.BlockSpec((rows, LANES), lambda s, p: (s, which * pairs + p))

    block = pl.BlockSpec((rows, LANES), lambda s, p: (s, p))
    table = pl.BlockSpec((LANES, rows), lambda s, p: (0, s))
    low = jax.ShapeDtypeStruct((seqs * rows, width), bf16)
    return pl.pallas_call(
        attend_kernel,
        grid=(seqs, pairs),
        in_specs=[part(0), part(1), part(2), pl.BlockSpec((3, LANES), lambda s, p: (0, p))]
        + [table] * 3,
        out_specs=[block] * 4 + [pl.BlockSpec((1, 2, rows), lambda s, p: (s * pairs + p, 0, 0))],
        out_shape=[low] * 4 + [jax.ShapeDtypeStruct((seqs * pairs, 2, rows), f32)],
        compiler_params=pltpu.CompilerParams(vmem_limit_bytes=GRANT),
        cost_estimate=pl.CostEstimate(flops=20 * 10**9, bytes_accessed=10**7, transcendentals=0),
        name="attend",
    )(mixed_qkv, mixed_qkv, mixed_qkv, bias, *tables)


def attend_back(query, key, value, back, log_total, tables, seqs):
    rows, width = query.shape[0] // seqs, query.shape[1]
    pairs = width // LANES
    block = pl.BlockSpec((rows, LANES), lambda s, p: (s, p))
    table = pl.BlockSpec((LANES, rows), lambda s, p: (0, s))
    return pl.pallas_call(
        attend_back_kernel,
        grid=(seqs, pairs),
        in_specs=[block] * 4
        + [pl.BlockSpec((1, 2, rows), lambda s, p: (s * pairs + p, 0, 0))]
        + [table] * 3,
        out_specs=pl.BlockSpec((rows, 3 * width), lambda s, p: (s, 0)),
        out_shape=jax.ShapeDtypeStruct((seqs * rows, 3 * width), bf16),
        scratch_shapes=[pltpu.VMEM((rows, LANES), f32)] * 3,
        compiler_params=pltpu.CompilerParams(vmem_limit_bytes=GRANT),
        cost_estimate=pl.CostEstimate(flops=30 * 10**9, bytes_accessed=10**7, transcendentals=0),
        name="attend_back",
    )(query, key, value, back, log_total, *tables)


def bits_of(count):
    bits = []
    bit = 1
    while bit < count:
        bits.append(bit)
        bit *= 2
    return bits


def flipped(index, bit):
    return index + bit * (1 - 2 * ((index // bit) % 2))


def run_chains(chains):
    chains = [chain for chain in chains]
    for chain in chains:
        next(chain)
    while chains:
        left = []
        for chain in chains:
            try:
                next(chain)
                left.append(chain)
            except StopIteration:
                pass
        chains = left


class Sems:
    def __init__(self, send, recv):
        self.send, self.recv, self.used = send, recv, 0

    def take(self):
        self.used += 1
        return self.send.at[self.used - 1], self.recv.at[self.used - 1]


def remote(src, dst, sems, target):
    return pltpu.make_async_remote_copy(
        src_ref=src,
        dst_ref=dst,
        send_sem=sems[0],
        recv_sem=sems[1],
        device_id=target,
        device_id_type=pl.DeviceIdType.MESH,
    )


def greet(ctx, dp):
    here, mine = lax.axis_index("ctx"), lax.axis_index("dp")
    barrier = pltpu.get_barrier_semaphore()
    targets = [{"ctx": lax.rem(here + by, ctx)} for by in range(1, ctx)]
    targets += [{"dp": flipped(mine, bit)} for bit in bits_of(dp)]
    for target in targets:
        pl.semaphore_signal(barrier, inc=1, device_id=target, device_id_type=pl.DeviceIdType.MESH)
    pl.semaphore_wait(barrier, len(targets))


def line_chain(src, out, sems, ctx):
    here = lax.axis_index("ctx")
    ups = [sems.take() for _ in range(1, ctx)]
    downs = [sems.take() for _ in range(1, ctx)]

    def hop(block, slot, step, going):
        by = 1 if going is ups else -1
        return remote(block, out.at[slot], going[step], {"ctx": here + by})

    @pl.when(here < ctx - 1)
    def _():
        hop(src, here, 0, ups).start()

    @pl.when(here > 0)
    def _():
        hop(src, here, 0, downs).start()

    yield
    for step in range(1, ctx):
        for going, sign in ((ups, -1), (downs, 1)):
            slot = here + sign * step
            inside = (slot >= 0) if sign < 0 else (slot < ctx)
            more = (here < ctx - 1) if sign < 0 else (here > 0)
            if step < ctx - 1:

                @pl.when(jnp.logical_and(inside, more))
                def _():
                    hop(out.at[slot], slot, step - 1, going).wait_recv()
                    hop(out.at[slot], slot, step, going).start()

                @pl.when(jnp.logical_and(inside, jnp.logical_not(more)))
                def _():
                    hop(out.at[slot], slot, step - 1, going).wait_recv()

            else:

                @pl.when(inside)
                def _():
                    hop(out.at[slot], slot, step - 1, going).wait_recv()

        yield

    for step in range(ctx - 1):
        for going, sign in ((ups, -1), (downs, 1)):
            slot = here + sign * step
            inside = (slot >= 0) if sign < 0 else (slot < ctx)
            more = (here < ctx - 1) if sign < 0 else (here > 0)

            @pl.when(jnp.logical_and(inside, more))
            def _():
                hop(out.at[slot], slot, step, going).wait_send()


def weight_chain(cuts, out, sems, own_sem, ctx, dp):
    here, mine = lax.axis_index("ctx"), lax.axis_index("dp")
    rows = cuts[0][0].shape[0]
    slab = rows * ctx
    half = slab // 2

    def piece(owner, cut):
        at = pl.ds(pl.multiple_of((mine * ctx + owner) * rows, rows), rows)
        return out.at[at, pl.ds(cut[3], cut[1])]

    def taken(peer, cut):
        block, width, first, _ = cut
        if first is None:
            return block
        return block.at[:, pl.ds(pl.multiple_of(first + peer * width, LANES), width)]

    def part(owner, which):
        return out.at[pl.ds(pl.multiple_of(owner * slab + which * half, half), half)]

    trades, own = [], []
    for by in range(1, ctx):
        peer = lax.rem(here + by, ctx)
        source = lax.rem(here + ctx - by, ctx)
        for cut in cuts:
            sem = sems.take()
            copy = remote(taken(peer, cut), piece(here, cut), sem, {"ctx": peer})
            copy.start()
            trades.append((copy, remote(taken(peer, cut), piece(source, cut), sem, {"ctx": peer})))
    for index, cut in enumerate(cuts):
        copy = pltpu.make_async_copy(taken(here, cut), piece(here, cut), own_sem.at[index])
        copy.start()
        own.append(copy)
    yield
    for _, arrival in trades:
        arrival.wait_recv()
    for copy in own:
        copy.wait()
    far = bits_of(dp)[1:]
    orders = [far + [1], far[::-1] + [1]]
    held = [[mine], [mine]]
    sent = []
    for stage in range(len(far) + 1):
        arrivals = []
        for which in range(2):
            bit = orders[which][stage]
            for owner in list(held[which]):
                sem = sems.take()
                copy = remote(part(owner, which), part(owner, which), sem, {"dp": flipped(mine, bit)})
                copy.start()
                sent.append(copy)
                coming = flipped(owner, bit)
                arrivals.append(remote(part(coming, which), part(coming, which), sem, {"dp": flipped(mine, bit)}))
                held[which].append(coming)
        yield
        for arrival in arrivals:
            arrival.wait_recv()
    for copy, _ in trades:
        copy.wait_send()
    for copy in sent:
        copy.wait_send()


def cuts_of(blocks, ctx):
    qkv, fc1, out, fc2, small = blocks
    head_cols, ff_cols = D // ctx, FF // ctx
    first = [(qkv, head_cols, part * D, part * head_cols) for part in range(3)]
    first.append((fc1, ff_cols, 0, 3 * head_cols))
    return [first, [(out, head_cols, 0, 0), (fc2, ff_cols, 0, head_cols)], [(small, LANES, None, 0)]]


def gather_kernel(ctx, dp, seqs, *refs):
    tokens, places, blocks = refs[0], refs[1], refs[2:7]
    tok_out, place_out, outs = refs[7], refs[8], refs[9:12]
    send, recv, own_sems, tok_sems = refs[12:]
    here = lax.axis_index("ctx")
    sems = Sems(send, recv)
    greet(ctx, dp)
    chains = [line_chain(places, place_out, sems, ctx)]
    for group, cuts in enumerate(cuts_of(blocks, ctx)):
        chains.append(weight_chain(cuts, outs[group], sems, own_sems.at[group], ctx, dp))
        if group < seqs:
            chains.append(line_chain(tokens.at[group], tok_out.at[group], sems, ctx))
    local = [
        pltpu.make_async_copy(tokens.at[seq], tok_out.at[seq, here], tok_sems.at[seq])
        for seq in range(seqs)
    ]
    local.append(pltpu.make_async_copy(places, place_out.at[here], tok_sems.at[seqs]))
    for copy in local:
        copy.start()
    run_chains(chains)
    for copy in local:
        copy.wait()


def gather_all(tokens, places, blocks, ctx, dp):
    seqs, span = tokens.shape[0], tokens.shape[1]
    rows = blocks[0].shape[0] * ctx * dp
    head_cols, ff_cols = D // ctx, FF // ctx
    copies = (seqs + 1) * 2 * (ctx - 1) + 7 * (ctx - 1) + 3 * 2 * (dp - 1)
    hbm = pl.BlockSpec(memory_space=pl.ANY)
    outs = pl.pallas_call(
        functools.partial(gather_kernel, ctx, dp, seqs),
        in_specs=[hbm] * 7,
        out_specs=[hbm] * 5,
        out_shape=[
            jax.ShapeDtypeStruct((seqs, ctx, span, D), bf16),
            jax.ShapeDtypeStruct((ctx,) + places.shape, f32),
            jax.ShapeDtypeStruct((rows, 3 * head_cols + ff_cols), bf16),
            jax.ShapeDtypeStruct((rows, head_cols + ff_cols), bf16),
            jax.ShapeDtypeStruct((rows, LANES), bf16),
        ],
        scratch_shapes=[
            pltpu.SemaphoreType.DMA((copies,)),
            pltpu.SemaphoreType.DMA((copies,)),
            pltpu.SemaphoreType.DMA((3, 4)),
            pltpu.SemaphoreType.DMA((seqs + 1,)),
        ],
        compiler_params=pltpu.CompilerParams(collective_id=1, has_side_effects=True),
        name="gather_all",
    )(tokens, places, *blocks)
    return outs[0], outs[1], outs[2:]


def add_into(target, other, rows):
    step = 32

    @pl.loop(0, rows // step)
    def _(index):
        here = pl.ds(pl.multiple_of(index * step, step), step)
        target[here, :] = target[here, :] + other[here, :]


def without(pattern, bit):
    return tuple(item for item in pattern if item != bit)


def patterns_of(bits):
    found = [()]
    for bit in bits:
        found += [pattern + (bit,) for pattern in found]
    return found


def owner_of(mine, pattern):
    for bit in pattern:
        mine = flipped(mine, bit)
    return mine


def patterns_for(dp):
    return sorted(patterns_of(bits_of(dp)[1:]), key=len, reverse=True)


class Slabs:
    def __init__(self, plan, x_v, turned, x_sems):
        self.plan, self.x_v, self.turned, self.x_sems = plan, x_v, turned, x_sems
        self.next = 0
        for index in (0, 1):
            self.start(index)
        self.wait(0)
        turned[0] = x_v[0].T

    def copies(self, index):
        arrays, owner = self.plan[index]
        slab = self.turned.shape[1]
        at = pl.ds(pl.multiple_of(owner * slab, LANES), slab)
        found = []
        for seq, array in enumerate(arrays):
            length = array.shape[0]
            found.append(
                pltpu.make_async_copy(
                    array.at[:, at],
                    self.x_v.at[index % 2, pl.ds(seq * length, length)],
                    self.x_sems.at[index % 2, seq],
                )
            )
        return found

    def start(self, index):
        for copy in self.copies(index):
            copy.start()

    def wait(self, index):
        for copy in self.copies(index):
            copy.wait()

    def multiply(self, y_v, cols, store):
        index = self.next
        self.next += 1
        more = index + 1 < len(self.plan)
        if index + 2 < len(self.plan):
            self.start(index + 2)
        if more:
            self.wait(index + 1)
        tile, rows = cols // 2, self.turned.shape[2] // 2

        @pl.loop(0, 2)
        def _(part):
            at = pl.ds(pl.multiple_of(part * tile, LANES), tile)
            if more:
                some = pl.ds(pl.multiple_of(part * rows, rows), rows)
                self.turned[(index + 1) % 2, :, some] = self.x_v[(index + 1) % 2, some, :].T
            store(at, mm(self.turned[index % 2], y_v[:, at], (1, 0)))


def pooled_chain(ys, parts, slabs, boxes, land_core, lands, sems, y_v, y_sems, own_sem, ctx, dp):
    here, mine = lax.axis_index("ctx"), lax.axis_index("dp")
    slab, cols = land_core.shape[1:]
    rows, half = slab // ctx, slab // 2
    far = bits_of(dp)[1:]
    patterns = patterns_for(dp)
    partner = flipped(mine, 1)
    loads = []
    for arrays, first in ys:
        for seq, array in enumerate(arrays):
            length, width = array.shape
            loads.append(
                pltpu.make_async_copy(
                    array,
                    y_v.at[pl.ds(seq * length, length), pl.ds(first, width)],
                    y_sems.at[len(loads)],
                )
            )
    for load in loads:
        load.start()
    for load in loads:
        load.wait()
    sent = []
    for index in range(len(patterns)):
        if boxes["sent"][index] is not None:
            boxes["sent"][index].wait_send()
        box = boxes["box"].at[index, :, pl.ds(0, cols)]

        def store(at, vals, index=index):
            boxes["box"][index, :, at] = vals.astype(bf16)

        slabs.multiply(y_v, cols, store)
        copy = remote(box, land_core.at[index], sems.take(), {"dp": partner})
        copy.start()
        boxes["sent"][index] = copy
        sent.append(copy)
    yield
    arrived, sent = sent, []
    held, coming = [{}, {}], [[], []]
    orders = [far, far[::-1]]
    used = 0

    def pass_on(which, stage, pattern, block):
        nonlocal used
        bit = orders[which][stage]
        copy = remote(block, lands.at[used], sems.take(), {"dp": flipped(mine, bit)})
        copy.start()
        sent.append(copy)
        coming[which].append((copy, lands.at[used], without(pattern, bit)))
        used += 1

    for index, pattern in enumerate(patterns):
        arrived[index].wait_recv()

        def store(at, vals, index=index):
            land_core[index, :, at] = (vals + land_core[index, :, at].astype(f32)).astype(bf16)

        slabs.multiply(y_v, cols, store)
        for which in range(2):
            block = land_core.at[index, pl.ds(which * half, half)]
            if orders[which][0] in pattern:
                pass_on(which, 0, pattern, block)
            else:
                held[which][pattern] = block
        if index == len(patterns) // 2 - 1:
            yield
    for stage in range(len(far)):
        yield
        for which in range(2):
            kept, arrivals = {}, coming[which]
            coming[which] = []
            for copy, landing, pattern in arrivals:
                copy.wait_recv()
                add_into(landing, held[which][pattern], half)
                if stage + 1 < len(far) and orders[which][stage + 1] in pattern:
                    pass_on(which, stage + 1, pattern, landing)
                else:
                    kept[pattern] = landing
            held[which] = kept
    final = [held[0][()], held[1][()]]
    trades = []

    def piece(which, peer, part):
        first = pl.multiple_of(peer * rows - which * half, rows)
        return final[which].at[pl.ds(first, rows), pl.ds(part[1], part[2])]

    def target(source, part):
        first = pl.multiple_of(part[3] + source * part[2], LANES)
        return part[0].at[:, pl.ds(first, part[2])]

    for by in range(1, ctx):
        peer = lax.rem(here + by, ctx)
        source = lax.rem(here + ctx - by, ctx)
        for part in parts:
            sem = sems.take()
            for which in range(2):

                @pl.when(peer // (ctx // 2) == which)
                def _():
                    remote(piece(which, peer, part), target(here, part), sem, {"ctx": peer}).start()

            trades.append((sem, peer, source, part))
    for which in range(2):

        @pl.when(here // (ctx // 2) == which)
        def _():
            for part in parts:
                copy = pltpu.make_async_copy(piece(which, here, part), target(here, part), own_sem)
                copy.start()
                copy.wait()

    yield
    for sem, peer, source, part in trades:
        some = final[0].at[pl.ds(0, rows), pl.ds(part[1], part[2])]
        remote(some, target(source, part), sem, {"ctx": peer}).wait_recv()
    for sem, peer, source, part in trades:
        some = final[0].at[pl.ds(0, rows), pl.ds(part[1], part[2])]
        remote(some, target(source, part), sem, {"ctx": peer}).wait_send()
    for copy in sent:
        copy.wait_send()


def sum_chain(partial, out, held, downs_land, ups_land, sems, load_sem, ctx):
    here = lax.axis_index("ctx")
    rows = held.shape[0] // ctx
    load = pltpu.make_async_copy(partial, held, load_sem)
    load.start()
    down_sems = [sems.take() for _ in range(1, ctx)]
    up_sems = [sems.take() for _ in range(1, ctx)]

    def chunk(index):
        return held.at[pl.ds(pl.multiple_of(index * rows, rows), rows)]

    def hop(block, step, down):
        lands, going = (downs_land, down_sems) if down else (ups_land, up_sems)
        by = -1 if down else 1
        return remote(block, lands.at[step - 1], going[step - 1], {"ctx": here + by})

    load.wait()

    @pl.when(here == ctx - 1)
    def _():
        for step in range(1, ctx):
            hop(chunk(step - 1), step, True).start()

    @pl.when(here == 0)
    def _():
        for step in range(1, ctx):
            hop(chunk(ctx - step), step, False).start()

    yield
    for step in range(2, ctx):

        @pl.when(jnp.logical_and(here < ctx - 1, here + step - ctx >= 0))
        def _():
            block = downs_land.at[step - 2]
            hop(block, step - 1, True).wait_recv()
            add_into(block, chunk(here + step - ctx), rows)
            hop(block, step, True).start()

        @pl.when(jnp.logical_and(here > 0, here + ctx - step <= ctx - 1))
        def _():
            block = ups_land.at[step - 2]
            hop(block, step - 1, False).wait_recv()
            add_into(block, chunk(here + ctx - step), rows)
            hop(block, step, False).start()

        yield

    @pl.when(here < ctx - 1)
    def _():
        hop(downs_land.at[ctx - 2], ctx - 1, True).wait_recv()

    @pl.when(here > 0)
    def _():
        hop(ups_land.at[ctx - 2], ctx - 1, False).wait_recv()

    step = 32

    @pl.loop(0, rows // step)
    def _(index):
        at = pl.ds(pl.multiple_of(index * step, step), step)
        mine = held[pl.ds(pl.multiple_of(here * rows + index * step, step), step), :].astype(f32)
        down = downs_land[ctx - 2, at, :].astype(f32)
        up = ups_land[ctx - 2, at, :].astype(f32)
        out[at, :] = (
            mine + jnp.where(here < ctx - 1, down, 0.0) + jnp.where(here > 0, up, 0.0)
        )

    for step in range(1, ctx):

        @pl.when(here + step - ctx >= 0)
        def _():
            hop(chunk(0), step, True).wait_send()

        @pl.when(here + ctx - step <= ctx - 1)
        def _():
            hop(chunk(0), step, False).wait_send()


def reduce_kernel(ctx, dp, seqs, *refs):
    partial, normal, attended, hidden, cot, d_qkv, d_pre = ([ref] for ref in refs[:7])
    length = partial[0].shape[0] // seqs
    partial = partial[0].at[pl.ds((seqs - 1) * length, length)]
    refs = refs[7:]
    sum_out, qkv_out, fc1_out, out_out, fc2_out = refs[:5]
    held, downs_land, ups_land, box, x_v, turned, y_v = refs[5:12]
    land_core, lands = refs[12:15], refs[15:18]
    send, recv, load_sem, x_sems, y_sems, own_sems = refs[18:]
    head_cols, ff_cols = D // ctx, FF // ctx
    parts = [
        [(out_out, 0, head_cols, 0), (fc2_out, head_cols, ff_cols, 0)],
        [(fc1_out, 0, ff_cols, 0)],
        [(qkv_out, part * head_cols, head_cols, part * D) for part in range(3)],
    ]
    ys = [[(attended, 0), (hidden, head_cols)], [(d_pre, 0)], [(d_qkv, 0)]]
    mine = lax.axis_index("dp")
    plan = []
    for arrays in (cot, normal, normal):
        for first in (flipped(mine, 1), mine):
            plan += [(arrays, owner_of(first, pattern)) for pattern in patterns_for(dp)]
    sems = Sems(send, recv)
    greet(ctx, dp)
    slabs = Slabs(plan, x_v, turned, x_sems)
    boxes = {"box": box, "sent": [None] * (dp // 2)}
    line = sum_chain(partial, sum_out, held, downs_land, ups_land, sems, load_sem, ctx)
    groups = [
        pooled_chain(
            ys[group], parts[group], slabs, boxes, land_core[group], lands[group],
            sems, y_v, y_sems, own_sems.at[group], ctx, dp,
        )
        for group in range(3)
    ]
    first, second, third = groups
    order = [line, first, first, first, second, first, line, second, second, first]
    order += [third, second, line, third, third, first, second, third, third, second, line, third, line]
    run_in(order, [line] + groups)
    for copy in boxes["sent"]:
        copy.wait_send()


def run_in(order, chains):
    ended = set()
    turn = 0
    while len(ended) < len(chains):
        chain = order[turn] if turn < len(order) else chains[(turn - len(order)) % len(chains)]
        turn += 1
        if id(chain) in ended:
            continue
        try:
            next(chain)
        except StopIteration:
            ended.add(id(chain))


def reduce_all(partial, normal, attended, hidden, cot, d_qkv, d_pre, seqs, ctx, dp):
    length = partial.shape[0] // seqs
    rows = length // ctx
    slab = D // dp
    copies = 2 * (ctx - 1) + 3 * (dp // 2 + dp - 2) + 6 * (ctx - 1)
    hbm = pl.BlockSpec(memory_space=pl.ANY)
    vmem = pl.BlockSpec(memory_space=pltpu.VMEM)
    head_cols, ff_cols = D // ctx, FF // ctx
    cols = [head_cols + ff_cols, ff_cols, 3 * head_cols]
    outs = pl.pallas_call(
        functools.partial(reduce_kernel, ctx, dp, seqs),
        in_specs=[hbm] * 7,
        out_specs=[vmem] + [hbm] * 4,
        out_shape=[jax.ShapeDtypeStruct((rows, partial.shape[1]), f32)]
        + [jax.ShapeDtypeStruct((slab // ctx, width), bf16) for width in (3 * D, FF, D, FF)],
        scratch_shapes=[pltpu.VMEM((length, partial.shape[1]), bf16)]
        + [pltpu.VMEM((ctx - 1, rows, partial.shape[1]), bf16)] * 2
        + [
            pltpu.VMEM((dp // 2, slab, cols[0]), bf16),
            pltpu.VMEM((2, seqs * length, slab), bf16),
            pltpu.VMEM((2, slab, seqs * length), bf16),
            pltpu.VMEM((seqs * length, cols[0]), bf16),
        ]
        + [pltpu.VMEM((dp // 2, slab, width), bf16) for width in cols]
        + [pltpu.VMEM((dp - 2, slab // 2, width), bf16) for width in cols]
        + [
            pltpu.SemaphoreType.DMA((copies,)),
            pltpu.SemaphoreType.DMA((copies,)),
            pltpu.SemaphoreType.DMA,
            pltpu.SemaphoreType.DMA((2, seqs)),
            pltpu.SemaphoreType.DMA((2 * seqs,)),
            pltpu.SemaphoreType.DMA((3,)),
        ],
        compiler_params=pltpu.CompilerParams(
            collective_id=2, has_side_effects=True, vmem_limit_bytes=GRANT
        ),
        cost_estimate=pl.CostEstimate(flops=150 * 10**9, bytes_accessed=10**8, transcendentals=0),
        name="reduce_all",
    )(partial, normal, attended, hidden, cot, d_qkv, d_pre)
    return outs[0], outs[1:]


def normalised(rows_in):
    row_mean = jnp.mean(rows_in, axis=-1, keepdims=True)
    centred = rows_in - row_mean
    variance = jnp.mean(centred * centred, axis=-1, keepdims=True)
    inv_std = lax.rsqrt(variance + 1e-05)
    return centred * inv_std, inv_std


def gelu_both(pre):
    return jax.vjp(lambda vals: jax.nn.gelu(vals, approximate=True), pre)


def per_device(
    tokens,
    cotangent,
    positions,
    wqkv_master,
    fc1_master,
    out_master,
    fc2_master,
    small_master,
    wqkv_first,
    wqkv_second,
    fc1_first,
    fc1_second,
    out_first,
    out_second,
    fc2_first,
    fc2_second,
    small_first,
    small_second,
):
    seqs, span = tokens.shape[0], tokens.shape[1]
    ctx, dp = lax.axis_size("ctx"), lax.axis_size("dp")
    ctx_index = lax.axis_index("ctx")
    length = span * ctx
    total_rows = seqs * length
    own_rows = wqkv_master.shape[0]
    head_cols, ff_cols = D // ctx, FF // ctx

    gate = lax.optimization_barrier
    small_low = jnp.pad(small_master.astype(bf16), ((0, 0), (0, LANES - small_master.shape[1])))
    blocks = [wqkv_master, fc1_master, out_master, fc2_master]
    blocks = [block.astype(bf16) for block in blocks] + [small_low]
    places = jnp.pad(positions.astype(f32).reshape(-1, LANES), ((0, 8 - seqs * span // LANES), (0, 0)))
    tok_all, place, (in_w, of_w, small_all) = gather_all(tokens, places, blocks, ctx, dp)
    qkv_w, fc1_w = in_w[:, : 3 * head_cols], in_w[:, 3 * head_cols :]
    params = small_all[:, :16].astype(f32)
    place = place[:, : seqs * span // LANES].reshape(ctx, seqs, span)
    place = jnp.transpose(place, (1, 0, 2)).reshape(total_rows)
    half_rot = ROT // 2
    exponent = jnp.arange(half_rot, dtype=f32) * (-2.0 / ROT)
    frequency = jnp.power(f32(10000.0), exponent)
    angles = frequency[:, None] * place[None, :]
    cos_s, sin_s = jnp.cos(angles), jnp.sin(angles)
    none = jnp.zeros_like(cos_s)
    rest = jnp.zeros((HD - ROT, total_rows), f32)
    tables = [
        jnp.concatenate([cos_s, cos_s, rest + 1.0] * 2, axis=0),
        jnp.concatenate([-sin_s, none, rest] * 2, axis=0),
        jnp.concatenate([none, sin_s, rest] * 2, axis=0),
    ]

    def my_part(values, cols):
        return lax.dynamic_slice_in_dim(values, ctx_index * cols, cols, values.ndim - 1)

    qkv_bias = my_part(params[:, 2:5].T, head_cols)
    fc1_bias = my_part(params[:, 6:10].T.reshape(FF), ff_cols)
    gain, shift = params[:, 0], params[:, 1]
    def scattered(partial):
        return lax.psum_scatter(partial, "ctx", scatter_dimension=1, tiled=True).astype(f32)

    cot, tok_all = gate((cotangent, tok_all))
    cot_all = lax.all_gather(cot, "ctx", axis=1, tiled=True).reshape(total_rows, D)
    normal_low = normalised(tok_all.reshape(total_rows, D).astype(f32))[0]
    normal_low = (normal_low * gain + shift).astype(bf16)
    projected = mm(normal_low, in_w[:, : 3 * head_cols], (1, 0))
    query, key, value, attended, log_total = attend(projected, qkv_bias, tables, seqs)
    pre = mm(normal_low, in_w[:, 3 * head_cols :], (1, 0)) + fc1_bias
    hidden = gelu_both(pre)[0].astype(bf16)
    branch = mm(jnp.concatenate([attended, hidden], axis=1), of_w, (1, 1)).astype(bf16)
    pre, hidden, branch, cot_all = gate((pre, hidden, branch, cot_all))
    mix = scattered(branch.reshape(seqs, length, D))
    back = mm(cot_all, of_w[:, :head_cols], (1, 0)).astype(bf16)
    grad_hidden = mm(cot_all, of_w[:, head_cols:], (1, 0))
    d_pre = gelu_both(pre)[1](grad_hidden)[0].astype(bf16)
    d_qkv = attend_back(query, key, value, back, log_total, tables, seqs)
    d_part = mm(jnp.concatenate([d_qkv, d_pre], axis=1), in_w, (1, 1)).astype(bf16)
    sum_qkv, sum_pre = (jnp.sum(part, axis=0, dtype=f32) for part in (d_qkv, d_pre))
    d_qkv, d_pre, d_part, mix, sum_qkv, sum_pre = gate(
        (d_qkv, d_pre, d_part, mix, sum_qkv, sum_pre)
    )
    others = scattered(d_part[: total_rows - length].reshape(seqs - 1, length, D))
    sum_out = jnp.sum(cotangent.astype(f32), axis=(0, 1))[None]
    normed, inv_std = normalised(tokens.astype(f32))
    last, grads = reduce_all(
        d_part, normal_low, attended, hidden, cot_all, d_qkv, d_pre, seqs, ctx, dp
    )
    d_normal = [others[seq] for seq in range(seqs - 1)] + [last]

    def spread(sums, count, cols):
        whole = jnp.zeros((count, ctx * cols), f32)
        return lax.dynamic_update_slice_in_dim(whole, sums.reshape(count, cols), ctx_index * cols, 1)

    sum_qkv = spread(sum_qkv, 3, head_cols)
    sum_pre = spread(sum_pre, 1, ff_cols).reshape(4, D)
    gain_terms = sum(jnp.sum(part * normed[seq], axis=0) for seq, part in enumerate(d_normal))[None]
    shift_terms = sum(jnp.sum(part, axis=0) for part in d_normal)[None]
    small_terms = jnp.concatenate(
        [gain_terms, shift_terms, sum_qkv, sum_out, sum_pre, sum_out], axis=0
    )
    small_sent = jnp.transpose(small_terms.reshape(11, ctx * dp, own_rows), (1, 0, 2))
    small_sent, d_normal, grads, mix = gate((small_sent, d_normal, grads, mix))
    small_got = lax.all_to_all(small_sent.reshape(ctx * dp, 1, 11 * own_rows), EVERY, 0, 0, tiled=True)
    small_grad = jnp.sum(small_got, axis=(0, 1)).reshape(11, own_rows).T

    qkv_grad, fc1_grad, out_grad, fc2_grad = (grad.astype(f32) for grad in grads)
    mixed = (tokens.astype(f32) + mix + params[:, 5] + params[:, 10]).astype(bf16)
    d_scaled = jnp.stack(d_normal) * gain
    input_grad = cotangent.astype(f32) + inv_std * (
        d_scaled
        - jnp.mean(d_scaled, axis=-1, keepdims=True)
        - normed * jnp.mean(d_scaled * normed, axis=-1, keepdims=True)
    )
    qkv_new = adamw(wqkv_master, wqkv_first, wqkv_second, qkv_grad, 0.04, 0.1)
    fc1_new = adamw(fc1_master, fc1_first, fc1_second, fc1_grad, 0.04, 0.1)
    out_new = adamw(out_master, out_first, out_second, out_grad, 0.4, 0.1)
    fc2_new = adamw(fc2_master, fc2_first, fc2_second, fc2_grad, 0.02, 0.1)
    small_new = adamw(small_master, small_first, small_second, small_grad, 0.3, 0.0)
    return (mixed, input_grad, *qkv_new, *fc1_new, *out_new, *fc2_new, *small_new)


def solution(mesh):
    split = P("dp", "ctx", None)
    rows = P(("dp", "ctx"), None)
    return jax.shard_map(
        per_device,
        mesh=mesh,
        in_specs=(split, split, P("dp", "ctx")) + (rows,) * 15,
        out_specs=(split, split) + (rows,) * 15,
        check_vma=False,
    )
```

```python
import functools

import jax
import jax.numpy as jnp
from jax import lax
from jax.experimental import pallas as pl
from jax.experimental.pallas import tpu as pltpu
from jax.sharding import PartitionSpec as P

D = 2048
H = 32
HD = 64
ROT = 32
FF = 8192
STEP = 10
LANES = 128
BLOCK = 256

beta_one = 0.9
beta_two = 0.95
epsilon = 1e-08

f32 = jnp.float32
bf16 = jnp.bfloat16
EVERY = ("dp", "ctx")
GRANT = 58 * 1024 * 1024


def adamw(weight, first_old, second_old, gradient, step_rate, decay):
    first_new = beta_one * first_old + (1.0 - beta_one) * gradient
    second_new = beta_two * second_old + (1.0 - beta_two) * gradient * gradient
    first_hat = first_new / (1.0 - beta_one**STEP)
    second_hat = second_new / (1.0 - beta_two**STEP)
    weight_new = weight - step_rate * (
        first_hat / (jnp.sqrt(second_hat) + epsilon) + decay * weight
    )
    return (first_new, second_new, weight_new)


def mm(left, right, dims):
    return lax.dot_general(left, right, ((dims[:1], dims[1:]), ((), ())), preferred_element_type=f32)


def rotated(vals, cos_t, lead, trail):
    return (
        vals * cos_t + pltpu.roll(vals, LANES - 16, 1) * lead + pltpu.roll(vals, 16, 1) * trail
    )


def unrotated(vals, cos_t, lead, trail):
    return (
        vals * cos_t - pltpu.roll(vals, LANES - 16, 1) * lead - pltpu.roll(vals, 16, 1) * trail
    )


def attend_kernel(
    q_in, k_in, v_in, bias, cos_ref, lead_ref, trail_ref, q_out, k_out, v_out, o_out, log_out
):
    rows = q_in.shape[0]
    cos_t, lead, trail = cos_ref[...].T, lead_ref[...].T, trail_ref[...].T
    scale = HD ** (-0.5)
    query = rotated(q_in[...] + bias[0:1, :], cos_t, lead, trail).astype(bf16)
    key = rotated(k_in[...] + bias[1:2, :], cos_t, lead, trail).astype(bf16)
    value = (v_in[...] + bias[2:3, :]).astype(bf16)
    query = query * jnp.asarray(scale, bf16)
    q_out[...] = query
    k_out[...] = key
    v_out[...] = value
    lane = lax.broadcasted_iota(jnp.int32, (BLOCK, LANES), 1)
    on_diagonal = lax.broadcasted_iota(jnp.int32, (BLOCK, BLOCK), 1) <= lax.broadcasted_iota(
        jnp.int32, (BLOCK, BLOCK), 0
    )
    for step in range(rows // BLOCK):
        start = step * BLOCK
        stop = start + BLOCK
        out = None
        for head in range(2):
            mine = (lane < HD) if head == 0 else (lane >= HD)
            q_head = jnp.where(mine, query[start:stop], jnp.zeros((), bf16))
            last = jnp.where(on_diagonal, mm(q_head, key[start:stop], (1, 1)), -1e30)
            parts = [last]
            if start:
                parts = [mm(q_head, key[:start], (1, 1)), last]
            best = functools.reduce(
                jnp.maximum, [jnp.max(part, axis=1, keepdims=True) for part in parts]
            )
            parts = [jnp.exp(part - best) for part in parts]
            total = sum(jnp.sum(part, axis=1, keepdims=True) for part in parts)
            log_out[0, head, start:stop] = (best + jnp.log(total))[:, 0]
            mixed = mm(parts[-1].astype(bf16), value[start:stop], (1, 0))
            if start:
                mixed = mixed + mm(parts[0].astype(bf16), value[:start], (1, 0))
            mixed = mixed / total
            out = mixed if head == 0 else jnp.where(mine, mixed, out)
        o_out[start:stop, :] = out.astype(bf16)


def attend_back_kernel(
    q_in, k_in, v_in, g_in, log_in, cos_ref, lead_ref, trail_ref, d_out, dq_sum, dk_sum, dv_sum
):
    rows = q_in.shape[0]
    scale = HD ** (-0.5)
    lane = lax.broadcasted_iota(jnp.int32, (BLOCK, LANES), 1)
    on_diagonal = lax.broadcasted_iota(jnp.int32, (BLOCK, BLOCK), 0) <= lax.broadcasted_iota(
        jnp.int32, (BLOCK, BLOCK), 1
    )
    dk_sum[...] = jnp.zeros_like(dk_sum)
    dv_sum[...] = jnp.zeros_like(dv_sum)
    key_all = k_in[...]
    value_all = v_in[...]
    zero = jnp.zeros((), bf16)
    for step in range(rows // BLOCK):
        start = step * BLOCK
        stop = start + BLOCK
        d_query = None
        for head in range(2):
            mine = (lane < HD) if head == 0 else (lane >= HD)
            q_head = jnp.where(mine, q_in[start:stop], zero)
            g_head = jnp.where(mine, g_in[start:stop], zero)
            log_row = log_in[0, head : head + 1, start:stop]
            last = jnp.where(
                on_diagonal, jnp.exp(mm(key_all[start:stop], q_head, (1, 1)) - log_row), 0.0
            )
            probs = [(start, stop, last)]
            if start:
                probs.append((0, start, jnp.exp(mm(key_all[:start], q_head, (1, 1)) - log_row)))
            grads = [mm(value_all[lo:hi], g_head, (1, 1)) for lo, hi, _ in probs]
            delta = sum(
                jnp.sum(prob * grad, axis=0, keepdims=True)
                for (_, _, prob), grad in zip(probs, grads)
            )
            part = None
            for (lo, hi, prob), grad in zip(probs, grads):
                d_score = (prob * (grad - delta)).astype(bf16)
                dv_sum[lo:hi, :] += mm(prob.astype(bf16), g_head, (1, 0))
                dk_sum[lo:hi, :] += mm(d_score, q_head, (1, 0))
                added = mm(d_score, key_all[lo:hi], (0, 0))
                part = added if part is None else part + added
            d_query = part if head == 0 else jnp.where(mine, part, d_query)
        dq_sum[start:stop, :] = d_query * scale
    cos_t, lead, trail = cos_ref[...].T, lead_ref[...].T, trail_ref[...].T
    width = d_out.shape[1] // 3

    def put(which, vals):
        first = pl.multiple_of(which * width + pl.program_id(1) * LANES, LANES)
        d_out[:, pl.ds(first, LANES)] = vals.astype(bf16)

    put(0, unrotated(dq_sum[...], cos_t, lead, trail))
    put(1, unrotated(dk_sum[...], cos_t, lead, trail))
    put(2, dv_sum[...])


def attend(mixed_qkv, bias, tables, seqs):
    rows, width = mixed_qkv.shape[0] // seqs, mixed_qkv.shape[1] // 3
    pairs = width // LANES

    def part(which):
        return pl.BlockSpec((rows, LANES), lambda s, p: (s, which * pairs + p))

    block = pl.BlockSpec((rows, LANES), lambda s, p: (s, p))
    table = pl.BlockSpec((LANES, rows), lambda s, p: (0, s))
    low = jax.ShapeDtypeStruct((seqs * rows, width), bf16)
    return pl.pallas_call(
        attend_kernel,
        grid=(seqs, pairs),
        in_specs=[part(0), part(1), part(2), pl.BlockSpec((3, LANES), lambda s, p: (0, p))]
        + [table] * 3,
        out_specs=[block] * 4 + [pl.BlockSpec((1, 2, rows), lambda s, p: (s * pairs + p, 0, 0))],
        out_shape=[low] * 4 + [jax.ShapeDtypeStruct((seqs * pairs, 2, rows), f32)],
        compiler_params=pltpu.CompilerParams(vmem_limit_bytes=GRANT),
        cost_estimate=pl.CostEstimate(flops=20 * 10**9, bytes_accessed=10**7, transcendentals=0),
        name="attend",
    )(mixed_qkv, mixed_qkv, mixed_qkv, bias, *tables)


def attend_back(query, key, value, back, log_total, tables, seqs):
    rows, width = query.shape[0] // seqs, query.shape[1]
    pairs = width // LANES
    block = pl.BlockSpec((rows, LANES), lambda s, p: (s, p))
    table = pl.BlockSpec((LANES, rows), lambda s, p: (0, s))
    return pl.pallas_call(
        attend_back_kernel,
        grid=(seqs, pairs),
        in_specs=[block] * 4
        + [pl.BlockSpec((1, 2, rows), lambda s, p: (s * pairs + p, 0, 0))]
        + [table] * 3,
        out_specs=pl.BlockSpec((rows, 3 * width), lambda s, p: (s, 0)),
        out_shape=jax.ShapeDtypeStruct((seqs * rows, 3 * width), bf16),
        scratch_shapes=[pltpu.VMEM((rows, LANES), f32)] * 3,
        compiler_params=pltpu.CompilerParams(vmem_limit_bytes=GRANT),
        cost_estimate=pl.CostEstimate(flops=30 * 10**9, bytes_accessed=10**7, transcendentals=0),
        name="attend_back",
    )(query, key, value, back, log_total, *tables)


def bits_of(count):
    bits = []
    bit = 1
    while bit < count:
        bits.append(bit)
        bit *= 2
    return bits


def flipped(index, bit):
    return index + bit * (1 - 2 * ((index // bit) % 2))


def run_chains(chains):
    chains = [chain for chain in chains]
    for chain in chains:
        next(chain)
    while chains:
        left = []
        for chain in chains:
            try:
                next(chain)
                left.append(chain)
            except StopIteration:
                pass
        chains = left


class Sems:
    def __init__(self, send, recv):
        self.send, self.recv, self.used = send, recv, 0

    def take(self):
        self.used += 1
        return self.send.at[self.used - 1], self.recv.at[self.used - 1]


def remote(src, dst, sems, target):
    return pltpu.make_async_remote_copy(
        src_ref=src,
        dst_ref=dst,
        send_sem=sems[0],
        recv_sem=sems[1],
        device_id=target,
        device_id_type=pl.DeviceIdType.MESH,
    )


def greet(ctx, dp):
    here, mine = lax.axis_index("ctx"), lax.axis_index("dp")
    barrier = pltpu.get_barrier_semaphore()
    targets = [{"ctx": lax.rem(here + by, ctx)} for by in range(1, ctx)]
    targets += [{"dp": flipped(mine, bit)} for bit in bits_of(dp)]
    for target in targets:
        pl.semaphore_signal(barrier, inc=1, device_id=target, device_id_type=pl.DeviceIdType.MESH)
    pl.semaphore_wait(barrier, len(targets))


def line_chain(src, out, sems, ctx):
    here = lax.axis_index("ctx")
    ups = [sems.take() for _ in range(1, ctx)]
    downs = [sems.take() for _ in range(1, ctx)]

    def hop(block, slot, step, going):
        by = 1 if going is ups else -1
        return remote(block, out.at[slot], going[step], {"ctx": here + by})

    @pl.when(here < ctx - 1)
    def _():
        hop(src, here, 0, ups).start()

    @pl.when(here > 0)
    def _():
        hop(src, here, 0, downs).start()

    yield
    for step in range(1, ctx):
        for going, sign in ((ups, -1), (downs, 1)):
            slot = here + sign * step
            inside = (slot >= 0) if sign < 0 else (slot < ctx)
            more = (here < ctx - 1) if sign < 0 else (here > 0)
            if step < ctx - 1:

                @pl.when(jnp.logical_and(inside, more))
                def _():
                    hop(out.at[slot], slot, step - 1, going).wait_recv()
                    hop(out.at[slot], slot, step, going).start()

                @pl.when(jnp.logical_and(inside, jnp.logical_not(more)))
                def _():
                    hop(out.at[slot], slot, step - 1, going).wait_recv()

            else:

                @pl.when(inside)
                def _():
                    hop(out.at[slot], slot, step - 1, going).wait_recv()

        yield

    for step in range(ctx - 1):
        for going, sign in ((ups, -1), (downs, 1)):
            slot = here + sign * step
            inside = (slot >= 0) if sign < 0 else (slot < ctx)
            more = (here < ctx - 1) if sign < 0 else (here > 0)

            @pl.when(jnp.logical_and(inside, more))
            def _():
                hop(out.at[slot], slot, step, going).wait_send()


def weight_chain(cuts, out, sems, own_sem, ctx, dp):
    here, mine = lax.axis_index("ctx"), lax.axis_index("dp")
    rows = cuts[0][0].shape[0]
    slab = rows * ctx
    half = slab // 2

    def piece(owner, cut):
        at = pl.ds(pl.multiple_of((mine * ctx + owner) * rows, rows), rows)
        return out.at[at, pl.ds(cut[3], cut[1])]

    def taken(peer, cut):
        block, width, first, _ = cut
        if first is None:
            return block
        return block.at[:, pl.ds(pl.multiple_of(first + peer * width, LANES), width)]

    def part(owner, which):
        return out.at[pl.ds(pl.multiple_of(owner * slab + which * half, half), half)]

    trades, own = [], []
    for by in range(1, ctx):
        peer = lax.rem(here + by, ctx)
        source = lax.rem(here + ctx - by, ctx)
        for cut in cuts:
            sem = sems.take()
            copy = remote(taken(peer, cut), piece(here, cut), sem, {"ctx": peer})
            copy.start()
            trades.append((copy, remote(taken(peer, cut), piece(source, cut), sem, {"ctx": peer})))
    for index, cut in enumerate(cuts):
        copy = pltpu.make_async_copy(taken(here, cut), piece(here, cut), own_sem.at[index])
        copy.start()
        own.append(copy)
    yield
    for _, arrival in trades:
        arrival.wait_recv()
    for copy in own:
        copy.wait()
    far = bits_of(dp)[1:]
    orders = [far + [1], far[::-1] + [1]]
    held = [[mine], [mine]]
    sent = []
    for stage in range(len(far) + 1):
        arrivals = []
        for which in range(2):
            bit = orders[which][stage]
            for owner in list(held[which]):
                sem = sems.take()
                copy = remote(part(owner, which), part(owner, which), sem, {"dp": flipped(mine, bit)})
                copy.start()
                sent.append(copy)
                coming = flipped(owner, bit)
                arrivals.append(remote(part(coming, which), part(coming, which), sem, {"dp": flipped(mine, bit)}))
                held[which].append(coming)
        yield
        for arrival in arrivals:
            arrival.wait_recv()
    for copy, _ in trades:
        copy.wait_send()
    for copy in sent:
        copy.wait_send()


def cuts_of(blocks, ctx):
    qkv, fc1, out, fc2, small = blocks
    head_cols, ff_cols = D // ctx, FF // ctx
    first = [(qkv, head_cols, part * D, part * head_cols) for part in range(3)]
    first.append((fc1, ff_cols, 0, 3 * head_cols))
    return [first, [(out, head_cols, 0, 0), (fc2, ff_cols, 0, head_cols)], [(small, LANES, None, 0)]]


def gather_kernel(ctx, dp, seqs, *refs):
    tokens, places, blocks = refs[0], refs[1], refs[2:7]
    tok_out, place_out, outs = refs[7], refs[8], refs[9:12]
    send, recv, own_sems, tok_sems = refs[12:]
    here = lax.axis_index("ctx")
    sems = Sems(send, recv)
    greet(ctx, dp)
    chains = [line_chain(places, place_out, sems, ctx)]
    for group, cuts in enumerate(cuts_of(blocks, ctx)):
        chains.append(weight_chain(cuts, outs[group], sems, own_sems.at[group], ctx, dp))
        if group < seqs:
            chains.append(line_chain(tokens.at[group], tok_out.at[group], sems, ctx))
    local = [
        pltpu.make_async_copy(tokens.at[seq], tok_out.at[seq, here], tok_sems.at[seq])
        for seq in range(seqs)
    ]
    local.append(pltpu.make_async_copy(places, place_out.at[here], tok_sems.at[seqs]))
    for copy in local:
        copy.start()
    run_chains(chains)
    for copy in local:
        copy.wait()


def gather_all(tokens, places, blocks, ctx, dp):
    seqs, span = tokens.shape[0], tokens.shape[1]
    rows = blocks[0].shape[0] * ctx * dp
    head_cols, ff_cols = D // ctx, FF // ctx
    copies = (seqs + 1) * 2 * (ctx - 1) + 7 * (ctx - 1) + 3 * 2 * (dp - 1)
    hbm = pl.BlockSpec(memory_space=pl.ANY)
    outs = pl.pallas_call(
        functools.partial(gather_kernel, ctx, dp, seqs),
        in_specs=[hbm] * 7,
        out_specs=[hbm] * 5,
        out_shape=[
            jax.ShapeDtypeStruct((seqs, ctx, span, D), bf16),
            jax.ShapeDtypeStruct((ctx,) + places.shape, f32),
            jax.ShapeDtypeStruct((rows, 3 * head_cols + ff_cols), bf16),
            jax.ShapeDtypeStruct((rows, head_cols + ff_cols), bf16),
            jax.ShapeDtypeStruct((rows, LANES), bf16),
        ],
        scratch_shapes=[
            pltpu.SemaphoreType.DMA((copies,)),
            pltpu.SemaphoreType.DMA((copies,)),
            pltpu.SemaphoreType.DMA((3, 4)),
            pltpu.SemaphoreType.DMA((seqs + 1,)),
        ],
        compiler_params=pltpu.CompilerParams(collective_id=1, has_side_effects=True),
        name="gather_all",
    )(tokens, places, *blocks)
    return outs[0], outs[1], outs[2:]


def add_into(target, other, rows):
    step = 32

    @pl.loop(0, rows // step)
    def _(index):
        here = pl.ds(pl.multiple_of(index * step, step), step)
        target[here, :] = target[here, :] + other[here, :]


def without(pattern, bit):
    return tuple(item for item in pattern if item != bit)


def patterns_of(bits):
    found = [()]
    for bit in bits:
        found += [pattern + (bit,) for pattern in found]
    return found


def owner_of(mine, pattern):
    for bit in pattern:
        mine = flipped(mine, bit)
    return mine


def patterns_for(dp):
    return sorted(patterns_of(bits_of(dp)[1:]), key=len, reverse=True)


class Slabs:
    def __init__(self, plan, x_v, turned, x_sems):
        self.plan, self.x_v, self.turned, self.x_sems = plan, x_v, turned, x_sems
        self.next = 0
        for index in (0, 1):
            self.start(index)
        self.wait(0)
        turned[0] = x_v[0].T

    def copies(self, index):
        arrays, owner = self.plan[index]
        slab = self.turned.shape[1]
        at = pl.ds(pl.multiple_of(owner * slab, LANES), slab)
        found = []
        for seq, array in enumerate(arrays):
            length = array.shape[0]
            found.append(
                pltpu.make_async_copy(
                    array.at[:, at],
                    self.x_v.at[index % 2, pl.ds(seq * length, length)],
                    self.x_sems.at[index % 2, seq],
                )
            )
        return found

    def start(self, index):
        for copy in self.copies(index):
            copy.start()

    def wait(self, index):
        for copy in self.copies(index):
            copy.wait()

    def multiply(self, y_v, cols, store):
        index = self.next
        self.next += 1
        more = index + 1 < len(self.plan)
        if index + 2 < len(self.plan):
            self.start(index + 2)
        if more:
            self.wait(index + 1)
        tile, rows = cols // 2, self.turned.shape[2] // 2

        @pl.loop(0, 2)
        def _(part):
            at = pl.ds(pl.multiple_of(part * tile, LANES), tile)
            if more:
                some = pl.ds(pl.multiple_of(part * rows, rows), rows)
                self.turned[(index + 1) % 2, :, some] = self.x_v[(index + 1) % 2, some, :].T
            store(at, mm(self.turned[index % 2], y_v[:, at], (1, 0)))


def pooled_chain(ys, parts, slabs, boxes, land_core, lands, sems, y_v, y_sems, own_sem, ctx, dp):
    here, mine = lax.axis_index("ctx"), lax.axis_index("dp")
    slab, cols = land_core.shape[1:]
    rows, half = slab // ctx, slab // 2
    far = bits_of(dp)[1:]
    patterns = patterns_for(dp)
    partner = flipped(mine, 1)
    loads = []
    for arrays, first in ys:
        for seq, array in enumerate(arrays):
            length, width = array.shape
            loads.append(
                pltpu.make_async_copy(
                    array,
                    y_v.at[pl.ds(seq * length, length), pl.ds(first, width)],
                    y_sems.at[len(loads)],
                )
            )
    for load in loads:
        load.start()
    for load in loads:
        load.wait()
    sent = []
    for index in range(len(patterns)):
        if boxes["sent"][index] is not None:
            boxes["sent"][index].wait_send()
        box = boxes["box"].at[index, :, pl.ds(0, cols)]

        def store(at, vals, index=index):
            boxes["box"][index, :, at] = vals.astype(bf16)

        slabs.multiply(y_v, cols, store)
        copy = remote(box, land_core.at[index], sems.take(), {"dp": partner})
        copy.start()
        boxes["sent"][index] = copy
        sent.append(copy)
    yield
    arrived, sent = sent, []
    held, coming = [{}, {}], [[], []]
    orders = [far, far[::-1]]
    used = 0

    def pass_on(which, stage, pattern, block):
        nonlocal used
        bit = orders[which][stage]
        copy = remote(block, lands.at[used], sems.take(), {"dp": flipped(mine, bit)})
        copy.start()
        sent.append(copy)
        coming[which].append((copy, lands.at[used], without(pattern, bit)))
        used += 1

    for index, pattern in enumerate(patterns):
        arrived[index].wait_recv()

        def store(at, vals, index=index):
            land_core[index, :, at] = (vals + land_core[index, :, at].astype(f32)).astype(bf16)

        slabs.multiply(y_v, cols, store)
        for which in range(2):
            block = land_core.at[index, pl.ds(which * half, half)]
            if orders[which][0] in pattern:
                pass_on(which, 0, pattern, block)
            else:
                held[which][pattern] = block
        if index == len(patterns) // 2 - 1:
            yield
    for stage in range(len(far)):
        yield
        for which in range(2):
            kept, arrivals = {}, coming[which]
            coming[which] = []
            for copy, landing, pattern in arrivals:
                copy.wait_recv()
                add_into(landing, held[which][pattern], half)
                if stage + 1 < len(far) and orders[which][stage + 1] in pattern:
                    pass_on(which, stage + 1, pattern, landing)
                else:
                    kept[pattern] = landing
            held[which] = kept
    final = [held[0][()], held[1][()]]
    trades = []

    def piece(which, peer, part):
        first = pl.multiple_of(peer * rows - which * half, rows)
        return final[which].at[pl.ds(first, rows), pl.ds(part[1], part[2])]

    def target(source, part):
        first = pl.multiple_of(part[3] + source * part[2], LANES)
        return part[0].at[:, pl.ds(first, part[2])]

    for by in range(1, ctx):
        peer = lax.rem(here + by, ctx)
        source = lax.rem(here + ctx - by, ctx)
        for part in parts:
            sem = sems.take()
            for which in range(2):

                @pl.when(peer // (ctx // 2) == which)
                def _():
                    remote(piece(which, peer, part), target(here, part), sem, {"ctx": peer}).start()

            trades.append((sem, peer, source, part))
    for which in range(2):

        @pl.when(here // (ctx // 2) == which)
        def _():
            for part in parts:
                copy = pltpu.make_async_copy(piece(which, here, part), target(here, part), own_sem)
                copy.start()
                copy.wait()

    yield
    for sem, peer, source, part in trades:
        some = final[0].at[pl.ds(0, rows), pl.ds(part[1], part[2])]
        remote(some, target(source, part), sem, {"ctx": peer}).wait_recv()
    for sem, peer, source, part in trades:
        some = final[0].at[pl.ds(0, rows), pl.ds(part[1], part[2])]
        remote(some, target(source, part), sem, {"ctx": peer}).wait_send()
    for copy in sent:
        copy.wait_send()


def sum_chain(partial, out, held, downs_land, ups_land, sems, load_sem, ctx):
    here = lax.axis_index("ctx")
    rows = held.shape[0] // ctx
    load = pltpu.make_async_copy(partial, held, load_sem)
    load.start()
    down_sems = [sems.take() for _ in range(1, ctx)]
    up_sems = [sems.take() for _ in range(1, ctx)]

    def chunk(index):
        return held.at[pl.ds(pl.multiple_of(index * rows, rows), rows)]

    def hop(block, step, down):
        lands, going = (downs_land, down_sems) if down else (ups_land, up_sems)
        by = -1 if down else 1
        return remote(block, lands.at[step - 1], going[step - 1], {"ctx": here + by})

    load.wait()

    @pl.when(here == ctx - 1)
    def _():
        for step in range(1, ctx):
            hop(chunk(step - 1), step, True).start()

    @pl.when(here == 0)
    def _():
        for step in range(1, ctx):
            hop(chunk(ctx - step), step, False).start()

    yield
    for step in range(2, ctx):

        @pl.when(jnp.logical_and(here < ctx - 1, here + step - ctx >= 0))
        def _():
            block = downs_land.at[step - 2]
            hop(block, step - 1, True).wait_recv()
            add_into(block, chunk(here + step - ctx), rows)
            hop(block, step, True).start()

        @pl.when(jnp.logical_and(here > 0, here + ctx - step <= ctx - 1))
        def _():
            block = ups_land.at[step - 2]
            hop(block, step - 1, False).wait_recv()
            add_into(block, chunk(here + ctx - step), rows)
            hop(block, step, False).start()

        yield

    @pl.when(here < ctx - 1)
    def _():
        hop(downs_land.at[ctx - 2], ctx - 1, True).wait_recv()

    @pl.when(here > 0)
    def _():
        hop(ups_land.at[ctx - 2], ctx - 1, False).wait_recv()

    step = 32

    @pl.loop(0, rows // step)
    def _(index):
        at = pl.ds(pl.multiple_of(index * step, step), step)
        mine = held[pl.ds(pl.multiple_of(here * rows + index * step, step), step), :].astype(f32)
        down = downs_land[ctx - 2, at, :].astype(f32)
        up = ups_land[ctx - 2, at, :].astype(f32)
        out[at, :] = (
            mine + jnp.where(here < ctx - 1, down, 0.0) + jnp.where(here > 0, up, 0.0)
        )

    for step in range(1, ctx):

        @pl.when(here + step - ctx >= 0)
        def _():
            hop(chunk(0), step, True).wait_send()

        @pl.when(here + ctx - step <= ctx - 1)
        def _():
            hop(chunk(0), step, False).wait_send()


def reduce_kernel(ctx, dp, seqs, *refs):
    partial, normal, attended, hidden, cot, d_qkv, d_pre = ([ref] for ref in refs[:7])
    partial = partial[0]
    refs = refs[7:]
    sum_out, qkv_out, fc1_out, out_out, fc2_out = refs[:5]
    held, downs_land, ups_land, box, x_v, turned, y_v = refs[5:12]
    land_core, lands = refs[12:15], refs[15:18]
    send, recv, load_sem, x_sems, y_sems, own_sems = refs[18:]
    head_cols, ff_cols = D // ctx, FF // ctx
    parts = [
        [(out_out, 0, head_cols, 0), (fc2_out, head_cols, ff_cols, 0)],
        [(fc1_out, 0, ff_cols, 0)],
        [(qkv_out, part * head_cols, head_cols, part * D) for part in range(3)],
    ]
    ys = [[(attended, 0), (hidden, head_cols)], [(d_pre, 0)], [(d_qkv, 0)]]
    mine = lax.axis_index("dp")
    plan = []
    for arrays in (cot, normal, normal):
        for first in (flipped(mine, 1), mine):
            plan += [(arrays, owner_of(first, pattern)) for pattern in patterns_for(dp)]
    sems = Sems(send, recv)
    greet(ctx, dp)
    slabs = Slabs(plan, x_v, turned, x_sems)
    boxes = {"box": box, "sent": [None] * (dp // 2)}
    line = sum_chain(partial, sum_out, held, downs_land, ups_land, sems, load_sem, ctx)
    groups = [
        pooled_chain(
            ys[group], parts[group], slabs, boxes, land_core[group], lands[group],
            sems, y_v, y_sems, own_sems.at[group], ctx, dp,
        )
        for group in range(3)
    ]
    first, second, third = groups
    order = [line, first, first, first, second, first, line, second, second, first]
    order += [third, second, line, third, third, first, second, third, third, second, line, third, line]
    run_in(order, [line] + groups)
    for copy in boxes["sent"]:
        copy.wait_send()


def run_in(order, chains):
    ended = set()
    turn = 0
    while len(ended) < len(chains):
        chain = order[turn] if turn < len(order) else chains[(turn - len(order)) % len(chains)]
        turn += 1
        if id(chain) in ended:
            continue
        try:
            next(chain)
        except StopIteration:
            ended.add(id(chain))


def reduce_all(partial, normal, attended, hidden, cot, d_qkv, d_pre, seqs, ctx, dp):
    length = partial.shape[0]
    rows = length // ctx
    slab = D // dp
    copies = 2 * (ctx - 1) + 3 * (dp // 2 + dp - 2) + 6 * (ctx - 1)
    hbm = pl.BlockSpec(memory_space=pl.ANY)
    vmem = pl.BlockSpec(memory_space=pltpu.VMEM)
    head_cols, ff_cols = D // ctx, FF // ctx
    cols = [head_cols + ff_cols, ff_cols, 3 * head_cols]
    outs = pl.pallas_call(
        functools.partial(reduce_kernel, ctx, dp, seqs),
        in_specs=[hbm] * 7,
        out_specs=[vmem] + [hbm] * 4,
        out_shape=[jax.ShapeDtypeStruct((rows, partial.shape[1]), f32)]
        + [jax.ShapeDtypeStruct((slab // ctx, width), bf16) for width in (3 * D, FF, D, FF)],
        scratch_shapes=[pltpu.VMEM((length, partial.shape[1]), bf16)]
        + [pltpu.VMEM((ctx - 1, rows, partial.shape[1]), bf16)] * 2
        + [
            pltpu.VMEM((dp // 2, slab, cols[0]), bf16),
            pltpu.VMEM((2, seqs * length, slab), bf16),
            pltpu.VMEM((2, slab, seqs * length), bf16),
            pltpu.VMEM((seqs * length, cols[0]), bf16),
        ]
        + [pltpu.VMEM((dp // 2, slab, width), bf16) for width in cols]
        + [pltpu.VMEM((dp - 2, slab // 2, width), bf16) for width in cols]
        + [
            pltpu.SemaphoreType.DMA((copies,)),
            pltpu.SemaphoreType.DMA((copies,)),
            pltpu.SemaphoreType.DMA,
            pltpu.SemaphoreType.DMA((2, seqs)),
            pltpu.SemaphoreType.DMA((2 * seqs,)),
            pltpu.SemaphoreType.DMA((3,)),
        ],
        compiler_params=pltpu.CompilerParams(
            collective_id=2, has_side_effects=True, vmem_limit_bytes=GRANT
        ),
        cost_estimate=pl.CostEstimate(flops=150 * 10**9, bytes_accessed=10**8, transcendentals=0),
        name="reduce_all",
    )(partial, normal, attended, hidden, cot, d_qkv, d_pre)
    return outs[0], outs[1:]


def normalised(rows_in):
    row_mean = jnp.mean(rows_in, axis=-1, keepdims=True)
    centred = rows_in - row_mean
    variance = jnp.mean(centred * centred, axis=-1, keepdims=True)
    inv_std = lax.rsqrt(variance + 1e-05)
    return centred * inv_std, inv_std


def gelu_both(pre):
    return jax.vjp(lambda vals: jax.nn.gelu(vals, approximate=True), pre)


def finish_kernel(early, tok, cot, mix, others, last, rows, mixed, input_grad, sums):
    step = pl.program_id(0)
    vals = tok[...].astype(f32)
    mixed[...] = (vals + mix[...].astype(f32) + rows[1:2, :] + rows[2:3, :]).astype(bf16)
    normed, inv_std = normalised(vals)
    grad = jnp.where(step < early, others[...].astype(f32), last[...])

    @pl.when(step == 0)
    def _():
        sums[...] = jnp.zeros_like(sums)

    sums[0:1, :] += jnp.sum(grad * normed, axis=0, keepdims=True)
    sums[1:2, :] += jnp.sum(grad, axis=0, keepdims=True)
    scaled = grad * rows[0:1, :]
    input_grad[...] = cot[...].astype(f32) + inv_std * (
        scaled
        - jnp.mean(scaled, axis=-1, keepdims=True)
        - normed * jnp.mean(scaled * normed, axis=-1, keepdims=True)
    )


def finish(tok, cot, mix, others, last, rows):
    total, height = tok.shape[0], 128
    early = others.shape[0] // height
    block = pl.BlockSpec((height, D), lambda i: (i, 0))
    return pl.pallas_call(
        functools.partial(finish_kernel, early),
        grid=(total // height,),
        in_specs=[block] * 3
        + [
            pl.BlockSpec((height, D), lambda i: (jnp.minimum(i, early - 1), 0)),
            pl.BlockSpec((height, D), lambda i: (jnp.maximum(i - early, 0), 0)),
            pl.BlockSpec(rows.shape, lambda i: (0, 0)),
        ],
        out_specs=[block, block, pl.BlockSpec((8, D), lambda i: (0, 0))],
        out_shape=[
            jax.ShapeDtypeStruct((total, D), bf16),
            jax.ShapeDtypeStruct((total, D), f32),
            jax.ShapeDtypeStruct((8, D), f32),
        ],
        compiler_params=pltpu.CompilerParams(vmem_limit_bytes=GRANT),
        name="finish",
    )(tok, cot, mix, others, last, rows)


def per_device(
    tokens,
    cotangent,
    positions,
    wqkv_master,
    fc1_master,
    out_master,
    fc2_master,
    small_master,
    wqkv_first,
    wqkv_second,
    fc1_first,
    fc1_second,
    out_first,
    out_second,
    fc2_first,
    fc2_second,
    small_first,
    small_second,
):
    seqs, span = tokens.shape[0], tokens.shape[1]
    ctx, dp = lax.axis_size("ctx"), lax.axis_size("dp")
    ctx_index = lax.axis_index("ctx")
    length = span * ctx
    total_rows = seqs * length
    own_rows = wqkv_master.shape[0]
    head_cols, ff_cols = D // ctx, FF // ctx

    gate = lax.optimization_barrier
    small_low = jnp.pad(small_master.astype(bf16), ((0, 0), (0, LANES - small_master.shape[1])))
    blocks = [wqkv_master, fc1_master, out_master, fc2_master]
    blocks = [block.astype(bf16) for block in blocks] + [small_low]
    places = jnp.pad(positions.astype(f32).reshape(-1, LANES), ((0, 8 - seqs * span // LANES), (0, 0)))
    tok_all, place, (in_w, of_w, small_all) = gather_all(tokens, places, blocks, ctx, dp)
    qkv_w, fc1_w = in_w[:, : 3 * head_cols], in_w[:, 3 * head_cols :]
    params = small_all[:, :16].astype(f32)
    place = place[:, : seqs * span // LANES].reshape(ctx, seqs, span)
    place = jnp.transpose(place, (1, 0, 2)).reshape(total_rows)
    half_rot = ROT // 2
    exponent = jnp.arange(half_rot, dtype=f32) * (-2.0 / ROT)
    frequency = jnp.power(f32(10000.0), exponent)
    angles = frequency[:, None] * place[None, :]
    cos_s, sin_s = jnp.cos(angles), jnp.sin(angles)
    none = jnp.zeros_like(cos_s)
    rest = jnp.zeros((HD - ROT, total_rows), f32)
    tables = [
        jnp.concatenate([cos_s, cos_s, rest + 1.0] * 2, axis=0),
        jnp.concatenate([-sin_s, none, rest] * 2, axis=0),
        jnp.concatenate([none, sin_s, rest] * 2, axis=0),
    ]

    def my_part(values, cols):
        return lax.dynamic_slice_in_dim(values, ctx_index * cols, cols, values.ndim - 1)

    qkv_bias = my_part(params[:, 2:5].T, head_cols)
    fc1_bias = my_part(params[:, 6:10].T.reshape(FF), ff_cols)
    gain, shift = params[:, 0], params[:, 1]
    def scattered(partial):
        return lax.psum_scatter(partial, "ctx", scatter_dimension=1, tiled=True)

    cot, tok_all = gate((cotangent, tok_all))
    cot_all = lax.all_gather(cot, "ctx", axis=1, tiled=True).reshape(total_rows, D)
    normal_low = normalised(tok_all.reshape(total_rows, D).astype(f32))[0]
    normal_low = (normal_low * gain + shift).astype(bf16)
    projected = mm(normal_low, in_w[:, : 3 * head_cols], (1, 0))
    query, key, value, attended, log_total = attend(projected, qkv_bias, tables, seqs)
    pre = mm(normal_low, in_w[:, 3 * head_cols :], (1, 0)) + fc1_bias
    hidden = gelu_both(pre)[0].astype(bf16)
    branch = mm(jnp.concatenate([attended, hidden], axis=1), of_w, (1, 1)).astype(bf16)
    sum_out = jnp.sum(cotangent.astype(f32), axis=(0, 1))[None]
    pre, hidden, branch, sum_out = gate((pre, hidden, branch, sum_out))
    pre, hidden, branch, cot_all = gate((pre, hidden, branch, cot_all))
    mix = scattered(branch.reshape(seqs, length, D))
    back = mm(cot_all, of_w[:, :head_cols], (1, 0)).astype(bf16)
    grad_hidden = mm(cot_all, of_w[:, head_cols:], (1, 0))
    d_pre = gelu_both(pre)[1](grad_hidden)[0].astype(bf16)
    d_qkv = attend_back(query, key, value, back, log_total, tables, seqs)
    def spread(sums, count, cols):
        whole = jnp.zeros((count, ctx * cols), f32)
        return lax.dynamic_update_slice_in_dim(whole, sums.reshape(count, cols), ctx_index * cols, 1)

    sum_qkv, sum_pre = (jnp.sum(part, axis=0, dtype=f32) for part in (d_qkv, d_pre))
    sum_pre = spread(sum_pre, 1, ff_cols).reshape(4, D)
    small_terms = jnp.concatenate(
        [spread(sum_qkv, 3, head_cols), sum_out, sum_pre, sum_out], axis=0
    )

    def normal_back(first, last):
        both = jnp.concatenate([d_qkv[first:last], d_pre[first:last]], axis=1)
        return mm(both, in_w, (1, 1)).astype(bf16)

    d_first, d_last = normal_back(0, total_rows - length), normal_back(total_rows - length, total_rows)
    d_qkv, d_pre, d_first, d_last, small_terms = gate((d_qkv, d_pre, d_first, d_last, small_terms))
    d_qkv, d_pre, d_first, d_last, mix = gate((d_qkv, d_pre, d_first, d_last, mix))
    others = scattered(d_first.reshape(seqs - 1, length, D))
    last, grads = reduce_all(
        d_last, normal_low, attended, hidden, cot_all, d_qkv, d_pre, seqs, ctx, dp
    )
    mixed, input_grad, sums = finish(
        tokens.reshape(-1, D), cotangent.reshape(-1, D), mix.reshape(-1, D), others.reshape(-1, D),
        last, jnp.stack([gain, params[:, 5], params[:, 10]]),
    )
    mixed, input_grad = mixed.reshape(tokens.shape), input_grad.reshape(tokens.shape)
    small_terms = jnp.concatenate([sums[:2], small_terms], axis=0)
    small_sent = jnp.transpose(small_terms.reshape(11, ctx * dp, own_rows), (1, 0, 2))
    small_sent, grads = gate((small_sent, grads))
    small_got = lax.all_to_all(small_sent.reshape(ctx * dp, 1, 11 * own_rows), EVERY, 0, 0, tiled=True)
    small_grad = jnp.sum(small_got, axis=(0, 1)).reshape(11, own_rows).T

    qkv_grad, fc1_grad, out_grad, fc2_grad = (grad.astype(f32) for grad in grads)
    qkv_new = adamw(wqkv_master, wqkv_first, wqkv_second, qkv_grad, 0.04, 0.1)
    fc1_new = adamw(fc1_master, fc1_first, fc1_second, fc1_grad, 0.04, 0.1)
    out_new = adamw(out_master, out_first, out_second, out_grad, 0.4, 0.1)
    fc2_new = adamw(fc2_master, fc2_first, fc2_second, fc2_grad, 0.02, 0.1)
    small_new = adamw(small_master, small_first, small_second, small_grad, 0.3, 0.0)
    return (mixed, input_grad, *qkv_new, *fc1_new, *out_new, *fc2_new, *small_new)


def solution(mesh):
    split = P("dp", "ctx", None)
    rows = P(("dp", "ctx"), None)
    return jax.shard_map(
        per_device,
        mesh=mesh,
        in_specs=(split, split, P("dp", "ctx")) + (rows,) * 15,
        out_specs=(split, split) + (rows,) * 15,
        check_vma=False,
    )
```

```python
import functools

import jax
import jax.numpy as jnp
from jax import lax
from jax.experimental import pallas as pl
from jax.experimental.pallas import tpu as pltpu
from jax.sharding import PartitionSpec as P

D = 2048
H = 32
HD = 64
ROT = 32
FF = 8192
STEP = 10
LANES = 128
BLOCK = 256

beta_one = 0.9
beta_two = 0.95
epsilon = 1e-08

f32 = jnp.float32
bf16 = jnp.bfloat16
EVERY = ("dp", "ctx")
GRANT = 58 * 1024 * 1024


def adamw(weight, first_old, second_old, gradient, step_rate, decay):
    first_new = beta_one * first_old + (1.0 - beta_one) * gradient
    second_new = beta_two * second_old + (1.0 - beta_two) * gradient * gradient
    first_hat = first_new / (1.0 - beta_one**STEP)
    second_hat = second_new / (1.0 - beta_two**STEP)
    weight_new = weight - step_rate * (
        first_hat / (jnp.sqrt(second_hat) + epsilon) + decay * weight
    )
    return (first_new, second_new, weight_new)


def mm(left, right, dims):
    return lax.dot_general(left, right, ((dims[:1], dims[1:]), ((), ())), preferred_element_type=f32)


def rotated(vals, cos_t, lead, trail):
    return (
        vals * cos_t + pltpu.roll(vals, LANES - 16, 1) * lead + pltpu.roll(vals, 16, 1) * trail
    )


def unrotated(vals, cos_t, lead, trail):
    return (
        vals * cos_t - pltpu.roll(vals, LANES - 16, 1) * lead - pltpu.roll(vals, 16, 1) * trail
    )


def attend_kernel(
    q_in, k_in, v_in, bias, cos_ref, lead_ref, trail_ref, q_out, k_out, v_out, o_out, log_out
):
    rows = q_in.shape[0]
    cos_t, lead, trail = cos_ref[...].T, lead_ref[...].T, trail_ref[...].T
    scale = HD ** (-0.5)
    query = rotated(q_in[...] + bias[0:1, :], cos_t, lead, trail).astype(bf16)
    key = rotated(k_in[...] + bias[1:2, :], cos_t, lead, trail).astype(bf16)
    value = (v_in[...] + bias[2:3, :]).astype(bf16)
    query = query * jnp.asarray(scale, bf16)
    q_out[...] = query
    k_out[...] = key
    v_out[...] = value
    lane = lax.broadcasted_iota(jnp.int32, (BLOCK, LANES), 1)
    on_diagonal = lax.broadcasted_iota(jnp.int32, (BLOCK, BLOCK), 1) <= lax.broadcasted_iota(
        jnp.int32, (BLOCK, BLOCK), 0
    )
    for step in range(rows // BLOCK):
        start = step * BLOCK
        stop = start + BLOCK
        out = None
        for head in range(2):
            mine = (lane < HD) if head == 0 else (lane >= HD)
            q_head = jnp.where(mine, query[start:stop], jnp.zeros((), bf16))
            last = jnp.where(on_diagonal, mm(q_head, key[start:stop], (1, 1)), -1e30)
            parts = [last]
            if start:
                parts = [mm(q_head, key[:start], (1, 1)), last]
            best = functools.reduce(
                jnp.maximum, [jnp.max(part, axis=1, keepdims=True) for part in parts]
            )
            parts = [jnp.exp(part - best) for part in parts]
            total = sum(jnp.sum(part, axis=1, keepdims=True) for part in parts)
            log_out[0, head, start:stop] = (best + jnp.log(total))[:, 0]
            mixed = mm(parts[-1].astype(bf16), value[start:stop], (1, 0))
            if start:
                mixed = mixed + mm(parts[0].astype(bf16), value[:start], (1, 0))
            mixed = mixed / total
            out = mixed if head == 0 else jnp.where(mine, mixed, out)
        o_out[start:stop, :] = out.astype(bf16)


def attend_back_kernel(
    q_in, k_in, v_in, g_in, log_in, cos_ref, lead_ref, trail_ref, d_out, dq_sum, dk_sum, dv_sum
):
    rows = q_in.shape[0]
    scale = HD ** (-0.5)
    lane = lax.broadcasted_iota(jnp.int32, (BLOCK, LANES), 1)
    on_diagonal = lax.broadcasted_iota(jnp.int32, (BLOCK, BLOCK), 0) <= lax.broadcasted_iota(
        jnp.int32, (BLOCK, BLOCK), 1
    )
    dk_sum[...] = jnp.zeros_like(dk_sum)
    dv_sum[...] = jnp.zeros_like(dv_sum)
    key_all = k_in[...]
    value_all = v_in[...]
    zero = jnp.zeros((), bf16)
    for step in range(rows // BLOCK):
        start = step * BLOCK
        stop = start + BLOCK
        d_query = None
        for head in range(2):
            mine = (lane < HD) if head == 0 else (lane >= HD)
            q_head = jnp.where(mine, q_in[start:stop], zero)
            g_head = jnp.where(mine, g_in[start:stop], zero)
            log_row = log_in[0, head : head + 1, start:stop]
            last = jnp.where(
                on_diagonal, jnp.exp(mm(key_all[start:stop], q_head, (1, 1)) - log_row), 0.0
            )
            probs = [(start, stop, last)]
            if start:
                probs.append((0, start, jnp.exp(mm(key_all[:start], q_head, (1, 1)) - log_row)))
            grads = [mm(value_all[lo:hi], g_head, (1, 1)) for lo, hi, _ in probs]
            delta = sum(
                jnp.sum(prob * grad, axis=0, keepdims=True)
                for (_, _, prob), grad in zip(probs, grads)
            )
            part = None
            for (lo, hi, prob), grad in zip(probs, grads):
                d_score = (prob * (grad - delta)).astype(bf16)
                dv_sum[lo:hi, :] += mm(prob.astype(bf16), g_head, (1, 0))
                dk_sum[lo:hi, :] += mm(d_score, q_head, (1, 0))
                added = mm(d_score, key_all[lo:hi], (0, 0))
                part = added if part is None else part + added
            d_query = part if head == 0 else jnp.where(mine, part, d_query)
        dq_sum[start:stop, :] = d_query * scale
    cos_t, lead, trail = cos_ref[...].T, lead_ref[...].T, trail_ref[...].T
    width = d_out.shape[1] // 3

    def put(which, vals):
        first = pl.multiple_of(which * width + pl.program_id(1) * LANES, LANES)
        d_out[:, pl.ds(first, LANES)] = vals.astype(bf16)

    put(0, unrotated(dq_sum[...], cos_t, lead, trail))
    put(1, unrotated(dk_sum[...], cos_t, lead, trail))
    put(2, dv_sum[...])


def attend(mixed_qkv, bias, tables, seqs):
    rows, width = mixed_qkv.shape[0] // seqs, mixed_qkv.shape[1] // 3
    pairs = width // LANES

    def part(which):
        return pl.BlockSpec((rows, LANES), lambda s, p: (s, which * pairs + p))

    block = pl.BlockSpec((rows, LANES), lambda s, p: (s, p))
    table = pl.BlockSpec((LANES, rows), lambda s, p: (0, s))
    low = jax.ShapeDtypeStruct((seqs * rows, width), bf16)
    return pl.pallas_call(
        attend_kernel,
        grid=(seqs, pairs),
        in_specs=[part(0), part(1), part(2), pl.BlockSpec((3, LANES), lambda s, p: (0, p))]
        + [table] * 3,
        out_specs=[block] * 4 + [pl.BlockSpec((1, 2, rows), lambda s, p: (s * pairs + p, 0, 0))],
        out_shape=[low] * 4 + [jax.ShapeDtypeStruct((seqs * pairs, 2, rows), f32)],
        compiler_params=pltpu.CompilerParams(vmem_limit_bytes=GRANT),
        cost_estimate=pl.CostEstimate(flops=20 * 10**9, bytes_accessed=10**7, transcendentals=0),
        name="attend",
    )(mixed_qkv, mixed_qkv, mixed_qkv, bias, *tables)


def attend_back(query, key, value, back, log_total, tables, seqs):
    rows, width = query.shape[0] // seqs, query.shape[1]
    pairs = width // LANES
    block = pl.BlockSpec((rows, LANES), lambda s, p: (s, p))
    table = pl.BlockSpec((LANES, rows), lambda s, p: (0, s))
    return pl.pallas_call(
        attend_back_kernel,
        grid=(seqs, pairs),
        in_specs=[block] * 4
        + [pl.BlockSpec((1, 2, rows), lambda s, p: (s * pairs + p, 0, 0))]
        + [table] * 3,
        out_specs=pl.BlockSpec((rows, 3 * width), lambda s, p: (s, 0)),
        out_shape=jax.ShapeDtypeStruct((seqs * rows, 3 * width), bf16),
        scratch_shapes=[pltpu.VMEM((rows, LANES), f32)] * 3,
        compiler_params=pltpu.CompilerParams(vmem_limit_bytes=GRANT),
        cost_estimate=pl.CostEstimate(flops=30 * 10**9, bytes_accessed=10**7, transcendentals=0),
        name="attend_back",
    )(query, key, value, back, log_total, *tables)


def bits_of(count):
    bits = []
    bit = 1
    while bit < count:
        bits.append(bit)
        bit *= 2
    return bits


def flipped(index, bit):
    return index + bit * (1 - 2 * ((index // bit) % 2))


def run_chains(chains):
    while chains:
        left = []
        for chain in chains:
            try:
                next(chain)
                left.append(chain)
            except StopIteration:
                pass
        chains = left


class Sems:
    def __init__(self, send, recv):
        self.send, self.recv, self.used = send, recv, 0

    def take(self):
        self.used += 1
        return self.send.at[self.used - 1], self.recv.at[self.used - 1]


def remote(src, dst, sems, target):
    return pltpu.make_async_remote_copy(
        src_ref=src,
        dst_ref=dst,
        send_sem=sems[0],
        recv_sem=sems[1],
        device_id=target,
        device_id_type=pl.DeviceIdType.MESH,
    )


def greet(ctx, dp):
    here, mine = lax.axis_index("ctx"), lax.axis_index("dp")
    barrier = pltpu.get_barrier_semaphore()
    targets = [{"ctx": lax.rem(here + by, ctx)} for by in range(1, ctx)]
    targets += [{"dp": flipped(mine, bit)} for bit in bits_of(dp)]
    for target in targets:
        pl.semaphore_signal(barrier, inc=1, device_id=target, device_id_type=pl.DeviceIdType.MESH)
    pl.semaphore_wait(barrier, len(targets))


def line_chain(src, out, sems, ctx):
    here = lax.axis_index("ctx")
    ups = [sems.take() for _ in range(1, ctx)]
    downs = [sems.take() for _ in range(1, ctx)]

    def hop(block, slot, step, going):
        by = 1 if going is ups else -1
        return remote(block, out.at[slot], going[step], {"ctx": here + by})

    @pl.when(here < ctx - 1)
    def _():
        hop(src, here, 0, ups).start()

    @pl.when(here > 0)
    def _():
        hop(src, here, 0, downs).start()

    yield
    for step in range(1, ctx):
        for going, sign in ((ups, -1), (downs, 1)):
            slot = here + sign * step
            inside = (slot >= 0) if sign < 0 else (slot < ctx)
            more = (here < ctx - 1) if sign < 0 else (here > 0)
            if step < ctx - 1:

                @pl.when(jnp.logical_and(inside, more))
                def _():
                    hop(out.at[slot], slot, step - 1, going).wait_recv()
                    hop(out.at[slot], slot, step, going).start()

                @pl.when(jnp.logical_and(inside, jnp.logical_not(more)))
                def _():
                    hop(out.at[slot], slot, step - 1, going).wait_recv()

            else:

                @pl.when(inside)
                def _():
                    hop(out.at[slot], slot, step - 1, going).wait_recv()

        yield

    for step in range(ctx - 1):
        for going, sign in ((ups, -1), (downs, 1)):
            slot = here + sign * step
            inside = (slot >= 0) if sign < 0 else (slot < ctx)
            more = (here < ctx - 1) if sign < 0 else (here > 0)

            @pl.when(jnp.logical_and(inside, more))
            def _():
                hop(out.at[slot], slot, step, going).wait_send()


def weight_chain(cuts, out, sems, own_sem, ctx, dp):
    here, mine = lax.axis_index("ctx"), lax.axis_index("dp")
    rows = cuts[0][0].shape[0]
    slab = rows * ctx
    half = slab // 2

    def piece(owner, cut):
        at = pl.ds(pl.multiple_of((mine * ctx + owner) * rows, rows), rows)
        return out.at[at, pl.ds(cut[3], cut[1])]

    def taken(peer, cut):
        block, width, first, _ = cut
        if first is None:
            return block
        return block.at[:, pl.ds(pl.multiple_of(first + peer * width, LANES), width)]

    def part(owner, which):
        return out.at[pl.ds(pl.multiple_of(owner * slab + which * half, half), half)]

    trades, own = [], []
    for by in range(1, ctx):
        peer = lax.rem(here + by, ctx)
        source = lax.rem(here + ctx - by, ctx)
        for cut in cuts:
            sem = sems.take()
            copy = remote(taken(peer, cut), piece(here, cut), sem, {"ctx": peer})
            copy.start()
            trades.append((copy, remote(taken(peer, cut), piece(source, cut), sem, {"ctx": peer})))
    for index, cut in enumerate(cuts):
        copy = pltpu.make_async_copy(taken(here, cut), piece(here, cut), own_sem.at[index])
        copy.start()
        own.append(copy)
    yield
    for _, arrival in trades:
        arrival.wait_recv()
    for copy in own:
        copy.wait()
    far = bits_of(dp)[1:]
    orders = [far + [1], far[::-1] + [1]]
    held = [[mine], [mine]]
    sent = []
    for stage in range(len(far) + 1):
        arrivals = []
        for which in range(2):
            bit = orders[which][stage]
            for owner in list(held[which]):
                sem = sems.take()
                copy = remote(part(owner, which), part(owner, which), sem, {"dp": flipped(mine, bit)})
                copy.start()
                sent.append(copy)
                coming = flipped(owner, bit)
                arrivals.append(remote(part(coming, which), part(coming, which), sem, {"dp": flipped(mine, bit)}))
                held[which].append(coming)
        yield
        for arrival in arrivals:
            arrival.wait_recv()
    for copy, _ in trades:
        copy.wait_send()
    for copy in sent:
        copy.wait_send()


def cuts_of(blocks, ctx):
    qkv, fc1, out, fc2, small = blocks
    head_cols, ff_cols = D // ctx, FF // ctx
    first = [(qkv, head_cols, part * D, part * head_cols) for part in range(3)]
    first.append((fc1, ff_cols, 0, 3 * head_cols))
    return [first, [(out, head_cols, 0, 0), (fc2, ff_cols, 0, head_cols)], [(small, LANES, None, 0)]]


def rounded_into(target, source):
    @pl.loop(0, source.shape[0] // 16)
    def _(index):
        at = pl.ds(pl.multiple_of(index * 16, 16), 16)
        target[at, :] = source[at, :].astype(bf16)


def gather_kernel(ctx, dp, seqs, *refs):
    tokens, places, masters, small = refs[0], refs[1], refs[2:6], refs[6]
    tok_out, place_out, outs = refs[7], refs[8], refs[9:12]
    wide, low = refs[12:16], refs[16:20]
    send, recv, own_sems, tok_sems, load_sems = refs[20:]
    here = lax.axis_index("ctx")
    sems = Sems(send, recv)
    loads = [
        pltpu.make_async_copy(masters[index], wide[index], load_sems.at[index]) for index in range(4)
    ]
    for load in loads:
        load.start()
    greet(ctx, dp)
    weights = []
    for group, cuts in enumerate(cuts_of([*low, small], ctx)):
        for index in ((0, 1), (2, 3), ())[group]:
            loads[index].wait()
            rounded_into(low[index], wide[index])
        weights.append(weight_chain(cuts, outs[group], sems, own_sems.at[group], ctx, dp))
        next(weights[group])
    place = line_chain(places, place_out, sems, ctx)
    lines = [line_chain(tokens.at[seq], tok_out.at[seq], sems, ctx) for seq in range(seqs)]
    for chain in (place, *lines):
        next(chain)
    chains = [place, weights[0], lines[0], weights[1], *lines[1:], weights[2]]
    local = [
        pltpu.make_async_copy(tokens.at[seq], tok_out.at[seq, here], tok_sems.at[seq])
        for seq in range(seqs)
    ]
    local.append(pltpu.make_async_copy(places, place_out.at[here], tok_sems.at[seqs]))
    for copy in local:
        copy.start()
    run_chains(chains)
    for copy in local:
        copy.wait()


def gather_all(tokens, places, blocks, ctx, dp):
    seqs, span = tokens.shape[0], tokens.shape[1]
    rows = blocks[0].shape[0] * ctx * dp
    head_cols, ff_cols = D // ctx, FF // ctx
    copies = (seqs + 1) * 2 * (ctx - 1) + 7 * (ctx - 1) + 3 * 2 * (dp - 1)
    hbm = pl.BlockSpec(memory_space=pl.ANY)
    outs = pl.pallas_call(
        functools.partial(gather_kernel, ctx, dp, seqs),
        in_specs=[hbm] * 7,
        out_specs=[hbm] * 5,
        out_shape=[
            jax.ShapeDtypeStruct((seqs, ctx, span, D), bf16),
            jax.ShapeDtypeStruct((ctx,) + places.shape, f32),
            jax.ShapeDtypeStruct((rows, 3 * head_cols + ff_cols), bf16),
            jax.ShapeDtypeStruct((rows, head_cols + ff_cols), bf16),
            jax.ShapeDtypeStruct((rows, LANES), bf16),
        ],
        scratch_shapes=[
            *[pltpu.VMEM(block.shape, f32) for block in blocks[:4]],
            *[pltpu.VMEM(block.shape, bf16) for block in blocks[:4]],
            pltpu.SemaphoreType.DMA((copies,)),
            pltpu.SemaphoreType.DMA((copies,)),
            pltpu.SemaphoreType.DMA((3, 4)),
            pltpu.SemaphoreType.DMA((seqs + 1,)),
            pltpu.SemaphoreType.DMA((4,)),
        ],
        compiler_params=pltpu.CompilerParams(
            collective_id=1, has_side_effects=True, vmem_limit_bytes=GRANT
        ),
        name="gather_all",
    )(tokens, places, *blocks)
    return outs[0], outs[1], outs[2:]


def add_into(target, other, rows):
    step = 32

    @pl.loop(0, rows // step)
    def _(index):
        here = pl.ds(pl.multiple_of(index * step, step), step)
        target[here, :] = target[here, :] + other[here, :]


def without(pattern, bit):
    return tuple(item for item in pattern if item != bit)


def patterns_of(bits):
    found = [()]
    for bit in bits:
        found += [pattern + (bit,) for pattern in found]
    return found


def owner_of(mine, pattern):
    for bit in pattern:
        mine = flipped(mine, bit)
    return mine


def patterns_for(dp):
    return sorted(patterns_of(bits_of(dp)[1:]), key=len, reverse=True)


class Slabs:
    def __init__(self, plan, x_v, turned, x_sems):
        self.plan, self.x_v, self.turned, self.x_sems = plan, x_v, turned, x_sems
        self.next = 0
        for index in (0, 1):
            self.start(index)
        self.wait(0)
        turned[0] = x_v[0].T

    def copies(self, index):
        arrays, owner = self.plan[index]
        slab = self.turned.shape[1]
        at = pl.ds(pl.multiple_of(owner * slab, LANES), slab)
        found = []
        for seq, array in enumerate(arrays):
            length = array.shape[0]
            found.append(
                pltpu.make_async_copy(
                    array.at[:, at],
                    self.x_v.at[index % 2, pl.ds(seq * length, length)],
                    self.x_sems.at[index % 2, seq],
                )
            )
        return found

    def start(self, index):
        for copy in self.copies(index):
            copy.start()

    def wait(self, index):
        for copy in self.copies(index):
            copy.wait()

    def multiply(self, y_v, cols, store):
        index = self.next
        self.next += 1
        more = index + 1 < len(self.plan)
        if index + 2 < len(self.plan):
            self.start(index + 2)
        if more:
            self.wait(index + 1)
        tile, rows = cols // 2, self.turned.shape[2] // 2

        @pl.loop(0, 2)
        def _(part):
            at = pl.ds(pl.multiple_of(part * tile, LANES), tile)
            if more:
                some = pl.ds(pl.multiple_of(part * rows, rows), rows)
                self.turned[(index + 1) % 2, :, some] = self.x_v[(index + 1) % 2, some, :].T
            store(at, mm(self.turned[index % 2], y_v[:, at], (1, 0)))


def pooled_chain(ys, parts, slabs, boxes, land_core, lands, sems, y_v, y_sems, own_sem, ctx, dp):
    here, mine = lax.axis_index("ctx"), lax.axis_index("dp")
    slab, cols = land_core.shape[1:]
    rows, half = slab // ctx, slab // 2
    far = bits_of(dp)[1:]
    patterns = patterns_for(dp)
    partner = flipped(mine, 1)
    loads = []
    for arrays, first in ys:
        for seq, array in enumerate(arrays):
            length, width = array.shape
            loads.append(
                pltpu.make_async_copy(
                    array,
                    y_v.at[pl.ds(seq * length, length), pl.ds(first, width)],
                    y_sems.at[len(loads)],
                )
            )
    for load in loads:
        load.start()
    for load in loads:
        load.wait()
    sent = []
    for index in range(len(patterns)):
        if boxes["sent"][index] is not None:
            boxes["sent"][index].wait_send()
        box = boxes["box"].at[index, :, pl.ds(0, cols)]

        def store(at, vals, index=index):
            boxes["box"][index, :, at] = vals.astype(bf16)

        slabs.multiply(y_v, cols, store)
        copy = remote(box, land_core.at[index], sems.take(), {"dp": partner})
        copy.start()
        boxes["sent"][index] = copy
        sent.append(copy)
    yield
    arrived, sent = sent, []
    held, coming = [{}, {}], [[], []]
    orders = [far, far[::-1]]
    used = 0

    def pass_on(which, stage, pattern, block):
        nonlocal used
        bit = orders[which][stage]
        copy = remote(block, lands.at[used], sems.take(), {"dp": flipped(mine, bit)})
        copy.start()
        sent.append(copy)
        coming[which].append((copy, lands.at[used], without(pattern, bit)))
        used += 1

    for index, pattern in enumerate(patterns):
        arrived[index].wait_recv()

        def store(at, vals, index=index):
            land_core[index, :, at] = (vals + land_core[index, :, at].astype(f32)).astype(bf16)

        slabs.multiply(y_v, cols, store)
        for which in range(2):
            block = land_core.at[index, pl.ds(which * half, half)]
            if orders[which][0] in pattern:
                pass_on(which, 0, pattern, block)
            else:
                held[which][pattern] = block
        if index == len(patterns) // 2 - 1:
            yield
    for stage in range(len(far)):
        yield
        for which in range(2):
            kept, arrivals = {}, coming[which]
            coming[which] = []
            for copy, landing, pattern in arrivals:
                copy.wait_recv()
                add_into(landing, held[which][pattern], half)
                if stage + 1 < len(far) and orders[which][stage + 1] in pattern:
                    pass_on(which, stage + 1, pattern, landing)
                else:
                    kept[pattern] = landing
            held[which] = kept
    final = [held[0][()], held[1][()]]
    trades = []

    def piece(which, peer, part):
        first = pl.multiple_of(peer * rows - which * half, rows)
        return final[which].at[pl.ds(first, rows), pl.ds(part[1], part[2])]

    def target(source, part):
        first = pl.multiple_of(part[3] + source * part[2], LANES)
        return part[0].at[:, pl.ds(first, part[2])]

    for by in range(1, ctx):
        peer = lax.rem(here + by, ctx)
        source = lax.rem(here + ctx - by, ctx)
        for part in parts:
            sem = sems.take()
            for which in range(2):

                @pl.when(peer // (ctx // 2) == which)
                def _():
                    remote(piece(which, peer, part), target(here, part), sem, {"ctx": peer}).start()

            trades.append((sem, peer, source, part))
    for which in range(2):

        @pl.when(here // (ctx // 2) == which)
        def _():
            for part in parts:
                copy = pltpu.make_async_copy(piece(which, here, part), target(here, part), own_sem)
                copy.start()
                copy.wait()

    yield
    for sem, peer, source, part in trades:
        some = final[0].at[pl.ds(0, rows), pl.ds(part[1], part[2])]
        remote(some, target(source, part), sem, {"ctx": peer}).wait_recv()
    for sem, peer, source, part in trades:
        some = final[0].at[pl.ds(0, rows), pl.ds(part[1], part[2])]
        remote(some, target(source, part), sem, {"ctx": peer}).wait_send()
    for copy in sent:
        copy.wait_send()


def sum_chain(partial, out, held, downs_land, ups_land, sems, load_sem, ctx):
    here = lax.axis_index("ctx")
    rows = held.shape[0] // ctx
    load = pltpu.make_async_copy(partial, held, load_sem)
    load.start()
    down_sems = [sems.take() for _ in range(1, ctx)]
    up_sems = [sems.take() for _ in range(1, ctx)]

    def chunk(index):
        return held.at[pl.ds(pl.multiple_of(index * rows, rows), rows)]

    def hop(block, step, down):
        lands, going = (downs_land, down_sems) if down else (ups_land, up_sems)
        by = -1 if down else 1
        return remote(block, lands.at[step - 1], going[step - 1], {"ctx": here + by})

    load.wait()

    @pl.when(here == ctx - 1)
    def _():
        for step in range(1, ctx):
            hop(chunk(step - 1), step, True).start()

    @pl.when(here == 0)
    def _():
        for step in range(1, ctx):
            hop(chunk(ctx - step), step, False).start()

    yield
    for step in range(2, ctx):

        @pl.when(jnp.logical_and(here < ctx - 1, here + step - ctx >= 0))
        def _():
            block = downs_land.at[step - 2]
            hop(block, step - 1, True).wait_recv()
            add_into(block, chunk(here + step - ctx), rows)
            hop(block, step, True).start()

        @pl.when(jnp.logical_and(here > 0, here + ctx - step <= ctx - 1))
        def _():
            block = ups_land.at[step - 2]
            hop(block, step - 1, False).wait_recv()
            add_into(block, chunk(here + ctx - step), rows)
            hop(block, step, False).start()

        yield

    @pl.when(here < ctx - 1)
    def _():
        hop(downs_land.at[ctx - 2], ctx - 1, True).wait_recv()

    @pl.when(here > 0)
    def _():
        hop(ups_land.at[ctx - 2], ctx - 1, False).wait_recv()

    step = 32

    @pl.loop(0, rows // step)
    def _(index):
        at = pl.ds(pl.multiple_of(index * step, step), step)
        mine = held[pl.ds(pl.multiple_of(here * rows + index * step, step), step), :].astype(f32)
        down = downs_land[ctx - 2, at, :].astype(f32)
        up = ups_land[ctx - 2, at, :].astype(f32)
        out[at, :] = (
            mine + jnp.where(here < ctx - 1, down, 0.0) + jnp.where(here > 0, up, 0.0)
        )

    for step in range(1, ctx):

        @pl.when(here + step - ctx >= 0)
        def _():
            hop(chunk(0), step, True).wait_send()

        @pl.when(here + ctx - step <= ctx - 1)
        def _():
            hop(chunk(0), step, False).wait_send()


def reduce_kernel(ctx, dp, seqs, *refs):
    partial, normal, attended, hidden, cot, d_qkv, d_pre = ([ref] for ref in refs[:7])
    partial = partial[0]
    refs = refs[7:]
    sum_out, qkv_out, fc1_out, out_out, fc2_out = refs[:5]
    held, downs_land, ups_land, box, x_v, turned, y_v = refs[5:12]
    land_core, lands = refs[12:15], refs[15:18]
    send, recv, load_sem, x_sems, y_sems, own_sems = refs[18:]
    head_cols, ff_cols = D // ctx, FF // ctx
    parts = [
        [(out_out, 0, head_cols, 0), (fc2_out, head_cols, ff_cols, 0)],
        [(fc1_out, 0, ff_cols, 0)],
        [(qkv_out, part * head_cols, head_cols, part * D) for part in range(3)],
    ]
    ys = [[(attended, 0), (hidden, head_cols)], [(d_pre, 0)], [(d_qkv, 0)]]
    mine = lax.axis_index("dp")
    plan = []
    for arrays in (cot, normal, normal):
        for first in (flipped(mine, 1), mine):
            plan += [(arrays, owner_of(first, pattern)) for pattern in patterns_for(dp)]
    sems = Sems(send, recv)
    greet(ctx, dp)
    slabs = Slabs(plan, x_v, turned, x_sems)
    boxes = {"box": box, "sent": [None] * (dp // 2)}
    line = sum_chain(partial, sum_out, held, downs_land, ups_land, sems, load_sem, ctx)
    groups = [
        pooled_chain(
            ys[group], parts[group], slabs, boxes, land_core[group], lands[group],
            sems, y_v, y_sems, own_sems.at[group], ctx, dp,
        )
        for group in range(3)
    ]
    first, second, third = groups
    order = [line, first, first, first, second, first, line, second, second, first]
    order += [third, second, line, third, third, first, second, third, third, second, line, third, line]
    run_in(order, [line] + groups)
    for copy in boxes["sent"]:
        copy.wait_send()


def run_in(order, chains):
    ended = set()
    turn = 0
    while len(ended) < len(chains):
        chain = order[turn] if turn < len(order) else chains[(turn - len(order)) % len(chains)]
        turn += 1
        if id(chain) in ended:
            continue
        try:
            next(chain)
        except StopIteration:
            ended.add(id(chain))


def reduce_all(partial, normal, attended, hidden, cot, d_qkv, d_pre, seqs, ctx, dp):
    length = partial.shape[0]
    rows = length // ctx
    slab = D // dp
    copies = 2 * (ctx - 1) + 3 * (dp // 2 + dp - 2) + 6 * (ctx - 1)
    hbm = pl.BlockSpec(memory_space=pl.ANY)
    vmem = pl.BlockSpec(memory_space=pltpu.VMEM)
    head_cols, ff_cols = D // ctx, FF // ctx
    cols = [head_cols + ff_cols, ff_cols, 3 * head_cols]
    outs = pl.pallas_call(
        functools.partial(reduce_kernel, ctx, dp, seqs),
        in_specs=[hbm] * 7,
        out_specs=[vmem] + [hbm] * 4,
        out_shape=[jax.ShapeDtypeStruct((rows, partial.shape[1]), f32)]
        + [jax.ShapeDtypeStruct((slab // ctx, width), bf16) for width in (3 * D, FF, D, FF)],
        scratch_shapes=[pltpu.VMEM((length, partial.shape[1]), bf16)]
        + [pltpu.VMEM((ctx - 1, rows, partial.shape[1]), bf16)] * 2
        + [
            pltpu.VMEM((dp // 2, slab, cols[0]), bf16),
            pltpu.VMEM((2, seqs * length, slab), bf16),
            pltpu.VMEM((2, slab, seqs * length), bf16),
            pltpu.VMEM((seqs * length, cols[0]), bf16),
        ]
        + [pltpu.VMEM((dp // 2, slab, width), bf16) for width in cols]
        + [pltpu.VMEM((dp - 2, slab // 2, width), bf16) for width in cols]
        + [
            pltpu.SemaphoreType.DMA((copies,)),
            pltpu.SemaphoreType.DMA((copies,)),
            pltpu.SemaphoreType.DMA,
            pltpu.SemaphoreType.DMA((2, seqs)),
            pltpu.SemaphoreType.DMA((2 * seqs,)),
            pltpu.SemaphoreType.DMA((3,)),
        ],
        compiler_params=pltpu.CompilerParams(
            collective_id=2, has_side_effects=True, vmem_limit_bytes=GRANT
        ),
        cost_estimate=pl.CostEstimate(flops=150 * 10**9, bytes_accessed=10**8, transcendentals=0),
        name="reduce_all",
    )(partial, normal, attended, hidden, cot, d_qkv, d_pre)
    return outs[0], outs[1:]


def normalised(rows_in):
    row_mean = jnp.mean(rows_in, axis=-1, keepdims=True)
    centred = rows_in - row_mean
    variance = jnp.mean(centred * centred, axis=-1, keepdims=True)
    inv_std = lax.rsqrt(variance + 1e-05)
    return centred * inv_std, inv_std


def gelu_both(pre):
    return jax.vjp(lambda vals: jax.nn.gelu(vals, approximate=True), pre)


def finish_kernel(early, tok, cot, mix, others, last, rows, mixed, input_grad, sums):
    step = pl.program_id(0)
    vals = tok[...].astype(f32)
    mixed[...] = (vals + mix[...].astype(f32) + rows[1:2, :] + rows[2:3, :]).astype(bf16)
    normed, inv_std = normalised(vals)
    grad = jnp.where(step < early, others[...].astype(f32), last[...])

    @pl.when(step == 0)
    def _():
        sums[...] = jnp.zeros_like(sums)

    sums[0:1, :] += jnp.sum(grad * normed, axis=0, keepdims=True)
    sums[1:2, :] += jnp.sum(grad, axis=0, keepdims=True)
    scaled = grad * rows[0:1, :]
    input_grad[...] = cot[...].astype(f32) + inv_std * (
        scaled
        - jnp.mean(scaled, axis=-1, keepdims=True)
        - normed * jnp.mean(scaled * normed, axis=-1, keepdims=True)
    )


def finish(tok, cot, mix, others, last, rows):
    total, height = tok.shape[0], 128
    early = others.shape[0] // height
    block = pl.BlockSpec((height, D), lambda i: (i, 0))
    return pl.pallas_call(
        functools.partial(finish_kernel, early),
        grid=(total // height,),
        in_specs=[block] * 3
        + [
            pl.BlockSpec((height, D), lambda i: (jnp.minimum(i, early - 1), 0)),
            pl.BlockSpec((height, D), lambda i: (jnp.maximum(i - early, 0), 0)),
            pl.BlockSpec(rows.shape, lambda i: (0, 0)),
        ],
        out_specs=[block, block, pl.BlockSpec((8, D), lambda i: (0, 0))],
        out_shape=[
            jax.ShapeDtypeStruct((total, D), bf16),
            jax.ShapeDtypeStruct((total, D), f32),
            jax.ShapeDtypeStruct((8, D), f32),
        ],
        compiler_params=pltpu.CompilerParams(vmem_limit_bytes=GRANT),
        name="finish",
    )(tok, cot, mix, others, last, rows)


def per_device(
    tokens,
    cotangent,
    positions,
    wqkv_master,
    fc1_master,
    out_master,
    fc2_master,
    small_master,
    wqkv_first,
    wqkv_second,
    fc1_first,
    fc1_second,
    out_first,
    out_second,
    fc2_first,
    fc2_second,
    small_first,
    small_second,
):
    seqs, span = tokens.shape[0], tokens.shape[1]
    ctx, dp = lax.axis_size("ctx"), lax.axis_size("dp")
    ctx_index = lax.axis_index("ctx")
    length = span * ctx
    total_rows = seqs * length
    own_rows = wqkv_master.shape[0]
    head_cols, ff_cols = D // ctx, FF // ctx

    gate = lax.optimization_barrier
    small_low = jnp.pad(small_master.astype(bf16), ((0, 0), (0, LANES - small_master.shape[1])))
    blocks = [wqkv_master, fc1_master, out_master, fc2_master, small_low]
    places = jnp.pad(positions.astype(f32).reshape(-1, LANES), ((0, 8 - seqs * span // LANES), (0, 0)))
    tok_all, place, (in_w, of_w, small_all) = gather_all(tokens, places, blocks, ctx, dp)
    qkv_w, fc1_w = in_w[:, : 3 * head_cols], in_w[:, 3 * head_cols :]
    params = small_all[:, :16].astype(f32)
    place = place[:, : seqs * span // LANES].reshape(ctx, seqs, span)
    place = jnp.transpose(place, (1, 0, 2)).reshape(total_rows)
    half_rot = ROT // 2
    exponent = jnp.arange(half_rot, dtype=f32) * (-2.0 / ROT)
    frequency = jnp.power(f32(10000.0), exponent)
    angles = frequency[:, None] * place[None, :]
    cos_s, sin_s = jnp.cos(angles), jnp.sin(angles)
    none = jnp.zeros_like(cos_s)
    rest = jnp.zeros((HD - ROT, total_rows), f32)
    tables = [
        jnp.concatenate([cos_s, cos_s, rest + 1.0] * 2, axis=0),
        jnp.concatenate([-sin_s, none, rest] * 2, axis=0),
        jnp.concatenate([none, sin_s, rest] * 2, axis=0),
    ]

    def my_part(values, cols):
        return lax.dynamic_slice_in_dim(values, ctx_index * cols, cols, values.ndim - 1)

    qkv_bias = my_part(params[:, 2:5].T, head_cols)
    fc1_bias = my_part(params[:, 6:10].T.reshape(FF), ff_cols)
    gain, shift = params[:, 0], params[:, 1]
    def scattered(partial):
        return lax.psum_scatter(partial, "ctx", scatter_dimension=1, tiled=True)

    cot, tok_all = gate((cotangent, tok_all))
    cot_all = lax.all_gather(cot, "ctx", axis=1, tiled=True).reshape(total_rows, D)
    normal_low = normalised(tok_all.reshape(total_rows, D).astype(f32))[0]
    normal_low = (normal_low * gain + shift).astype(bf16)
    projected = mm(normal_low, in_w[:, : 3 * head_cols], (1, 0))
    query, key, value, attended, log_total = attend(projected, qkv_bias, tables, seqs)
    pre = mm(normal_low, in_w[:, 3 * head_cols :], (1, 0)) + fc1_bias
    hidden = gelu_both(pre)[0].astype(bf16)
    branch = mm(jnp.concatenate([attended, hidden], axis=1), of_w, (1, 1)).astype(bf16)
    sum_out = jnp.sum(cotangent.astype(f32), axis=(0, 1))[None]
    pre, hidden, branch, sum_out = gate((pre, hidden, branch, sum_out))
    pre, hidden, branch, cot_all = gate((pre, hidden, branch, cot_all))
    mix = scattered(branch.reshape(seqs, length, D))
    back = mm(cot_all, of_w[:, :head_cols], (1, 0)).astype(bf16)
    grad_hidden = mm(cot_all, of_w[:, head_cols:], (1, 0))
    d_pre = gelu_both(pre)[1](grad_hidden)[0].astype(bf16)
    d_qkv = attend_back(query, key, value, back, log_total, tables, seqs)
    def spread(sums, count, cols):
        whole = jnp.zeros((count, ctx * cols), f32)
        return lax.dynamic_update_slice_in_dim(whole, sums.reshape(count, cols), ctx_index * cols, 1)

    sum_qkv, sum_pre = (jnp.sum(part, axis=0, dtype=f32) for part in (d_qkv, d_pre))
    sum_pre = spread(sum_pre, 1, ff_cols).reshape(4, D)
    small_terms = jnp.concatenate(
        [spread(sum_qkv, 3, head_cols), sum_out, sum_pre, sum_out], axis=0
    )

    def normal_back(first, last):
        both = jnp.concatenate([d_qkv[first:last], d_pre[first:last]], axis=1)
        return mm(both, in_w, (1, 1)).astype(bf16)

    d_first, d_last = normal_back(0, total_rows - length), normal_back(total_rows - length, total_rows)
    d_qkv, d_pre, d_first, d_last, small_terms = gate((d_qkv, d_pre, d_first, d_last, small_terms))
    d_qkv, d_pre, d_first, d_last, mix = gate((d_qkv, d_pre, d_first, d_last, mix))
    others = scattered(d_first.reshape(seqs - 1, length, D))
    last, grads = reduce_all(
        d_last, normal_low, attended, hidden, cot_all, d_qkv, d_pre, seqs, ctx, dp
    )
    mixed, input_grad, sums = finish(
        tokens.reshape(-1, D), cotangent.reshape(-1, D), mix.reshape(-1, D), others.reshape(-1, D),
        last, jnp.stack([gain, params[:, 5], params[:, 10]]),
    )
    mixed, input_grad = mixed.reshape(tokens.shape), input_grad.reshape(tokens.shape)
    small_terms = jnp.concatenate([sums[:2], small_terms], axis=0)
    small_sent = jnp.transpose(small_terms.reshape(11, ctx * dp, own_rows), (1, 0, 2))
    small_sent, grads = gate((small_sent, grads))
    small_got = lax.all_to_all(small_sent.reshape(ctx * dp, 1, 11 * own_rows), EVERY, 0, 0, tiled=True)
    small_grad = jnp.sum(small_got, axis=(0, 1)).reshape(11, own_rows).T

    qkv_grad, fc1_grad, out_grad, fc2_grad = (grad.astype(f32) for grad in grads)
    qkv_new = adamw(wqkv_master, wqkv_first, wqkv_second, qkv_grad, 0.04, 0.1)
    fc1_new = adamw(fc1_master, fc1_first, fc1_second, fc1_grad, 0.04, 0.1)
    out_new = adamw(out_master, out_first, out_second, out_grad, 0.4, 0.1)
    fc2_new = adamw(fc2_master, fc2_first, fc2_second, fc2_grad, 0.02, 0.1)
    small_new = adamw(small_master, small_first, small_second, small_grad, 0.3, 0.0)
    return (mixed, input_grad, *qkv_new, *fc1_new, *out_new, *fc2_new, *small_new)


def solution(mesh):
    split = P("dp", "ctx", None)
    rows = P(("dp", "ctx"), None)
    return jax.shard_map(
        per_device,
        mesh=mesh,
        in_specs=(split, split, P("dp", "ctx")) + (rows,) * 15,
        out_specs=(split, split) + (rows,) * 15,
        check_vma=False,
    )
```
